32 devices in a mesh: row: 8 (over y, x, core), col: 4 (over z).
Axes of the slice: x: 2, y: 2, z: 4, core: 2. Of those that a mesh axis runs over, the one named last changes fastest.
Arguments:
- source: bfloat16 [8192, 128], P(('row', 'col')), may hold values from -10 to 10
- target: bfloat16 [16384, 128], P(('col', 'row')), may hold values from -80 to 80
- target_potential: bfloat16 [16384], P(('col', 'row')), may hold values from -4 to 4
- prev_moment: float32 [128, 128], replicated, may hold values from -0.1 to 0.5
Outputs:
- moment: float32 [128, 128], replicated
- source_potential: float32 [8192], P('row')
- target_update: float32 [16384], P(('col', 'row'))
The draws below stay inside these ranges and needn't reach their ends.
All inputs are finite; a program needn't handle non-finite values.
Results may differ from the reference program's by a relative error of at most 0.0059.
Values may be sent and summed in bfloat16 or wider, within the bound.
No kernel may reach another device: no remote copies, remote signals or barrier semaphores. Data moves between devices by JAX's collectives and lax.ppermute only.
A program may use at most 64 MiB of HBM per device.

```python
import math
import jax
import jax.numpy as jnp
from jax import lax

D = 128
ITERS = 2
NS = 8192
NT = 16384


def shared_parts(key):
    centres = jnp.clip(jax.random.normal(jax.random.fold_in(key, 101), (32, D), jnp.float32), -5.0, 5.0)
    return centres


def log_draw(key, shape, low, high):
    return jnp.exp(jax.random.uniform(key, shape, jnp.float32, math.log(low), math.log(high)))


def draw_source(key, part):
    centres = shared_parts(key)
    labels = jax.random.randint(jax.random.fold_in(key, 11), (NS,), 0, 32)
    noise = jnp.clip(jax.random.normal(jax.random.fold_in(key, 12), (NS, D), jnp.float32), -5.0, 5.0)
    base = 0.45 * (0.7071 * centres[labels] + 0.7071 * noise)
    return base.astype(jnp.bfloat16)


def draw_target(key, part):
    centres = shared_parts(key)
    labels = jax.random.randint(jax.random.fold_in(key, 21), (NT,), 0, 32)
    noise = jnp.clip(jax.random.normal(jax.random.fold_in(key, 22), (NT, D), jnp.float32), -5.0, 5.0)
    base = 0.45 * (0.7071 * centres[labels] + 0.7071 * noise)
    return base.astype(jnp.bfloat16)


def draw_prev_moment(key, part):
    diag_values = 0.25 * log_draw(jax.random.fold_in(key, 41), (D,), 0.6, 1.6)
    noise = 0.015 * jnp.clip(jax.random.normal(jax.random.fold_in(key, 42), (D, D), jnp.float32), -4.0, 4.0)
    places = jnp.arange(D)
    on_diag = places[:, None] == places[None, :]
    return jnp.where(on_diag, diag_values[None, :], 0.0) + noise


def block_scale(stream_key, shape, split, smallest, high):
    def one(axis_at, shards_of):
        heights = jax.random.uniform(jax.random.fold_in(jax.random.fold_in(stream_key, 6), axis_at), (shards_of,), jnp.float32, smallest / len(split), high / len(split))
        return jnp.repeat(jnp.exp(heights), shape[axis_at] // shards_of).reshape((-1,) + (1,) * (len(shape) - axis_at - 1))

    loudness = one(*split[0])
    for cut in split[1:]:
        loudness = loudness * one(*cut)
    return loudness


def normal_values(stream_key, extent, width, reach, pieces=(), dtype=jnp.bfloat16):
    result = jax.random.normal(stream_key, extent, jnp.float32) * width
    if len(pieces) > 0:
        result = block_scale(stream_key, extent, pieces, -0.22, 0.18) * result
    return jnp.clip(result, min=-reach, max=reach).astype(dtype)


def setup_inputs(seed: int = 0) -> dict:
    keys = jax.random.split(jax.random.key(seed), 5)
    source = draw_source(jax.random.fold_in(keys[4], 71), 0)
    target = draw_target(jax.random.fold_in(keys[4], 71), 0)
    target_potential = normal_values(keys[2], (NT,), 1.0, 4.0, ((0, 32),))
    prev_moment = draw_prev_moment(jax.random.fold_in(keys[4], 71), 0)
    return dict(source=source, target=target, target_potential=target_potential, prev_moment=prev_moment)


def project(rows, matrix):
    return jnp.dot(rows.astype(jnp.float32), matrix.astype(jnp.float32), precision=lax.Precision.HIGHEST).astype(jnp.bfloat16)


def tile_costs(projected, target):
    return -4.0 * jnp.dot(projected, target.T, preferred_element_type=jnp.float32)


def log_totals(scores, axis):
    top_score = jnp.max(scores, axis=axis, keepdims=True)
    return jnp.squeeze(top_score, axis) + jnp.log(jnp.sum(jnp.exp(scores - top_score), axis=axis))


def reference(source, target, target_potential, prev_moment):
    block_rows = min(512, NS)
    blocks = source.reshape(NS // block_rows, block_rows, D)
    column = target_potential.astype(jnp.float32)

    def couple(total, rows):
        scores = column[None, :] - tile_costs(project(rows, prev_moment), target)
        spread = log_totals(scores, 1)
        weights = (jnp.exp(scores - spread[:, None]) / NS).astype(jnp.bfloat16)
        carried = jnp.dot(weights, target, preferred_element_type=jnp.float32)
        return total + jnp.dot(rows.astype(jnp.float32).T, carried, precision=lax.Precision.HIGHEST), None

    moment, _ = lax.scan(couple, jnp.zeros((D, D), jnp.float32), blocks)

    def column_step(carry, item):
        rows, potential = item
        top_score, mass_total = carry
        scores = potential[:, None] - tile_costs(project(rows, moment), target)
        new_top = jnp.maximum(top_score, jnp.max(scores, axis=0))
        mass_total = mass_total * jnp.exp(top_score - new_top) + jnp.sum(jnp.exp(scores - new_top[None, :]), axis=0)
        return (new_top, mass_total), None

    source_potential = jnp.zeros((NS // block_rows, block_rows), jnp.float32)
    for iteration in range(ITERS):
        current = column
        source_potential = lax.map(lambda rows: math.log(NT) - log_totals(current[None, :] - tile_costs(project(rows, moment), target), 1), blocks)
        start = (jnp.full((NT,), -jnp.inf, jnp.float32), jnp.zeros((NT,), jnp.float32))
        (top_score, mass_total), _ = lax.scan(column_step, start, (blocks, source_potential))
        column = math.log(NS) - (top_score + jnp.log(mass_total))
    return moment, source_potential.reshape(NS), column
```

```python
import functools
import math

import jax
import jax.numpy as jnp
from jax import lax
from jax.experimental import pallas as pl
from jax.experimental.pallas import tpu as pltpu
from jax.sharding import PartitionSpec as P

ITERS = 2
LANES = 128
NT_DIMS = (((1,), (1,)), ((), ()))
TN_DIMS = (((0,), (0,)), ((), ()))


def split3(x):
    high = x.astype(jnp.bfloat16)
    rest = x - high.astype(jnp.float32)
    mid = rest.astype(jnp.bfloat16)
    low = (rest - mid.astype(jnp.float32)).astype(jnp.bfloat16)
    return high, mid, low


def project4(rows, matrix):
    total = None
    for part in reversed(split3(matrix)):
        term = jnp.dot(rows, part, preferred_element_type=jnp.float32)
        total = term if total is None else total + term
    return (total.astype(jnp.bfloat16).astype(jnp.float32) * 4.0).astype(jnp.bfloat16)


def lane_fold(op, x):
    parts = [x[:, i : i + LANES] for i in range(0, x.shape[1], LANES)]
    return functools.reduce(op, parts)


def as_lanes(column):
    return jnp.broadcast_to(column, (LANES, LANES)).T[0:1, :]


def as_rows(lanes):
    return jnp.broadcast_to(lanes, (LANES, LANES)).T


def log_sum(parts):
    top = functools.reduce(jnp.maximum, parts)
    return top + jnp.log(sum(jnp.exp(p - top) for p in parts))


def potential_rows(block_ref, width):
    groups = width // LANES
    tail = block_ref[width:, :].astype(jnp.float32)
    return jnp.concatenate([tail[i : i + 1, :] for i in range(groups)], axis=1)


def row_pass(a, t_refs, column, scores, width, carry_targets):
    top = None
    for g, t_ref in enumerate(t_refs):
        s = column[g] + lax.dot_general(a, t_ref[:width, :], NT_DIMS, preferred_element_type=jnp.float32)
        scores[:, g * width : (g + 1) * width] = s
        m = lane_fold(jnp.maximum, s)
        top = m if top is None else jnp.maximum(top, m)
    top = jnp.max(top, axis=1, keepdims=True)
    mass, carried = None, None
    for g, t_ref in enumerate(t_refs):
        e = jnp.exp(scores[:, g * width : (g + 1) * width] - top)
        m = lane_fold(jnp.add, e)
        mass = m if mass is None else mass + m
        if carry_targets:
            c = jnp.dot(e.astype(jnp.bfloat16), t_ref[:width, :], preferred_element_type=jnp.float32)
            carried = c if carried is None else carried + c
    mass = jnp.sum(mass, axis=1, keepdims=True)
    return top + jnp.log(mass), mass, carried


def couple_kernel(ns, nt, width, *refs):
    s_refs, t_refs, moment_ref = refs[:ns], refs[ns : ns + nt], refs[ns + nt]
    lse_ref, carried_ref, a_ref, scores = refs[ns + nt + 1 :]
    c = lax.axis_index("col")
    piece = s_refs[0].shape[0]
    per = piece // LANES
    for k in range(ns):
        a_ref[k * piece : (k + 1) * piece, :] = project4(s_refs[k][...], moment_ref[...])
    column = [potential_rows(t, width) for t in t_refs]

    @pl.loop(0, ns * per)
    def _(i):
        rows = pl.ds(pl.multiple_of(i * LANES, LANES), LANES)
        lse, mass, carried = row_pass(a_ref[rows, :], t_refs, column, scores, width, True)
        carried_ref[rows, :] = carried / mass
        lse_ref[pl.ds((c ^ (i // per)) * per + i % per, 1), :] = as_lanes(lse)


def moment_kernel(ns, rows_total, pieces, *refs):
    s_refs, l_refs, carried_ref = refs[:ns], refs[ns : 2 * ns], refs[2 * ns]
    out_refs, total_ref = refs[2 * ns + 1 : -1], refs[-1]
    c = lax.axis_index("col")
    piece = s_refs[0].shape[0]
    per = piece // LANES
    scale = jnp.exp(l_refs[0][...] - log_sum([l[...] for l in l_refs])) * (1.0 / rows_total)
    weight, = (scale,)
    total_ref[0 : weight.shape[0], :] = weight
    total = None
    for k in range(ns):
        for j in range(per):
            w = as_rows(total_ref[pl.ds((c ^ k) * per + j, 1), :])
            at = (k * per + j) * LANES
            x = carried_ref[at : at + LANES, :] * w
            s = s_refs[k][j * LANES : (j + 1) * LANES, :]
            for part in reversed(split3(x)):
                term = lax.dot_general(s, part, TN_DIMS, preferred_element_type=jnp.float32)
                total = term if total is None else total + term
    if pieces == 1:
        out_refs[0][...] = total
        return
    r = lax.axis_index("row")
    total_ref[...] = total
    size = total.shape[0] // pieces
    for k in range(pieces):
        out_refs[k][...] = total_ref[pl.ds(pl.multiple_of((r ^ k) * size, size), size), :]


def add_kernel(*refs):
    refs[-1][...] = functools.reduce(jnp.add, [r[...] for r in refs[:-1]])


def first_rows_kernel(ns, nt, width, pieces, *refs):
    s_refs, t_refs, m_refs = refs[:ns], refs[ns : ns + nt], refs[ns + nt : ns + nt + pieces]
    moment_ref, a_ref, lse_ref, scores = refs[ns + nt + pieces :]
    c = lax.axis_index("col")
    piece = s_refs[0].shape[0]
    per = piece // LANES
    if pieces == 1:
        moment_ref[...] = m_refs[0][...]
    else:
        r = lax.axis_index("row")
        size = m_refs[0].shape[0]
        for k in range(pieces):
            moment_ref[pl.ds(pl.multiple_of((r ^ k) * size, size), size), :] = m_refs[k][...]
    for k in range(ns):
        a_ref[k * piece : (k + 1) * piece, :] = project4(s_refs[k][...], moment_ref[...])
    column = [potential_rows(t, width) for t in t_refs]

    @pl.loop(0, ns * per)
    def _(i):
        rows = pl.ds(pl.multiple_of(i * LANES, LANES), LANES)
        lse, _, _ = row_pass(a_ref[rows, :], t_refs, column, scores, width, False)
        lse_ref[pl.ds((c ^ (i // per)) * per + i % per, 1), :] = as_lanes(lse)


def rows_kernel(ns, nt, width, rows_total, *refs):
    a_ref, t_refs, l_refs = refs[0], refs[1 : 1 + nt], refs[1 + nt : 1 + 2 * nt]
    lse_ref, column_ref, scores = refs[1 + 2 * nt :]
    c, r = lax.axis_index("col"), lax.axis_index("row")
    per = a_ref.shape[0] // ns // LANES
    column_ref[...] = math.log(rows_total) - log_sum([l[...] for l in l_refs])
    column = [column_ref[pl.ds(r ^ k, 1), :] for k in range(nt)]

    @pl.loop(0, ns * per)
    def _(i):
        rows = pl.ds(pl.multiple_of(i * LANES, LANES), LANES)
        lse, _, _ = row_pass(a_ref[rows, :], t_refs, column, scores, width, False)
        lse_ref[pl.ds((c ^ (i // per)) * per + i % per, 1), :] = as_lanes(lse)


def columns_kernel(ns, nt, width, cols_total, last, *refs):
    a_ref, t_refs, l_refs = refs[0], refs[1 : 1 + nt], refs[1 + nt : 1 + nt + ns]
    out_refs, (sp_ref, spread_rows, scores) = refs[1 + nt + ns : -3], refs[-3:]
    c, r = lax.axis_index("col"), lax.axis_index("row")
    rows = a_ref.shape[0]
    per = rows // ns // LANES
    sp_ref[...] = math.log(cols_total) - log_sum([l[...] for l in l_refs])
    for k in range(ns):
        for j in range(per):
            at = (k * per + j) * LANES
            spread_rows[at : at + LANES, :] = as_rows(sp_ref[pl.ds((c ^ k) * per + j, 1), :])
    step = 256
    for g, t_ref in enumerate(t_refs):
        top = None
        for at in range(0, rows, step):
            s = lax.dot_general(
                a_ref[at : at + step, :], t_ref[:width, :], NT_DIMS, preferred_element_type=jnp.float32
            )
            s = s + jnp.concatenate([spread_rows[at : at + step, :]] * (width // LANES), axis=1)
            scores[g % 2, at : at + step, :] = s
            m = jnp.max(s.reshape(step // 8, 8, width), axis=0)
            top = m if top is None else jnp.maximum(top, m)
        top = jnp.max(top, axis=0, keepdims=True)
        mass = None
        for at in range(0, rows, step):
            e = jnp.exp(scores[g % 2, at : at + step, :] - top)
            m = jnp.sum(e.reshape(step // 8, 8, width), axis=0)
            mass = m if mass is None else mass + m
        lse = top + jnp.log(jnp.sum(mass, axis=0, keepdims=True))
        if last:
            out_refs[g][...] = lse
        else:
            out_refs[0][pl.ds(r ^ g, 1), :] = lse


def update_kernel(rows_total, *refs):
    refs[-1][...] = math.log(rows_total) - log_sum([r[...] for r in refs[:-1]])


def call(kernel, out, args, scratch=(), flops=0, exps=0):
    vmem = pl.BlockSpec(memory_space=pltpu.VMEM)
    bytes_accessed = sum(x.size * x.dtype.itemsize for x in list(args) + list(out))
    return pl.pallas_call(
        kernel,
        out_shape=list(out),
        in_specs=[vmem] * len(args),
        out_specs=[vmem] * len(out),
        scratch_shapes=list(scratch),
        compiler_params=pltpu.CompilerParams(vmem_limit_bytes=24 << 20),
        cost_estimate=pl.CostEstimate(flops=flops, bytes_accessed=bytes_accessed, transcendentals=exps),
    )(*args)


def swap(x, axis, k):
    return lax.ppermute(x, axis, [(i, i ^ k) for i in range(lax.axis_size(axis))])


def exchange(x, axis):
    return [x] + [swap(x, axis, k) for k in range(1, lax.axis_size(axis))]


def exchange_pairs(x, axis):
    n = lax.axis_size(axis)
    got = {0: x, 1: swap(x, axis, 1)}
    for k in range(2, n, 2):
        got[k] = swap(x, axis, k)
    for k in range(2, n, 2):
        got[k + 1] = swap(got[k], axis, 1)
    return [got[k] for k in range(n)]


def deal(parts, axis):
    return [parts[0]] + [swap(parts[k], axis, k) for k in range(1, len(parts))]


def per_device(source, target, target_potential, prev_moment):
    f32 = jnp.float32
    ns, nt = lax.axis_size("col"), lax.axis_size("row")
    piece, width = source.shape[0], target.shape[0]
    depth = source.shape[1]
    rows, cols = piece * ns, width * nt
    rows_total, cols_total = rows * nt, cols * ns
    groups = width // LANES
    tail = jnp.pad(target_potential.reshape(groups, LANES), ((0, 16 - groups), (0, 0)))
    t_blocks = exchange_pairs(jnp.concatenate([target, tail], axis=0), "row")
    s_pieces = exchange(source, "col")
    tile = jax.ShapeDtypeStruct((rows // LANES, LANES), f32)
    flops, exps = 2 * rows * cols * depth, rows * cols
    row_scores = pltpu.VMEM((LANES, cols), f32)

    lse, carried = call(
        functools.partial(couple_kernel, ns, nt, width),
        [tile, jax.ShapeDtypeStruct((rows, depth), f32)],
        s_pieces + t_blocks + [prev_moment],
        [pltpu.VMEM((rows, depth), jnp.bfloat16), row_scores],
        2 * flops,
        exps,
    )
    pieces = nt if depth % (8 * nt) == 0 else 1
    parts = call(
        functools.partial(moment_kernel, ns, rows_total, pieces),
        [jax.ShapeDtypeStruct((depth // pieces, depth), f32)] * pieces,
        s_pieces + exchange(lse, "col") + [carried],
        [pltpu.VMEM((depth, depth), f32)],
        6 * rows * depth * depth,
    )
    if pieces == 1:
        m_parts = [lax.psum(parts[0], ("row", "col"))]
    else:
        summed, = call(add_kernel, [jax.ShapeDtypeStruct(parts[0].shape, f32)], deal(parts, "row"))
        summed, = call(add_kernel, [jax.ShapeDtypeStruct(parts[0].shape, f32)], exchange(summed, "col"))
        m_parts = exchange(summed, "row")
    moment, a, lse = call(
        functools.partial(first_rows_kernel, ns, nt, width, pieces),
        [jax.ShapeDtypeStruct((depth, depth), f32), jax.ShapeDtypeStruct((rows, depth), jnp.bfloat16), tile],
        s_pieces + t_blocks + m_parts,
        [row_scores],
        flops,
        exps,
    )
    for iteration in range(ITERS):
        last = iteration == ITERS - 1
        if iteration > 0:
            lse, = call(
                functools.partial(rows_kernel, ns, nt, width, rows_total),
                [tile],
                [a] + t_blocks + exchange(column_lse, "row"),
                [pltpu.VMEM((nt, width), f32), row_scores],
                flops,
                exps,
            )
        one = jax.ShapeDtypeStruct((1, width), f32)
        out = [one] * nt if last else [jax.ShapeDtypeStruct((nt, width), f32)]
        *outs, source_potential = call(
            functools.partial(columns_kernel, ns, nt, width, cols_total, last),
            out + [tile],
            [a] + t_blocks + exchange(lse, "col"),
            [pltpu.VMEM((rows, LANES), f32), pltpu.VMEM((2, rows, width), f32)],
            flops,
            exps,
        )
        column_lse = outs[0]
    update, = call(functools.partial(update_kernel, rows_total), [one], deal(outs, "row"))
    return moment, source_potential.reshape(rows), update.reshape(width)


def solution(mesh):
    placed = (P(("row", "col"), None), P(("col", "row"), None), P(("col", "row")), P())
    return jax.shard_map(
        per_device,
        mesh=mesh,
        in_specs=placed,
        out_specs=(P(), P("row"), P(("col", "row"))),
        check_vma=False,
    )
```

```python
import functools
import math

import jax
import jax.numpy as jnp
from jax import lax
from jax.experimental import pallas as pl
from jax.experimental.pallas import tpu as pltpu
from jax.sharding import PartitionSpec as P

ITERS = 2
LANES = 128
NT_DIMS = (((1,), (1,)), ((), ()))
TN_DIMS = (((0,), (0,)), ((), ()))


def split3(x):
    high = x.astype(jnp.bfloat16)
    rest = x - high.astype(jnp.float32)
    mid = rest.astype(jnp.bfloat16)
    low = (rest - mid.astype(jnp.float32)).astype(jnp.bfloat16)
    return high, mid, low


def project4(rows, matrix):
    total = None
    for part in reversed(split3(matrix)):
        term = jnp.dot(rows, part, preferred_element_type=jnp.float32)
        total = term if total is None else total + term
    return (total.astype(jnp.bfloat16).astype(jnp.float32) * 4.0).astype(jnp.bfloat16)


def lane_fold(op, x):
    parts = [x[:, i : i + LANES] for i in range(0, x.shape[1], LANES)]
    return functools.reduce(op, parts)


def as_lanes(column):
    return jnp.broadcast_to(column, (LANES, LANES)).T[0:1, :]


def as_rows(lanes):
    return jnp.broadcast_to(lanes, (LANES, LANES)).T


def log_sum(parts):
    top = functools.reduce(jnp.maximum, parts)
    return top + jnp.log(sum(jnp.exp(p - top) for p in parts))


def potential_rows(block_ref, width):
    groups = width // LANES
    tail = block_ref[width:, :].astype(jnp.float32)
    return jnp.concatenate([tail[i : i + 1, :] for i in range(groups)], axis=1)


def row_pass(a, t_refs, column, scores, width, carry_targets):
    top = None
    for g, t_ref in enumerate(t_refs):
        s = column[g] + lax.dot_general(a, t_ref[:width, :], NT_DIMS, preferred_element_type=jnp.float32)
        scores[:, g * width : (g + 1) * width] = s
        m = lane_fold(jnp.maximum, s)
        top = m if top is None else jnp.maximum(top, m)
    top = jnp.max(top, axis=1, keepdims=True)
    mass, carried = None, None
    for g, t_ref in enumerate(t_refs):
        e = jnp.exp(scores[:, g * width : (g + 1) * width] - top)
        m = lane_fold(jnp.add, e)
        mass = m if mass is None else mass + m
        if carry_targets:
            c = jnp.dot(e.astype(jnp.bfloat16), t_ref[:width, :], preferred_element_type=jnp.float32)
            carried = c if carried is None else carried + c
    mass = jnp.sum(mass, axis=1, keepdims=True)
    return top + jnp.log(mass), mass, carried


def couple_kernel(ns, nt, width, *refs):
    s_refs, t_refs, moment_ref = refs[:ns], refs[ns : ns + nt], refs[ns + nt]
    lse_ref, carried_ref, a_ref, scores = refs[ns + nt + 1 :]
    c = lax.axis_index("col")
    piece = s_refs[0].shape[0]
    per = piece // LANES
    for k in range(ns):
        a_ref[k * piece : (k + 1) * piece, :] = project4(s_refs[k][...], moment_ref[...])
    column = [potential_rows(t, width) for t in t_refs]

    @pl.loop(0, ns * per)
    def _(i):
        rows = pl.ds(pl.multiple_of(i * LANES, LANES), LANES)
        lse, mass, carried = row_pass(a_ref[rows, :], t_refs, column, scores, width, True)
        carried_ref[rows, :] = carried / mass
        row = as_lanes(lse)
        for copy in range(ns):
            lse_ref[copy, pl.ds((c ^ (i // per)) * per + i % per, 1), :] = row


def moment_kernel(ns, rows_total, *refs):
    s_refs, own_ref, l_ref, carried_ref, out_ref, weight_ref = refs[:ns], *refs[ns:]
    c = lax.axis_index("col")
    piece = s_refs[0].shape[0]
    per = piece // LANES
    shift = log_sum([l_ref[k] for k in range(ns)])
    weight_ref[...] = jnp.exp(own_ref[0] - shift) * (1.0 / rows_total)
    total = None
    for k in range(ns):
        for j in range(per):
            w = as_rows(weight_ref[pl.ds((c ^ k) * per + j, 1), :])
            at = (k * per + j) * LANES
            x = carried_ref[at : at + LANES, :] * w
            s = s_refs[k][j * LANES : (j + 1) * LANES, :]
            for part in reversed(split3(x)):
                term = lax.dot_general(s, part, TN_DIMS, preferred_element_type=jnp.float32)
                total = term if total is None else total + term
    write_pieces(out_ref, total)


def write_pieces(out_ref, matrix):
    pieces, _, size = out_ref.shape
    depth = matrix.shape[1]
    if size % depth == 0:
        each = size // depth
        for i in range(matrix.shape[0]):
            out_ref[i // each, :, (i % each) * depth : (i % each + 1) * depth] = matrix[i : i + 1, :]
    else:
        each = depth // size
        for i in range(matrix.shape[0]):
            for j in range(each):
                out_ref[i * each + j] = matrix[i : i + 1, j * size : (j + 1) * size]


def read_pieces(ref, out_ref):
    pieces, _, size = ref.shape
    depth = out_ref.shape[1]
    if size % depth == 0:
        each = size // depth
        for i in range(out_ref.shape[0]):
            out_ref[i : i + 1, :] = ref[i // each, :, (i % each) * depth : (i % each + 1) * depth]
    else:
        each = depth // size
        for i in range(out_ref.shape[0]):
            for j in range(each):
                out_ref[i : i + 1, j * size : (j + 1) * size] = ref[i * each + j]


def add_kernel(x_ref, out_ref):
    total = functools.reduce(jnp.add, [x_ref[k] for k in range(x_ref.shape[0])])
    for k in range(out_ref.shape[0]):
        out_ref[k] = total


def first_rows_kernel(ns, nt, width, *refs):
    s_refs, t_refs, m_ref = refs[:ns], refs[ns : ns + nt], refs[ns + nt]
    moment_ref, a_ref, lse_ref, scores = refs[ns + nt + 1 :]
    piece = s_refs[0].shape[0]
    read_pieces(m_ref, moment_ref)
    for k in range(ns):
        a_ref[k * piece : (k + 1) * piece, :] = project4(s_refs[k][...], moment_ref[...])
    column = [potential_rows(t, width) for t in t_refs]
    all_rows(ns, a_ref, t_refs, column, scores, width, lse_ref)


def all_rows(ns, a_ref, t_refs, column, scores, width, lse_ref):
    c = lax.axis_index("col")
    per = a_ref.shape[0] // ns // LANES

    @pl.loop(0, ns * per)
    def _(i):
        rows = pl.ds(pl.multiple_of(i * LANES, LANES), LANES)
        lse, _, _ = row_pass(a_ref[rows, :], t_refs, column, scores, width, False)
        row = as_lanes(lse)
        for copy in range(ns):
            lse_ref[copy, pl.ds((c ^ (i // per)) * per + i % per, 1), :] = row


def rows_kernel(ns, nt, width, rows_total, *refs):
    a_ref, t_refs, l_ref = refs[0], refs[1 : 1 + nt], refs[1 + nt]
    lse_ref, column_ref, scores = refs[2 + nt :]
    r = lax.axis_index("row")
    column_ref[...] = math.log(rows_total) - log_sum([l_ref[k] for k in range(nt)])
    column = [column_ref[pl.ds(r ^ k, 1), :] for k in range(nt)]
    all_rows(ns, a_ref, t_refs, column, scores, width, lse_ref)


def columns_kernel(ns, nt, width, cols_total, last, *refs):
    a_ref, t_refs, l_ref = refs[0], refs[1 : 1 + nt], refs[1 + nt]
    out_ref, sp_ref, spread_rows, scores = refs[2 + nt :]
    c, r = lax.axis_index("col"), lax.axis_index("row")
    rows = a_ref.shape[0]
    per = rows // ns // LANES
    sp_ref[...] = math.log(cols_total) - log_sum([l_ref[k] for k in range(ns)])
    for k in range(ns):
        for j in range(per):
            at = (k * per + j) * LANES
            spread_rows[at : at + LANES, :] = as_rows(sp_ref[pl.ds((c ^ k) * per + j, 1), :])
    step = 256
    for g, t_ref in enumerate(t_refs):
        top = None
        for at in range(0, rows, step):
            s = lax.dot_general(
                a_ref[at : at + step, :], t_ref[:width, :], NT_DIMS, preferred_element_type=jnp.float32
            )
            s = s + jnp.concatenate([spread_rows[at : at + step, :]] * (width // LANES), axis=1)
            scores[g % 2, at : at + step, :] = s
            m = jnp.max(s.reshape(step // 8, 8, width), axis=0)
            top = m if top is None else jnp.maximum(top, m)
        top = jnp.max(top, axis=0, keepdims=True)
        mass = None
        for at in range(0, rows, step):
            e = jnp.exp(scores[g % 2, at : at + step, :] - top)
            m = jnp.sum(e.reshape(step // 8, 8, width), axis=0)
            mass = m if mass is None else mass + m
        lse = top + jnp.log(jnp.sum(mass, axis=0, keepdims=True))
        if last:
            out_ref[pl.ds(r ^ g, 1)] = lse[None]
        else:
            for copy in range(nt):
                out_ref[copy, pl.ds(r ^ g, 1), :] = lse


def update_kernel(rows_total, l_ref, out_ref):
    out_ref[...] = math.log(rows_total) - log_sum([l_ref[k] for k in range(l_ref.shape[0])])


def call(kernel, out, args, scratch=(), flops=0, exps=0):
    vmem = pl.BlockSpec(memory_space=pltpu.VMEM)
    bytes_accessed = sum(x.size * x.dtype.itemsize for x in list(args) + list(out))
    return pl.pallas_call(
        kernel,
        out_shape=list(out),
        in_specs=[vmem] * len(args),
        out_specs=[vmem] * len(out),
        scratch_shapes=list(scratch),
        compiler_params=pltpu.CompilerParams(vmem_limit_bytes=24 << 20),
        cost_estimate=pl.CostEstimate(flops=flops, bytes_accessed=bytes_accessed, transcendentals=exps),
    )(*args)


def swap(x, axis, k):
    return lax.ppermute(x, axis, [(i, i ^ k) for i in range(lax.axis_size(axis))])


def exchange(x, axis):
    return [x] + [swap(x, axis, k) for k in range(1, lax.axis_size(axis))]


def exchange_pairs(x, axis):
    n = lax.axis_size(axis)
    got = {0: x, 1: swap(x, axis, 1)}
    for k in range(2, n, 2):
        got[k] = swap(x, axis, k)
    for k in range(2, n, 2):
        got[k + 1] = swap(got[k], axis, 1)
    return [got[k] for k in range(n)]


def deal(x, axis):
    return lax.all_to_all(x, axis, 0, 0, tiled=True)


def per_device(source, target, target_potential, prev_moment):
    f32, shape = jnp.float32, jax.ShapeDtypeStruct
    ns, nt = lax.axis_size("col"), lax.axis_size("row")
    piece, width = source.shape[0], target.shape[0]
    depth = source.shape[1]
    rows, cols = piece * ns, width * nt
    rows_total, cols_total = rows * nt, cols * ns
    groups = width // LANES
    tail = jnp.pad(target_potential.reshape(groups, LANES), ((0, 16 - groups), (0, 0)))
    t_blocks = exchange_pairs(jnp.concatenate([target, tail], axis=0), "row")
    s_pieces = exchange(source, "col")
    tile = shape((rows // LANES, LANES), f32)
    tiles = shape((ns, rows // LANES, LANES), f32)
    flops, exps = 2 * rows * cols * depth, rows * cols
    row_scores = pltpu.VMEM((LANES, cols), f32)

    lse, carried = call(
        functools.partial(couple_kernel, ns, nt, width),
        [tiles, shape((rows, depth), f32)],
        s_pieces + t_blocks + [prev_moment],
        [pltpu.VMEM((rows, depth), jnp.bfloat16), row_scores],
        2 * flops,
        exps,
    )
    devices = ns * nt
    pieces = shape((devices, 1, depth * depth // devices), f32)
    parts, = call(
        functools.partial(moment_kernel, ns, rows_total),
        [pieces],
        s_pieces + [lse, deal(lse, "col"), carried],
        [pltpu.VMEM(tile.shape, f32)],
        6 * rows * depth * depth,
    )
    summed, = call(add_kernel, [pieces], [deal(parts, ("row", "col"))])
    moment, a, lse = call(
        functools.partial(first_rows_kernel, ns, nt, width),
        [shape((depth, depth), f32), shape((rows, depth), jnp.bfloat16), tiles],
        s_pieces + t_blocks + [deal(summed, ("row", "col"))],
        [row_scores],
        flops,
        exps,
    )
    for iteration in range(ITERS):
        last = iteration == ITERS - 1
        if iteration > 0:
            lse, = call(
                functools.partial(rows_kernel, ns, nt, width, rows_total),
                [tiles],
                [a] + t_blocks + [deal(column_lse, "row")],
                [pltpu.VMEM((nt, width), f32), row_scores],
                flops,
                exps,
            )
        column_lse, source_potential = call(
            functools.partial(columns_kernel, ns, nt, width, cols_total, last),
            [shape((nt, 1, width) if last else (nt, nt, width), f32), tile],
            [a] + t_blocks + [deal(lse, "col")],
            [pltpu.VMEM((rows, LANES), f32), pltpu.VMEM((2, rows, width), f32)],
            flops,
            exps,
        )
    update, = call(functools.partial(update_kernel, rows_total), [shape((1, width), f32)], [deal(column_lse, "row")])
    return moment, source_potential.reshape(rows), update.reshape(width)


def solution(mesh):
    placed = (P(("row", "col"), None), P(("col", "row"), None), P(("col", "row")), P())
    return jax.shard_map(
        per_device,
        mesh=mesh,
        in_specs=placed,
        out_specs=(P(), P("row"), P(("col", "row"))),
        check_vma=False,
    )
```

```python
import functools
import math

import jax
import jax.numpy as jnp
from jax import lax
from jax.experimental import pallas as pl
from jax.experimental.pallas import tpu as pltpu
from jax.sharding import PartitionSpec as P

ITERS = 2
LANES = 128
NT_DIMS = (((1,), (1,)), ((), ()))
TN_DIMS = (((0,), (0,)), ((), ()))


def split3(x):
    high = x.astype(jnp.bfloat16)
    rest = x - high.astype(jnp.float32)
    mid = rest.astype(jnp.bfloat16)
    low = (rest - mid.astype(jnp.float32)).astype(jnp.bfloat16)
    return high, mid, low


def project4(rows, matrix):
    total = None
    for part in reversed(split3(matrix)):
        term = jnp.dot(rows, part, preferred_element_type=jnp.float32)
        total = term if total is None else total + term
    return (total.astype(jnp.bfloat16).astype(jnp.float32) * 4.0).astype(jnp.bfloat16)


def lane_fold(op, x):
    parts = [x[:, i : i + LANES] for i in range(0, x.shape[1], LANES)]
    return functools.reduce(op, parts)


def as_lanes(column):
    return jnp.broadcast_to(column, (LANES, LANES)).T[0:1, :]


def as_rows(lanes):
    return jnp.broadcast_to(lanes, (LANES, LANES)).T


def log_sum(parts):
    top = functools.reduce(jnp.maximum, parts)
    return top + jnp.log(sum(jnp.exp(p - top) for p in parts))


def potential_rows(block_ref, width):
    groups = width // LANES
    tail = block_ref[width:, :].astype(jnp.float32)
    return jnp.concatenate([tail[i : i + 1, :] for i in range(groups)], axis=1)


def row_lse(a_ref, t_refs, column, scores, width, lse_ref, carried_ref=None):
    c = lax.axis_index("col")
    steps = a_ref.shape[0] // LANES
    per = steps // lax.axis_size("col")
    top = None
    for i in range(steps + 1):
        last_top, top, mass, carried = top, None, None, None
        for g, t_ref in enumerate(t_refs):
            at = slice(g * width, (g + 1) * width)
            if i < steps:
                a = a_ref[i * LANES : (i + 1) * LANES, :]
                s = lax.dot_general(a, t_ref[:width, :], NT_DIMS, preferred_element_type=jnp.float32)
                s = s + column[g]
                scores[i % 2, :, at] = s
                m = lane_fold(jnp.maximum, s)
                top = m if top is None else jnp.maximum(top, m)
            if i > 0:
                e = jnp.exp(scores[(i - 1) % 2, :, at] - last_top)
                m = lane_fold(jnp.add, e)
                mass = m if mass is None else mass + m
                if carried_ref is not None:
                    d = jnp.dot(e.astype(jnp.bfloat16), t_ref[:width, :], preferred_element_type=jnp.float32)
                    carried = d if carried is None else carried + d
        if i < steps:
            top = jnp.max(top, axis=1, keepdims=True)
        if i > 0:
            mass = jnp.sum(mass, axis=1, keepdims=True)
            if carried_ref is not None:
                carried_ref[(i - 1) * LANES : i * LANES, :] = carried / mass
            row = (c ^ ((i - 1) // per)) * per + (i - 1) % per
            lse_ref[pl.ds(row, 1), :] = as_lanes(last_top + jnp.log(mass))


def couple_kernel(ns, nt, width, *refs):
    s_refs, t_refs, moment_ref = refs[:ns], refs[ns : ns + nt], refs[ns + nt]
    lse_ref, carried_ref, a_ref, scores = refs[ns + nt + 1 :]
    piece = s_refs[0].shape[0]
    for k in range(ns):
        a_ref[k * piece : (k + 1) * piece, :] = project4(s_refs[k][...], moment_ref[...])
    column = [potential_rows(t, width) for t in t_refs]
    row_lse(a_ref, t_refs, column, scores, width, lse_ref, carried_ref)


def moment_kernel(ns, rows_total, *refs):
    s_refs, own_ref, l_refs, carried_ref = refs[:ns], refs[ns], refs[ns + 1 : ns + 3], refs[ns + 3]
    keep_ref, send_ref, weight_ref, total_ref = refs[ns + 4 :]
    c, r = lax.axis_index("col"), lax.axis_index("row")
    piece = s_refs[0].shape[0]
    per = piece // LANES
    shift = log_sum([l[...] for l in l_refs])
    weight_ref[...] = jnp.exp(own_ref[...] - shift) * (1.0 / rows_total)
    total = None
    for k in range(ns):
        for j in range(per):
            w = as_rows(weight_ref[pl.ds((c ^ k) * per + j, 1), :])
            at = (k * per + j) * LANES
            x = carried_ref[at : at + LANES, :] * w
            s = s_refs[k][j * LANES : (j + 1) * LANES, :]
            for part in reversed(split3(x)):
                term = lax.dot_general(s, part, TN_DIMS, preferred_element_type=jnp.float32)
                total = term if total is None else total + term
    total_ref[...] = total
    half = keep_ref.shape[0]
    keep_ref[...] = total_ref[pl.ds(pl.multiple_of((r & 1) * half, half), half), :]
    send_ref[...] = total_ref[pl.ds(pl.multiple_of((1 - (r & 1)) * half, half), half), :]


def add_kernel(x_ref, y_ref, out_ref):
    out_ref[...] = x_ref[...] + y_ref[...]


def log_sum_kernel(x_ref, y_ref, out_ref):
    out_ref[...] = log_sum([x_ref[...], y_ref[...]])


def first_rows_kernel(ns, nt, width, *refs):
    s_refs, t_refs, m_refs = refs[:ns], refs[ns : ns + nt], refs[ns + nt : ns + nt + 2]
    moment_ref, a_ref, lse_ref, scores = refs[ns + nt + 2 :]
    r = lax.axis_index("row")
    piece, half = s_refs[0].shape[0], m_refs[0].shape[0]
    for k in range(2):
        moment_ref[pl.ds(pl.multiple_of((k ^ (r & 1)) * half, half), half), :] = m_refs[k][...]
    for k in range(ns):
        a_ref[k * piece : (k + 1) * piece, :] = project4(s_refs[k][...], moment_ref[...])
    column = [potential_rows(t, width) for t in t_refs]
    row_lse(a_ref, t_refs, column, scores, width, lse_ref)


def rows_kernel(nt, width, rows_total, *refs):
    a_ref, t_refs, l_refs = refs[0], refs[1 : 1 + nt], refs[1 + nt : 3 + nt]
    lse_ref, column_ref, scores = refs[3 + nt :]
    r = lax.axis_index("row")
    column_ref[...] = math.log(rows_total) - log_sum([l[...] for l in l_refs])
    column = [column_ref[pl.ds(r ^ k, 1), :] for k in range(nt)]
    row_lse(a_ref, t_refs, column, scores, width, lse_ref)


def columns_kernel(ns, nt, width, cols_total, last, *refs):
    a_ref, t_refs, l_refs = refs[0], refs[1 : 1 + nt], refs[1 + nt : 3 + nt]
    out_refs, (sp_ref, spread_rows, scores) = refs[3 + nt : -3], refs[-3:]
    c, r = lax.axis_index("col"), lax.axis_index("row")
    rows = a_ref.shape[0]
    per = rows // ns // LANES
    sp_ref[...] = math.log(cols_total) - log_sum([l[...] for l in l_refs])
    for k in range(ns):
        for j in range(per):
            at = (k * per + j) * LANES
            spread_rows[at : at + LANES, :] = as_rows(sp_ref[pl.ds((c ^ k) * per + j, 1), :])
    step = LANES
    top = None
    for g in range(nt + 1):
        last_top, top, mass = top, None, None
        for at in range(0, rows, step):
            if g < nt:
                s = lax.dot_general(
                    a_ref[at : at + step, :], t_refs[g][:width, :], NT_DIMS, preferred_element_type=jnp.float32
                )
                s = s + jnp.concatenate([spread_rows[at : at + step, :]] * (width // LANES), axis=1)
                scores[g % 2, at : at + step, :] = s
                m = jnp.max(s.reshape(step // 8, 8, width), axis=0)
                top = m if top is None else jnp.maximum(top, m)
            if g > 0:
                e = jnp.exp(scores[(g - 1) % 2, at : at + step, :] - last_top)
                m = jnp.sum(e.reshape(step // 8, 8, width), axis=0)
                mass = m if mass is None else mass + m
        if g < nt:
            top = jnp.max(top, axis=0, keepdims=True)
        if g > 0:
            lse = last_top + jnp.log(jnp.sum(mass, axis=0, keepdims=True))
            if last:
                out_refs[(g - 1) % 2][(g - 1) // 2] = lse
            else:
                out_refs[0][pl.ds(r ^ (g - 1), 1), :] = lse


def halve_kernel(x_ref, y_ref, keep_ref, send_ref):
    for k in range(x_ref.shape[0]):
        (send_ref if k % 2 else keep_ref)[k // 2] = log_sum([x_ref[k], y_ref[k]])


def update_kernel(rows_total, x_ref, y_ref, out_ref):
    out_ref[...] = math.log(rows_total) - log_sum([x_ref[0], y_ref[0]])


def call(kernel, out, args, scratch=(), flops=0, exps=0):
    vmem = pl.BlockSpec(memory_space=pltpu.VMEM)
    bytes_accessed = sum(x.size * x.dtype.itemsize for x in list(args) + list(out))
    return pl.pallas_call(
        kernel,
        out_shape=list(out),
        in_specs=[vmem] * len(args),
        out_specs=[vmem] * len(out),
        scratch_shapes=list(scratch),
        compiler_params=pltpu.CompilerParams(vmem_limit_bytes=24 << 20),
        cost_estimate=pl.CostEstimate(flops=flops, bytes_accessed=bytes_accessed, transcendentals=exps),
    )(*args)


def swap(x, axis, k):
    return lax.ppermute(x, axis, [(i, i ^ k) for i in range(lax.axis_size(axis))])


def exchange(x, axis):
    return [x] + [swap(x, axis, k) for k in range(1, lax.axis_size(axis))]


def exchange_pairs(x, axis):
    n = lax.axis_size(axis)
    got = {0: x, 1: swap(x, axis, 1)}
    for k in range(2, n, 2):
        got[k] = swap(x, axis, k)
    for k in range(2, n, 2):
        got[k + 1] = swap(got[k], axis, 1)
    return [got[k] for k in range(n)]


def all_but_last(kernel, x, axis, first=1):
    k, n = first, lax.axis_size(axis)
    while 2 * k < n:
        x, = call(kernel, [jax.ShapeDtypeStruct(x.shape, x.dtype)], [x, swap(x, axis, k)])
        k *= 2
    return [x, swap(x, axis, k)]


def per_device(source, target, target_potential, prev_moment):
    f32, shape = jnp.float32, jax.ShapeDtypeStruct
    ns, nt = lax.axis_size("col"), lax.axis_size("row")
    piece, width = source.shape[0], target.shape[0]
    depth = source.shape[1]
    rows, cols = piece * ns, width * nt
    rows_total, cols_total = rows * nt, cols * ns
    groups = width // LANES
    tail = jnp.pad(target_potential.reshape(groups, LANES), ((0, 16 - groups), (0, 0)))
    t_blocks = exchange_pairs(jnp.concatenate([target, tail], axis=0), "row")
    s_pieces = exchange(source, "col")
    tile = shape((rows // LANES, LANES), f32)
    flops, exps = 2 * rows * cols * depth, rows * cols
    row_scores = pltpu.VMEM((2, LANES, cols), f32)

    lse, carried = call(
        functools.partial(couple_kernel, ns, nt, width),
        [tile, shape((rows, depth), f32)],
        s_pieces + t_blocks + [prev_moment],
        [pltpu.VMEM((rows, depth), jnp.bfloat16), row_scores],
        2 * flops,
        exps,
    )
    half = shape((depth // 2, depth), f32)
    keep, send = call(
        functools.partial(moment_kernel, ns, rows_total),
        [half, half],
        s_pieces + [lse] + all_but_last(log_sum_kernel, lse, "col") + [carried],
        [pltpu.VMEM(tile.shape, f32), pltpu.VMEM((depth, depth), f32)],
        6 * rows * depth * depth,
    )
    part, = call(add_kernel, [half], [keep, swap(send, "row", 1)])
    part, = call(add_kernel, [half], all_but_last(add_kernel, part, "row", 2))
    part, = call(add_kernel, [half], all_but_last(add_kernel, part, "col"))
    moment, a, lse = call(
        functools.partial(first_rows_kernel, ns, nt, width),
        [shape((depth, depth), f32), shape((rows, depth), jnp.bfloat16), tile],
        s_pieces + t_blocks + [part, swap(part, "row", 1)],
        [row_scores],
        flops,
        exps,
    )
    for iteration in range(ITERS):
        last = iteration == ITERS - 1
        if iteration > 0:
            lse, = call(
                functools.partial(rows_kernel, nt, width, rows_total),
                [tile],
                [a] + t_blocks + all_but_last(log_sum_kernel, column_lse, "row"),
                [pltpu.VMEM((nt, width), f32), row_scores],
                flops,
                exps,
            )
        blocks = shape((nt // 2, 1, width), f32)
        *outs, source_potential = call(
            functools.partial(columns_kernel, ns, nt, width, cols_total, last),
            ([blocks, blocks] if last else [shape((nt, width), f32)]) + [tile],
            [a] + t_blocks + all_but_last(log_sum_kernel, lse, "col"),
            [pltpu.VMEM((rows, LANES), f32), pltpu.VMEM((2, rows, width), f32)],
            flops,
            exps,
        )
        column_lse = outs[0]
    keep, send = outs
    k = 1
    while keep.shape[0] > 1:
        blocks = shape((keep.shape[0] // 2, 1, width), f32)
        keep, send = call(halve_kernel, [blocks, blocks], [keep, swap(send, "row", k)])
        k *= 2
    update, = call(
        functools.partial(update_kernel, rows_total), [shape((1, width), f32)], [keep, swap(send, "row", k)]
    )
    return moment, source_potential.reshape(rows), update.reshape(width)


def solution(mesh):
    placed = (P(("row", "col"), None), P(("col", "row"), None), P(("col", "row")), P())
    return jax.shard_map(
        per_device,
        mesh=mesh,
        in_specs=placed,
        out_specs=(P(), P("row"), P(("col", "row"))),
        check_vma=False,
    )
```

```python
import functools
import math

import jax
import jax.numpy as jnp
from jax import lax
from jax.experimental import pallas as pl
from jax.experimental.pallas import tpu as pltpu
from jax.sharding import PartitionSpec as P

ITERS = 2
LANES = 128
NT_DIMS = (((1,), (1,)), ((), ()))
TN_DIMS = (((0,), (0,)), ((), ()))


def split3(x):
    high = x.astype(jnp.bfloat16)
    rest = x - high.astype(jnp.float32)
    mid = rest.astype(jnp.bfloat16)
    low = (rest - mid.astype(jnp.float32)).astype(jnp.bfloat16)
    return high, mid, low


def project4(rows, matrix):
    total = None
    for part in reversed(split3(matrix)):
        term = jnp.dot(rows, part, preferred_element_type=jnp.float32)
        total = term if total is None else total + term
    return (total.astype(jnp.bfloat16).astype(jnp.float32) * 4.0).astype(jnp.bfloat16)


def lane_fold(op, x):
    parts = [x[:, i : i + LANES] for i in range(0, x.shape[1], LANES)]
    return functools.reduce(op, parts)


def as_lanes(column):
    return jnp.broadcast_to(column, (LANES, LANES)).T[0:1, :]


def as_rows(lanes):
    return jnp.broadcast_to(lanes, (LANES, LANES)).T


def tree(op, parts):
    while len(parts) > 1:
        parts = [op(parts[i], parts[i + 1]) for i in range(0, len(parts), 2)]
    return parts[0]


def log_sum(parts):
    top = functools.reduce(jnp.maximum, parts)
    return top + jnp.log(tree(jnp.add, [jnp.exp(p - top) for p in parts]))


def potential_rows(block_ref, width):
    groups = width // LANES
    tail = block_ref[width:, :].astype(jnp.float32)
    return jnp.concatenate([tail[i : i + 1, :] for i in range(groups)], axis=1)


def row_lse(a_ref, t_refs, column, scores, width, lse_ref, carried_ref=None):
    c = lax.axis_index("col")
    steps = a_ref.shape[0] // LANES
    per = steps // lax.axis_size("col")
    top = None
    for i in range(steps + 1):
        last_top, top, mass, carried = top, None, None, None
        for g, t_ref in enumerate(t_refs):
            at = slice(g * width, (g + 1) * width)
            if i < steps:
                a = a_ref[i * LANES : (i + 1) * LANES, :]
                s = lax.dot_general(a, t_ref[:width, :], NT_DIMS, preferred_element_type=jnp.float32)
                s = s + column[g]
                scores[i % 2, :, at] = s
                m = lane_fold(jnp.maximum, s)
                top = m if top is None else jnp.maximum(top, m)
            if i > 0:
                e = jnp.exp(scores[(i - 1) % 2, :, at] - last_top)
                m = lane_fold(jnp.add, e)
                mass = m if mass is None else mass + m
                if carried_ref is not None:
                    d = jnp.dot(e.astype(jnp.bfloat16), t_ref[:width, :], preferred_element_type=jnp.float32)
                    carried = d if carried is None else carried + d
        if i < steps:
            top = jnp.max(top, axis=1, keepdims=True)
        if i > 0:
            mass = jnp.sum(mass, axis=1, keepdims=True)
            if carried_ref is not None:
                carried_ref[(i - 1) * LANES : i * LANES, :] = carried / mass
            row = (c ^ ((i - 1) // per)) * per + (i - 1) % per
            lse_ref[pl.ds(row, 1), :] = as_lanes(last_top + jnp.log(mass))


def couple_kernel(ns, nt, width, *refs):
    s_refs, t_refs, moment_ref = refs[:ns], refs[ns : ns + nt], refs[ns + nt]
    lse_ref, carried_ref, a_ref, scores = refs[ns + nt + 1 :]
    piece = s_refs[0].shape[0]
    for k in range(ns):
        a_ref[k * piece : (k + 1) * piece, :] = project4(s_refs[k][...], moment_ref[...])
    column = [potential_rows(t, width) for t in t_refs]
    row_lse(a_ref, t_refs, column, scores, width, lse_ref, carried_ref)


def moment_kernel(ns, rows_total, *refs):
    s_refs, l_refs, carried_ref = refs[:ns], refs[ns : 2 * ns], refs[2 * ns]
    out_ref, weight_ref = refs[2 * ns + 1 :]
    c = lax.axis_index("col")
    piece = s_refs[0].shape[0]
    per = piece // LANES
    shift = log_sum([l[...] for l in l_refs])
    weight_ref[...] = jnp.exp(l_refs[0][...] - shift) * (1.0 / rows_total)
    total = None
    for k in range(ns):
        for j in range(per):
            w = as_rows(weight_ref[pl.ds((c ^ k) * per + j, 1), :])
            at = (k * per + j) * LANES
            x = carried_ref[at : at + LANES, :] * w
            s = s_refs[k][j * LANES : (j + 1) * LANES, :]
            for part in reversed(split3(x)):
                term = lax.dot_general(s, part, TN_DIMS, preferred_element_type=jnp.float32)
                total = term if total is None else total + term
    out_ref[...] = total


def add_kernel(*refs):
    refs[-1][...] = tree(jnp.add, [r[...] for r in refs[:-1]])


def log_sum_kernel(*refs):
    refs[-1][...] = log_sum([r[...] for r in refs[:-1]])


def on_core(core, here, passed):
    return jnp.where(lax.axis_index("row") % 2 == core, here, passed)


def first_rows_kernel(ns, nt, width, *refs):
    s_refs, t_refs, m_refs = refs[:ns], refs[ns : ns + nt], refs[ns + nt : ns + nt + 2]
    moment_ref, a_ref, lse_ref, scores = refs[ns + nt + 2 :]
    piece = s_refs[0].shape[0]
    moment_ref[...] = on_core(1, m_refs[0][...], m_refs[1][...])
    for k in range(ns):
        a_ref[k * piece : (k + 1) * piece, :] = project4(s_refs[k][...], moment_ref[...])
    column = [potential_rows(t, width) for t in t_refs]
    row_lse(a_ref, t_refs, column, scores, width, lse_ref)


def rows_kernel(nt, width, rows_total, *refs):
    a_ref, t_refs, l_refs = refs[0], refs[1 : 1 + nt], refs[1 + nt : 3 + nt]
    lse_ref, column_ref, scores = refs[3 + nt :]
    r = lax.axis_index("row")
    column_ref[...] = math.log(rows_total) - on_core(0, l_refs[0][...], l_refs[1][...])
    column = [column_ref[pl.ds(r ^ k, 1), :] for k in range(nt)]
    row_lse(a_ref, t_refs, column, scores, width, lse_ref)


def columns_kernel(ns, nt, width, cols_total, last, *refs):
    a_ref, t_refs, l_refs = refs[0], refs[1 : 1 + nt], refs[1 + nt : 1 + nt + ns]
    out_ref, sp_ref, spread_rows, scores = refs[1 + nt + ns :]
    c, r = lax.axis_index("col"), lax.axis_index("row")
    rows = a_ref.shape[0]
    per = rows // ns // LANES
    sp_ref[...] = math.log(cols_total) - log_sum([l[...] for l in l_refs])
    for k in range(ns):
        for j in range(per):
            at = (k * per + j) * LANES
            spread_rows[at : at + LANES, :] = as_rows(sp_ref[pl.ds((c ^ k) * per + j, 1), :])
    step = LANES
    top = None
    for g in range(nt + 1):
        last_top, top, mass = top, None, None
        for at in range(0, rows, step):
            if g < nt:
                s = lax.dot_general(
                    a_ref[at : at + step, :], t_refs[g][:width, :], NT_DIMS, preferred_element_type=jnp.float32
                )
                s = s + jnp.concatenate([spread_rows[at : at + step, :]] * (width // LANES), axis=1)
                scores[g % 2, at : at + step, :] = s
                m = jnp.max(s.reshape(step // 8, 8, width), axis=0)
                top = m if top is None else jnp.maximum(top, m)
            if g > 0:
                e = jnp.exp(scores[(g - 1) % 2, at : at + step, :] - last_top)
                m = jnp.sum(e.reshape(step // 8, 8, width), axis=0)
                mass = m if mass is None else mass + m
        if g < nt:
            top = jnp.max(top, axis=0, keepdims=True)
        if g > 0:
            lse = last_top + jnp.log(jnp.sum(mass, axis=0, keepdims=True))
            if last:
                out_ref[g - 1] = lse
            else:
                out_ref[pl.ds(r ^ (g - 1), 1), :] = lse


def pairs_kernel(x_ref, y_ref, *out_refs):
    for k, out_ref in enumerate(out_refs):
        for i in range(2):
            g = 2 * k + (i if k == 0 else 1 - i)
            out_ref[i] = log_sum([x_ref[g], y_ref[g ^ 1]])


def update_kernel(rows_total, x_ref, y_ref, out_ref):
    out_ref[...] = math.log(rows_total) - on_core(0, x_ref[0], y_ref[1])


def call(kernel, out, args, scratch=(), flops=0, exps=0):
    vmem = pl.BlockSpec(memory_space=pltpu.VMEM)
    bytes_accessed = sum(x.size * x.dtype.itemsize for x in list(args) + list(out))
    return pl.pallas_call(
        kernel,
        out_shape=list(out),
        in_specs=[vmem] * len(args),
        out_specs=[vmem] * len(out),
        scratch_shapes=list(scratch),
        compiler_params=pltpu.CompilerParams(vmem_limit_bytes=24 << 20),
        cost_estimate=pl.CostEstimate(flops=flops, bytes_accessed=bytes_accessed, transcendentals=exps),
    )(*args)


def swap(x, axis, k):
    return lax.ppermute(x, axis, [(i, i ^ k) for i in range(lax.axis_size(axis))])


def exchange(x, axis):
    return [x] + [swap(x, axis, k) for k in range(1, lax.axis_size(axis))]


def one_way(x, k, core):
    return lax.ppermute(x, "row", [(i, i ^ k ^ 1) for i in range(lax.axis_size("row")) if i % 2 == core])


def one_way_col(x, k, core):
    n = lax.axis_size("col")
    pairs = [
        (i * n + j, (i ^ 1) * n + (j ^ k)) for i in range(lax.axis_size("row")) if i % 2 == core for j in range(n)
    ]
    return lax.ppermute(x, ("row", "col"), pairs)


def combine(kernel, parts):
    return call(kernel, [jax.ShapeDtypeStruct(parts[0].shape, parts[0].dtype)], parts)[0]


def gather(block, piece):
    ns, nt = lax.axis_size("col"), lax.axis_size("row")
    blocks, pieces = {0: block}, {0: piece}
    for k in range(2, nt, 2):
        blocks[k] = swap(block, "row", k)
    for k in range(1, ns):
        pieces[k] = swap(piece, "col", k)
    far = {**blocks, **{nt + k: pieces[k] for k in range(1, ns)}}
    far = lax.optimization_barrier(far)
    for k in range(0, nt, 2):
        blocks[k + 1] = swap(far[k], "row", 1)
    return [blocks[k] for k in range(nt)], [pieces[k] for k in range(ns)]


def per_device(source, target, target_potential, prev_moment):
    f32, shape = jnp.float32, jax.ShapeDtypeStruct
    ns, nt = lax.axis_size("col"), lax.axis_size("row")
    piece, width = source.shape[0], target.shape[0]
    depth = source.shape[1]
    rows, cols = piece * ns, width * nt
    rows_total, cols_total = rows * nt, cols * ns
    groups = width // LANES
    tail = jnp.pad(target_potential.reshape(groups, LANES), ((0, 16 - groups), (0, 0)))
    t_blocks, s_pieces = gather(jnp.concatenate([target, tail], axis=0), source)
    tile = shape((rows // LANES, LANES), f32)
    flops, exps = 2 * rows * cols * depth, rows * cols
    row_scores = pltpu.VMEM((2, LANES, cols), f32)

    lse, carried = call(
        functools.partial(couple_kernel, ns, nt, width),
        [tile, shape((rows, depth), f32)],
        s_pieces + t_blocks + [prev_moment],
        [pltpu.VMEM((rows, depth), jnp.bfloat16), row_scores],
        2 * flops,
        exps,
    )
    part, = call(
        functools.partial(moment_kernel, ns, rows_total),
        [shape((depth, depth), f32)],
        s_pieces + exchange(lse, "col") + [carried],
        [pltpu.VMEM(tile.shape, f32)],
        6 * rows * depth * depth,
    )
    part = combine(add_kernel, [part, swap(part, "row", 1)])
    part = combine(add_kernel, [part] + [one_way(part, k, 1) for k in range(2, nt, 2)])
    part = combine(add_kernel, [one_way_col(part, k, 0) for k in range(ns)])
    moment, a, lse = call(
        functools.partial(first_rows_kernel, ns, nt, width),
        [shape((depth, depth), f32), shape((rows, depth), jnp.bfloat16), tile],
        s_pieces + t_blocks + [part, one_way(part, 0, 1)],
        [row_scores],
        flops,
        exps,
    )
    for iteration in range(ITERS):
        last = iteration == ITERS - 1
        if iteration > 0:
            both = combine(log_sum_kernel, [column_lse, swap(column_lse, "row", 1)])
            here = combine(log_sum_kernel, [both] + [one_way(both, k, 1) for k in range(2, nt, 2)])
            lse, = call(
                functools.partial(rows_kernel, nt, width, rows_total),
                [tile],
                [a] + t_blocks + [here, one_way(here, 0, 0)],
                [pltpu.VMEM((nt, width), f32), row_scores],
                flops,
                exps,
            )
        column_lse, source_potential = call(
            functools.partial(columns_kernel, ns, nt, width, cols_total, last),
            [shape((nt, 1, width) if last else (nt, width), f32), tile],
            [a] + t_blocks + exchange(lse, "col"),
            [pltpu.VMEM((rows, LANES), f32), pltpu.VMEM((2, rows, width), f32)],
            flops,
            exps,
        )
    pair = shape((2, 1, width), f32)
    own, *sent = call(pairs_kernel, [pair] * (nt // 2), [column_lse, swap(column_lse, "row", 1)])
    here = combine(log_sum_kernel, [own] + [one_way(x, 2 * k + 2, 1) for k, x in enumerate(sent)])
    update, = call(
        functools.partial(update_kernel, rows_total), [shape((1, width), f32)], [here, one_way(here, 0, 0)]
    )
    return moment, source_potential.reshape(rows), update.reshape(width)


def solution(mesh):
    placed = (P(("row", "col"), None), P(("col", "row"), None), P(("col", "row")), P())
    return jax.shard_map(
        per_device,
        mesh=mesh,
        in_specs=placed,
        out_specs=(P(), P("row"), P(("col", "row"))),
        check_vma=False,
    )
```

```python
import functools
import math

import jax
import jax.numpy as jnp
from jax import lax
from jax.experimental import pallas as pl
from jax.experimental.pallas import tpu as pltpu
from jax.sharding import PartitionSpec as P

ITERS = 2
LANES = 128
SUB = 16
SMALLEST = 1e-25
NT_DIMS = (((1,), (1,)), ((), ()))
TN_DIMS = (((0,), (0,)), ((), ()))


def split3(x):
    high = x.astype(jnp.bfloat16)
    rest = x - high.astype(jnp.float32)
    mid = rest.astype(jnp.bfloat16)
    low = (rest - mid.astype(jnp.float32)).astype(jnp.bfloat16)
    return high, mid, low


def project4(rows, matrix):
    total = None
    for part in reversed(split3(matrix)):
        term = jnp.dot(rows, part, preferred_element_type=jnp.float32)
        total = term if total is None else total + term
    return (total.astype(jnp.bfloat16).astype(jnp.float32) * 4.0).astype(jnp.bfloat16)


def lane_fold(op, x):
    parts = [x[:, i : i + LANES] for i in range(0, x.shape[1], LANES)]
    return functools.reduce(op, parts)


def as_lanes(column):
    return jnp.broadcast_to(column, (LANES, LANES)).T[0:1, :]


def as_rows(lanes):
    return jnp.broadcast_to(lanes, (LANES, LANES)).T


def tree(op, parts):
    while len(parts) > 1:
        parts = [op(parts[i], parts[i + 1]) for i in range(0, len(parts), 2)]
    return parts[0]


def log_sum(parts):
    top = functools.reduce(jnp.maximum, parts)
    return top + jnp.log(tree(jnp.add, [jnp.exp(p - top) for p in parts]))


def potential_rows(block_ref, width):
    groups = width // LANES
    tail = block_ref[width:, :].astype(jnp.float32)
    return jnp.concatenate([tail[i : i + 1, :] for i in range(groups)], axis=1)


def row_lse(a_ref, t_refs, column, scores, width, lse_ref, carried_ref=None, e_ref=None, top_ref=None):
    c = lax.axis_index("col")
    steps = a_ref.shape[0] // LANES
    per = steps // lax.axis_size("col")
    top = None
    for i in range(steps + 1):
        last_top, top, mass, carried = top, None, None, None
        for g, t_ref in enumerate(t_refs):
            at = slice(g * width, (g + 1) * width)
            if i < steps:
                a = a_ref[i * LANES : (i + 1) * LANES, :]
                s = lax.dot_general(a, t_ref[:width, :], NT_DIMS, preferred_element_type=jnp.float32)
                s = s + column[g]
                scores[i % 2, :, at] = s
                m = lane_fold(jnp.maximum, s)
                top = m if top is None else jnp.maximum(top, m)
            if i > 0:
                e = jnp.exp(scores[(i - 1) % 2, :, at] - last_top)
                m = lane_fold(jnp.add, e)
                mass = m if mass is None else mass + m
                if e_ref is not None:
                    e_ref[(i - 1) * LANES : i * LANES, at] = e.astype(jnp.bfloat16)
                if carried_ref is not None:
                    d = jnp.dot(e.astype(jnp.bfloat16), t_ref[:width, :], preferred_element_type=jnp.float32)
                    carried = d if carried is None else carried + d
        if i < steps:
            top = jnp.max(top, axis=1, keepdims=True)
        if i > 0:
            mass = jnp.sum(mass, axis=1, keepdims=True)
            if carried_ref is not None:
                carried_ref[(i - 1) * LANES : i * LANES, :] = carried / mass
            row = (c ^ ((i - 1) // per)) * per + (i - 1) % per
            lse_ref[pl.ds(row, 1), :] = as_lanes(last_top + jnp.log(mass))
            if top_ref is not None:
                top_ref[pl.ds(row, 1), :] = as_lanes(last_top)


def couple_kernel(ns, nt, width, *refs):
    s_refs, t_refs, moment_ref = refs[:ns], refs[ns : ns + nt], refs[ns + nt]
    lse_ref, carried_ref, a_ref, scores = refs[ns + nt + 1 :]
    piece = s_refs[0].shape[0]
    for k in range(ns):
        a_ref[k * piece : (k + 1) * piece, :] = project4(s_refs[k][...], moment_ref[...])
    column = [potential_rows(t, width) for t in t_refs]
    row_lse(a_ref, t_refs, column, scores, width, lse_ref, carried_ref)


def moment_kernel(ns, rows_total, *refs):
    s_refs, l_refs, carried_ref = refs[:ns], refs[ns : 2 * ns], refs[2 * ns]
    keep_ref, send_ref, weight_ref, total_ref = refs[2 * ns + 1 :]
    c, r = lax.axis_index("col"), lax.axis_index("row")
    piece = s_refs[0].shape[0]
    per = piece // LANES
    shift = log_sum([l[...] for l in l_refs])
    weight_ref[...] = jnp.exp(l_refs[0][...] - shift) * (1.0 / rows_total)
    total = None
    for k in range(ns):
        for j in range(per):
            w = as_rows(weight_ref[pl.ds((c ^ k) * per + j, 1), :])
            at = (k * per + j) * LANES
            x = carried_ref[at : at + LANES, :] * w
            s = s_refs[k][j * LANES : (j + 1) * LANES, :]
            for part in reversed(split3(x)):
                term = lax.dot_general(s, part, TN_DIMS, preferred_element_type=jnp.float32)
                total = term if total is None else total + term
    total_ref[...] = total
    half = keep_ref.shape[0]
    keep_ref[...] = total_ref[pl.ds(pl.multiple_of((r % 2) * half, half), half), :]
    send_ref[...] = total_ref[pl.ds(pl.multiple_of((1 - r % 2) * half, half), half), :]


def add_kernel(*refs):
    refs[-1][...] = tree(jnp.add, [r[...] for r in refs[:-1]])


def log_sum_kernel(*refs):
    refs[-1][...] = log_sum([r[...] for r in refs[:-1]])


def first_rows_kernel(ns, nt, width, *refs):
    s_refs, t_refs, m_refs = refs[:ns], refs[ns : ns + nt], refs[ns + nt : ns + nt + 2]
    moment_ref, a_ref, lse_ref, top_ref, e_ref, scores = refs[ns + nt + 2 :]
    r = lax.axis_index("row")
    piece, half = s_refs[0].shape[0], m_refs[0].shape[0]
    for k in range(2):
        moment_ref[pl.ds(pl.multiple_of((k ^ (r % 2)) * half, half), half), :] = m_refs[k][...]
    for k in range(ns):
        a_ref[k * piece : (k + 1) * piece, :] = project4(s_refs[k][...], moment_ref[...])
    column = [potential_rows(t, width) for t in t_refs]
    row_lse(a_ref, t_refs, column, scores, width, lse_ref, None, e_ref, top_ref)


def high_low(x):
    high = x.astype(jnp.bfloat16).astype(jnp.float32)
    at = lax.broadcasted_iota(jnp.int32, (SUB, x.shape[1]), 0)
    return jnp.where(at == 0, high, jnp.where(at == 1, x - high, 0.0)).astype(jnp.bfloat16)


def rows_kernel(nt, width, rows_total, *refs):
    a_ref, e_ref, top_ref, t_refs = refs[0], refs[1], refs[2], refs[3 : 3 + nt]
    l_refs = refs[3 + nt : 3 + nt + nt // 2]
    lse_ref, column_ref, weights, scores = refs[3 + nt + nt // 2 :]
    c, r = lax.axis_index("col"), lax.axis_index("row")
    column_ref[...] = math.log(rows_total) - log_sum([l[...] for l in l_refs])
    column = [column_ref[pl.ds(r ^ k, 1), :] for k in range(nt)]
    change = [column[k] - potential_rows(t_refs[k], width) for k in range(nt)]
    top = jnp.max(functools.reduce(jnp.maximum, change), axis=1, keepdims=True)
    for k in range(nt):
        weights[:, k * width : (k + 1) * width] = high_low(jnp.exp(change[k] - top))
    steps = a_ref.shape[0] // LANES
    per = steps // lax.axis_size("col")
    least = None
    for i in range(steps):
        e = e_ref[i * LANES : (i + 1) * LANES, :]
        sums = lax.dot_general(weights[...], e, NT_DIMS, preferred_element_type=jnp.float32)
        mass = sums[0:1, :] + sums[1:2, :]
        least = mass if least is None else jnp.minimum(least, mass)
        row = pl.ds((c ^ (i // per)) * per + i % per, 1)
        lse_ref[row, :] = top + top_ref[row, :] + jnp.log(mass)

    @pl.when(jnp.logical_not(jnp.min(least) > SMALLEST))
    def _():
        row_lse(a_ref, t_refs, column, scores, width, lse_ref)


def columns_kernel(ns, nt, width, cols_total, last, *refs):
    a_ref, e_ref, top_ref, t_refs, l_refs = refs[0], refs[1], refs[2], refs[3 : 3 + nt], refs[3 + nt : 3 + nt + ns]
    out_refs, (sp_ref, weight_rows, weights, spread_rows, scores) = refs[3 + nt + ns : -5], refs[-5:]
    c, r = lax.axis_index("col"), lax.axis_index("row")
    rows = a_ref.shape[0]
    per = rows // ns // LANES
    potential = math.log(cols_total) - log_sum([l[...] for l in l_refs])
    sp_ref[...] = potential
    shift = potential + top_ref[...]
    top = jnp.max(jnp.max(shift, axis=1, keepdims=True), axis=0, keepdims=True)
    weight_rows[...] = jnp.exp(shift - top)
    for k in range(ns):
        for j in range(per):
            at = (k * per + j) * LANES
            weights[:, at : at + LANES] = high_low(weight_rows[pl.ds((c ^ k) * per + j, 1), :])

    def store(g, lse):
        if last:
            out_refs[g % 2][g // 2] = lse
        else:
            out_refs[0][pl.ds(r ^ g, 1), :] = lse

    least = None
    for g in range(nt):
        e = e_ref[:, g * width : (g + 1) * width]
        sums = jnp.dot(weights[...], e, preferred_element_type=jnp.float32)
        mass = sums[0:1, :] + sums[1:2, :]
        least = mass if least is None else jnp.minimum(least, mass)
        store(g, top - potential_rows(t_refs[g], width) + jnp.log(mass))

    @pl.when(jnp.logical_not(jnp.min(least) > SMALLEST))
    def _():
        column_lse(ns, a_ref, t_refs, sp_ref, spread_rows, scores, width, store)


def column_lse(ns, a_ref, t_refs, sp_ref, spread_rows, scores, width, store):
    c = lax.axis_index("col")
    rows = a_ref.shape[0]
    per = rows // ns // LANES
    for k in range(ns):
        for j in range(per):
            at = (k * per + j) * LANES
            spread_rows[at : at + LANES, :] = as_rows(sp_ref[pl.ds((c ^ k) * per + j, 1), :])
    for g, t_ref in enumerate(t_refs):
        top = None
        for at in range(0, rows, LANES):
            a = a_ref[at : at + LANES, :]
            s = lax.dot_general(a, t_ref[:width, :], NT_DIMS, preferred_element_type=jnp.float32)
            s = s + jnp.concatenate([spread_rows[at : at + LANES, :]] * (width // LANES), axis=1)
            scores[at : at + LANES, :] = s
            m = jnp.max(s.reshape(LANES // 8, 8, width), axis=0)
            top = m if top is None else jnp.maximum(top, m)
        top = jnp.max(top, axis=0, keepdims=True)
        mass = None
        for at in range(0, rows, LANES):
            e = jnp.exp(scores[at : at + LANES, :] - top)
            m = jnp.sum(e.reshape(LANES // 8, 8, width), axis=0)
            mass = m if mass is None else mass + m
        store(g, top + jnp.log(jnp.sum(mass, axis=0, keepdims=True)))


def split_kernel(x_ref, y_ref, *out_refs):
    for k, out_ref in enumerate(out_refs):
        out_ref[...] = log_sum([x_ref[k], y_ref[k]])


def update_kernel(rows_total, *refs):
    refs[-1][...] = math.log(rows_total) - log_sum([l[...] for l in refs[:-1]])


def call(kernel, out, args, scratch=(), flops=0, exps=0):
    vmem = pl.BlockSpec(memory_space=pltpu.VMEM)
    bytes_accessed = sum(x.size * x.dtype.itemsize for x in list(args) + list(out))
    return pl.pallas_call(
        kernel,
        out_shape=list(out),
        in_specs=[vmem] * len(args),
        out_specs=[vmem] * len(out),
        scratch_shapes=list(scratch),
        compiler_params=pltpu.CompilerParams(vmem_limit_bytes=24 << 20),
        cost_estimate=pl.CostEstimate(flops=flops, bytes_accessed=bytes_accessed, transcendentals=exps),
    )(*args)


def swap(x, axis, k):
    return lax.ppermute(x, axis, [(i, i ^ k) for i in range(lax.axis_size(axis))])


def exchange(x, axis):
    return [x] + [swap(x, axis, k) for k in range(1, lax.axis_size(axis))]


def exchange_chips(x):
    return [x] + [swap(x, "row", k) for k in range(2, lax.axis_size("row"), 2)]


def combine(kernel, parts):
    return call(kernel, [jax.ShapeDtypeStruct(parts[0].shape, parts[0].dtype)], parts)[0]


def gather(block, piece):
    ns, nt = lax.axis_size("col"), lax.axis_size("row")
    blocks, pieces = {0: block}, {0: piece}
    for k in range(2, nt, 2):
        blocks[k] = swap(block, "row", k)
    for k in range(1, ns):
        pieces[k] = swap(piece, "col", k)
    near = {k: blocks[k] for k in range(0, nt, 2)}
    near, _ = lax.optimization_barrier((near, pieces))
    for k in range(0, nt, 2):
        blocks[k + 1] = swap(near[k], "row", 1)
    return [blocks[k] for k in range(nt)], [pieces[k] for k in range(ns)]


def per_device(source, target, target_potential, prev_moment):
    f32, shape = jnp.float32, jax.ShapeDtypeStruct
    ns, nt = lax.axis_size("col"), lax.axis_size("row")
    piece, width = source.shape[0], target.shape[0]
    depth = source.shape[1]
    rows, cols = piece * ns, width * nt
    rows_total, cols_total = rows * nt, cols * ns
    groups = width // LANES
    tail = jnp.pad(target_potential.reshape(groups, LANES), ((0, SUB - groups), (0, 0)))
    block = jnp.concatenate([target, tail], axis=0)
    t_blocks, s_pieces = gather(block, source)
    tile = shape((rows // LANES, LANES), f32)
    flops, exps = 2 * rows * cols * depth, rows * cols
    row_scores = pltpu.VMEM((2, LANES, cols), f32)

    lse, carried = call(
        functools.partial(couple_kernel, ns, nt, width),
        [tile, shape((rows, depth), f32)],
        s_pieces + t_blocks + [prev_moment],
        [pltpu.VMEM((rows, depth), jnp.bfloat16), row_scores],
        2 * flops,
        exps,
    )
    half = shape((depth // 2, depth), f32)
    keep, send = call(
        functools.partial(moment_kernel, ns, rows_total),
        [half, half],
        s_pieces + exchange(lse, "col") + [carried],
        [pltpu.VMEM(tile.shape, f32), pltpu.VMEM((depth, depth), f32)],
        6 * rows * depth * depth,
    )
    part = combine(add_kernel, [keep, swap(send, "row", 1)])
    part = combine(add_kernel, exchange(part, "col"))
    part = combine(add_kernel, exchange_chips(part))
    moment, a, lse, top, e = call(
        functools.partial(first_rows_kernel, ns, nt, width),
        [shape((depth, depth), f32), shape((rows, depth), jnp.bfloat16), tile, tile, shape((rows, cols), jnp.bfloat16)],
        s_pieces + t_blocks + [part, swap(part, "row", 1)],
        [row_scores],
        flops,
        exps,
    )
    for iteration in range(ITERS):
        last = iteration == ITERS - 1
        if iteration > 0:
            both = combine(log_sum_kernel, [column, swap(column, "row", 1)])
            lse, = call(
                functools.partial(rows_kernel, nt, width, rows_total),
                [tile],
                [a, e, top] + t_blocks + exchange_chips(both),
                [pltpu.VMEM((nt, width), f32), pltpu.VMEM((SUB, cols), jnp.bfloat16), row_scores],
                16 * rows * cols,
            )
        blocks = shape((nt // 2, 1, width), f32)
        column, *sent, source_potential = call(
            functools.partial(columns_kernel, ns, nt, width, cols_total, last),
            ([blocks, blocks] if last else [shape((nt, width), f32)]) + [tile],
            [a, e, top] + t_blocks + exchange(lse, "col"),
            [
                pltpu.VMEM(tile.shape, f32),
                pltpu.VMEM((SUB, rows), jnp.bfloat16),
                pltpu.VMEM((rows, LANES), f32),
                pltpu.VMEM((rows, width), f32),
            ],
            16 * rows * cols,
        )
    one = shape((1, width), f32)
    parts = call(split_kernel, [one] * (nt // 2), [column, swap(sent[0], "row", 1)])
    parts = [parts[0]] + [swap(x, "row", 2 * k) for k, x in enumerate(parts) if k > 0]
    update, = call(functools.partial(update_kernel, rows_total), [one], parts)
    return moment, source_potential.reshape(rows), update.reshape(width)


def solution(mesh):
    placed = (P(("row", "col"), None), P(("col", "row"), None), P(("col", "row")), P())
    return jax.shard_map(
        per_device,
        mesh=mesh,
        in_specs=placed,
        out_specs=(P(), P("row"), P(("col", "row"))),
        check_vma=False,
    )
```

```python
import functools
import math

import jax
import jax.numpy as jnp
from jax import lax
from jax.experimental import pallas as pl
from jax.experimental.pallas import tpu as pltpu
from jax.sharding import PartitionSpec as P

ITERS = 2
LANES = 128
SUB = 16
SMALLEST = 1e-16
LARGEST = 1e12
NT_DIMS = (((1,), (1,)), ((), ()))
TN_DIMS = (((0,), (0,)), ((), ()))


def split3(x):
    high = x.astype(jnp.bfloat16)
    rest = x - high.astype(jnp.float32)
    mid = rest.astype(jnp.bfloat16)
    low = (rest - mid.astype(jnp.float32)).astype(jnp.bfloat16)
    return high, mid, low


def project4(rows, matrix):
    total = None
    for part in reversed(split3(matrix)):
        term = jnp.dot(rows, part, preferred_element_type=jnp.float32)
        total = term if total is None else total + term
    return (total.astype(jnp.bfloat16).astype(jnp.float32) * 4.0).astype(jnp.bfloat16)


def lane_fold(op, x):
    parts = [x[:, i : i + LANES] for i in range(0, x.shape[1], LANES)]
    return functools.reduce(op, parts)


def as_lanes(column):
    return jnp.broadcast_to(column, (LANES, LANES)).T[0:1, :]


def as_rows(lanes):
    return jnp.broadcast_to(lanes, (LANES, LANES)).T


def tree(op, parts):
    while len(parts) > 1:
        parts = [op(parts[i], parts[i + 1]) for i in range(0, len(parts), 2)]
    return parts[0]


def log_sum(parts):
    top = functools.reduce(jnp.maximum, parts)
    return top + jnp.log(tree(jnp.add, [jnp.exp(p - top) for p in parts]))


def within(masses):
    low = jnp.min(functools.reduce(jnp.minimum, masses))
    high = jnp.max(functools.reduce(jnp.maximum, masses))
    return jnp.logical_and(low > SMALLEST, high < LARGEST)


def block_of(t_ref, g, width):
    return t_ref[g * width : (g + 1) * width, :LANES]


def shifted_rows(a_ref, t_ref, pot_ref, aug_ref, lse_ref, top_ref, mass_ref, e_ref, carried_ref=None):
    c = lax.axis_index("col")
    width = pot_ref.shape[1]
    blocks = pot_ref.shape[0]
    steps = a_ref.shape[0] // LANES
    per = steps // lax.axis_size("col")
    lane = lax.broadcasted_iota(jnp.int32, (LANES, LANES), 1)

    def row(i):
        return pl.ds((c ^ (i // per)) * per + i % per, 1)

    for i in range(steps):
        at = slice(i * LANES, (i + 1) * LANES)
        a = a_ref[at, :]
        s = lax.dot_general(a, block_of(t_ref, 0, width), NT_DIMS, preferred_element_type=jnp.float32)
        top = jnp.max(lane_fold(jnp.maximum, s + pot_ref[0:1, :]), axis=1, keepdims=True)
        top = top.astype(jnp.bfloat16).astype(jnp.float32)
        aug_ref[at, :LANES] = a
        aug_ref[at, LANES:] = jnp.where(lane == 0, 1.0, jnp.where(lane == 1, -top, 0.0)).astype(jnp.bfloat16)
        top_ref[row(i), :] = as_lanes(top)
    for i in range(steps + 1):
        mass, carried = None, None
        for g in range(blocks):
            cols = slice(g * width, (g + 1) * width)
            if i < steps:
                at = slice(i * LANES, (i + 1) * LANES)
                s = lax.dot_general(aug_ref[at, :], t_ref[cols, :], NT_DIMS, preferred_element_type=jnp.float32)
                e = jnp.exp(s)
                m = lane_fold(jnp.add, e)
                mass = m if mass is None else mass + m
                e_ref[at, cols] = e.astype(jnp.bfloat16)
            if i > 0 and carried_ref is not None:
                before = slice((i - 1) * LANES, i * LANES)
                d = jnp.dot(e_ref[before, cols], block_of(t_ref, g, width), preferred_element_type=jnp.float32)
                carried = d if carried is None else carried + d
        if i > 0 and carried_ref is not None:
            carried_ref[before, :] = carried / last_mass
        if i < steps:
            last_mass = jnp.sum(mass, axis=1, keepdims=True)
            mass_ref[row(i), :] = as_lanes(last_mass)
    lse_ref[...] = top_ref[...] + jnp.log(mass_ref[...])
    return within([mass_ref[...]])


def exact_rows(a_ref, t_ref, column, scores, lse_ref, top_ref=None, e_ref=None, carried_ref=None):
    c = lax.axis_index("col")
    steps = a_ref.shape[0] // LANES
    per = steps // lax.axis_size("col")
    width = column[0].shape[1]

    @pl.loop(0, steps)
    def _(i):
        rows = pl.ds(pl.multiple_of(i * LANES, LANES), LANES)
        top = None
        for g in range(len(column)):
            t = block_of(t_ref, g, width)
            s = column[g] + lax.dot_general(a_ref[rows, :], t, NT_DIMS, preferred_element_type=jnp.float32)
            scores[:, g * width : (g + 1) * width] = s
            m = lane_fold(jnp.maximum, s)
            top = m if top is None else jnp.maximum(top, m)
        top = jnp.max(top, axis=1, keepdims=True)
        mass, carried = None, None
        for g in range(len(column)):
            cols = slice(g * width, (g + 1) * width)
            e = jnp.exp(scores[:, cols] - top)
            m = lane_fold(jnp.add, e)
            mass = m if mass is None else mass + m
            if e_ref is not None:
                e_ref[rows, cols] = e.astype(jnp.bfloat16)
            if carried_ref is not None:
                t = block_of(t_ref, g, width)
                d = jnp.dot(e.astype(jnp.bfloat16), t, preferred_element_type=jnp.float32)
                carried = d if carried is None else carried + d
        mass = jnp.sum(mass, axis=1, keepdims=True)
        row = pl.ds((c ^ (i // per)) * per + i % per, 1)
        lse_ref[row, :] = as_lanes(top + jnp.log(mass))
        if top_ref is not None:
            top_ref[row, :] = as_lanes(top)
        if carried_ref is not None:
            carried_ref[rows, :] = carried / mass


def project_kernel(ns, *refs):
    s_refs, moment_ref, a_ref = refs[:ns], refs[ns], refs[ns + 1]
    piece = s_refs[0].shape[0]
    for k in range(ns):
        a_ref[k * piece : (k + 1) * piece, :] = project4(s_refs[k][...], moment_ref[...])


def couple_kernel(nt, width, *refs):
    a_ref, t_refs = refs[0], refs[1 : 1 + nt]
    lse_ref, carried_ref, t_ref, pot_ref, top_ref, mass_ref, e_ref, aug_ref, scores = refs[1 + nt :]
    lane = lax.broadcasted_iota(jnp.int32, (LANES, LANES), 1)
    for g in range(nt):
        t_ref[g * width : (g + 1) * width, :LANES] = t_refs[g][:width, :]
        potential = t_refs[g][width:, :].astype(jnp.float32)
        for j in range(width // LANES):
            row = potential[j : j + 1, :]
            at = g * width + j * LANES
            added = jnp.where(lane == 0, as_rows(row), jnp.where(lane == 1, 1.0, 0.0))
            t_ref[at : at + LANES, LANES:] = added.astype(jnp.bfloat16)
            pot_ref[g : g + 1, j * LANES : (j + 1) * LANES] = row
    fine = shifted_rows(a_ref, t_ref, pot_ref, aug_ref, lse_ref, top_ref, mass_ref, e_ref, carried_ref)

    @pl.when(jnp.logical_not(fine))
    def _():
        column = [pot_ref[g : g + 1, :] for g in range(nt)]
        exact_rows(a_ref, t_ref, column, scores, lse_ref, None, None, carried_ref)


def moment_kernel(ns, rows_total, *refs):
    s_refs, l_refs, carried_ref = refs[:ns], refs[ns : 2 * ns], refs[2 * ns]
    keep_ref, send_ref, weight_ref, total_ref = refs[2 * ns + 1 :]
    c, r = lax.axis_index("col"), lax.axis_index("row")
    piece = s_refs[0].shape[0]
    per = piece // LANES
    shift = log_sum([l[...] for l in l_refs])
    weight_ref[...] = jnp.exp(l_refs[0][...] - shift) * (1.0 / rows_total)
    total = None
    for k in range(ns):
        for j in range(per):
            w = as_rows(weight_ref[pl.ds((c ^ k) * per + j, 1), :])
            at = (k * per + j) * LANES
            x = carried_ref[at : at + LANES, :] * w
            s = s_refs[k][j * LANES : (j + 1) * LANES, :]
            for part in reversed(split3(x)):
                term = lax.dot_general(s, part, TN_DIMS, preferred_element_type=jnp.float32)
                total = term if total is None else total + term
    total_ref[...] = total
    half = keep_ref.shape[0]
    keep_ref[...] = total_ref[pl.ds(pl.multiple_of((r % 2) * half, half), half), :]
    send_ref[...] = total_ref[pl.ds(pl.multiple_of((1 - r % 2) * half, half), half), :]


def add_kernel(*refs):
    refs[-1][...] = tree(jnp.add, [r[...] for r in refs[:-1]])


def log_sum_kernel(*refs):
    refs[-1][...] = log_sum([r[...] for r in refs[:-1]])


def first_rows_kernel(ns, *refs):
    s_refs, t_ref, pot_ref, m_refs = refs[:ns], refs[ns], refs[ns + 1], refs[ns + 2 : ns + 4]
    moment_ref, a_ref, lse_ref, top_ref, e_ref, mass_ref, aug_ref, scores = refs[ns + 4 :]
    r = lax.axis_index("row")
    piece, half = s_refs[0].shape[0], m_refs[0].shape[0]
    for k in range(2):
        moment_ref[pl.ds(pl.multiple_of((k ^ (r % 2)) * half, half), half), :] = m_refs[k][...]
    for k in range(ns):
        a_ref[k * piece : (k + 1) * piece, :] = project4(s_refs[k][...], moment_ref[...])
    fine = shifted_rows(a_ref, t_ref, pot_ref, aug_ref, lse_ref, top_ref, mass_ref, e_ref)

    @pl.when(jnp.logical_not(fine))
    def _():
        column = [pot_ref[g : g + 1, :] for g in range(pot_ref.shape[0])]
        exact_rows(a_ref, t_ref, column, scores, lse_ref, top_ref, e_ref)


def high_low(x):
    high = x.astype(jnp.bfloat16).astype(jnp.float32)
    at = lax.broadcasted_iota(jnp.int32, (SUB, x.shape[1]), 0)
    return jnp.where(at == 0, high, jnp.where(at == 1, x - high, 0.0)).astype(jnp.bfloat16)


def rows_kernel(rows_total, *refs):
    a_ref, e_ref, top_ref, t_ref, pot_ref = refs[:5]
    l_refs, (lse_ref, column_ref, weights, scores) = refs[5:-4], refs[-4:]
    c, r = lax.axis_index("col"), lax.axis_index("row")
    nt, width = pot_ref.shape
    column_ref[...] = math.log(rows_total) - log_sum([l[...] for l in l_refs])
    column = [column_ref[pl.ds(r ^ k, 1), :] for k in range(nt)]
    change = [column[k] - pot_ref[k : k + 1, :] for k in range(nt)]
    top = jnp.max(functools.reduce(jnp.maximum, change), axis=1, keepdims=True)
    for k in range(nt):
        weights[:, k * width : (k + 1) * width] = high_low(jnp.exp(change[k] - top))
    steps = a_ref.shape[0] // LANES
    per = steps // lax.axis_size("col")
    masses = []
    for i in range(steps):
        e = e_ref[i * LANES : (i + 1) * LANES, :]
        sums = lax.dot_general(weights[...], e, NT_DIMS, preferred_element_type=jnp.float32)
        masses.append(sums[0:1, :] + sums[1:2, :])
        row = pl.ds((c ^ (i // per)) * per + i % per, 1)
        lse_ref[row, :] = top + top_ref[row, :] + jnp.log(masses[i])

    @pl.when(jnp.logical_not(within(masses)))
    def _():
        exact_rows(a_ref, t_ref, column, scores, lse_ref)


def columns_kernel(ns, cols_total, last, *refs):
    a_ref, e_ref, top_ref, t_ref, pot_ref, l_refs = *refs[:5], refs[5 : 5 + ns]
    out_refs, (sp_ref, weight_rows, weights, spread_rows, scores) = refs[5 + ns : -5], refs[-5:]
    c, r = lax.axis_index("col"), lax.axis_index("row")
    nt, width = pot_ref.shape
    rows = a_ref.shape[0]
    per = rows // ns // LANES
    potential = math.log(cols_total) - log_sum([l[...] for l in l_refs])
    sp_ref[...] = potential
    shift = potential + top_ref[...]
    top = jnp.max(jnp.max(shift, axis=1, keepdims=True), axis=0, keepdims=True)
    weight_rows[...] = jnp.exp(shift - top)
    for k in range(ns):
        for j in range(per):
            at = (k * per + j) * LANES
            weights[:, at : at + LANES] = high_low(weight_rows[pl.ds((c ^ k) * per + j, 1), :])

    def store(g, lse):
        if last:
            out_refs[g % 2][g // 2] = lse
        else:
            out_refs[0][pl.ds(r ^ g, 1), :] = lse

    masses = []
    for g in range(nt):
        e = e_ref[:, g * width : (g + 1) * width]
        sums = jnp.dot(weights[...], e, preferred_element_type=jnp.float32)
        masses.append(sums[0:1, :] + sums[1:2, :])
        store(g, top - pot_ref[g : g + 1, :] + jnp.log(masses[g]))

    @pl.when(jnp.logical_not(within(masses)))
    def _():
        exact_columns(ns, a_ref, t_ref, sp_ref, spread_rows, scores, store)


def exact_columns(ns, a_ref, t_ref, sp_ref, spread_rows, scores, store):
    c = lax.axis_index("col")
    rows, width = scores.shape
    per = rows // ns // LANES
    for k in range(ns):
        for j in range(per):
            at = (k * per + j) * LANES
            spread_rows[at : at + LANES, :] = as_rows(sp_ref[pl.ds((c ^ k) * per + j, 1), :])
    for g in range(t_ref.shape[0] // width):
        top = None
        for at in range(0, rows, LANES):
            a = a_ref[at : at + LANES, :]
            s = lax.dot_general(a, block_of(t_ref, g, width), NT_DIMS, preferred_element_type=jnp.float32)
            s = s + jnp.concatenate([spread_rows[at : at + LANES, :]] * (width // LANES), axis=1)
            scores[at : at + LANES, :] = s
            m = jnp.max(s.reshape(LANES // 8, 8, width), axis=0)
            top = m if top is None else jnp.maximum(top, m)
        top = jnp.max(top, axis=0, keepdims=True)
        mass = None
        for at in range(0, rows, LANES):
            e = jnp.exp(scores[at : at + LANES, :] - top)
            m = jnp.sum(e.reshape(LANES // 8, 8, width), axis=0)
            mass = m if mass is None else mass + m
        store(g, top + jnp.log(jnp.sum(mass, axis=0, keepdims=True)))


def split_kernel(x_ref, y_ref, *out_refs):
    for k, out_ref in enumerate(out_refs):
        out_ref[...] = log_sum([x_ref[k], y_ref[k]])


def update_kernel(rows_total, *refs):
    refs[-1][...] = math.log(rows_total) - log_sum([l[...] for l in refs[:-1]])


def call(kernel, out, args, scratch=(), flops=0, exps=0):
    vmem = pl.BlockSpec(memory_space=pltpu.VMEM)
    bytes_accessed = sum(x.size * x.dtype.itemsize for x in list(args) + list(out))
    return pl.pallas_call(
        kernel,
        out_shape=list(out),
        in_specs=[vmem] * len(args),
        out_specs=[vmem] * len(out),
        scratch_shapes=list(scratch),
        compiler_params=pltpu.CompilerParams(vmem_limit_bytes=24 << 20),
        cost_estimate=pl.CostEstimate(flops=flops, bytes_accessed=bytes_accessed, transcendentals=exps),
    )(*args)


def swap(x, axis, k):
    return lax.ppermute(x, axis, [(i, i ^ k) for i in range(lax.axis_size(axis))])


def exchange(x, axis):
    return [x] + [swap(x, axis, k) for k in range(1, lax.axis_size(axis))]


def exchange_chips(x):
    return [x] + [swap(x, "row", k) for k in range(2, lax.axis_size("row"), 2)]


def combine(kernel, parts):
    return call(kernel, [jax.ShapeDtypeStruct(parts[0].shape, parts[0].dtype)], parts)[0]


def per_device(source, target, target_potential, prev_moment):
    f32, bf16, shape = jnp.float32, jnp.bfloat16, jax.ShapeDtypeStruct
    ns, nt = lax.axis_size("col"), lax.axis_size("row")
    piece, width = source.shape[0], target.shape[0]
    depth = source.shape[1]
    rows, cols = piece * ns, width * nt
    rows_total, cols_total = rows * nt, cols * ns
    tile = shape((rows // LANES, LANES), f32)
    projected = shape((rows, depth), bf16)
    flops, exps = 2 * rows * cols * depth, rows * cols
    row_scores = pltpu.VMEM((LANES, cols), f32)
    small = pltpu.VMEM(tile.shape, f32)
    augmented = pltpu.VMEM((rows, 2 * depth), bf16)

    groups = width // LANES
    tail = jnp.pad(target_potential.reshape(groups, LANES), ((0, SUB - groups), (0, 0)))
    block = jnp.concatenate([target, tail], axis=0)
    far = exchange_chips(block)
    pieces = exchange(source, "col")
    a, = call(functools.partial(project_kernel, ns), [projected], pieces + [prev_moment], flops=6 * rows * depth * depth)
    far, a = lax.optimization_barrier((far, a))
    blocks = [x for pair in zip(far, [swap(x, "row", 1) for x in far]) for x in pair]
    lse, carried, t, pot = call(
        functools.partial(couple_kernel, nt, width),
        [tile, shape((rows, depth), f32), shape((cols, 2 * depth), bf16), shape((nt, width), f32)],
        [a] + blocks,
        [small, small, pltpu.VMEM((rows, cols), bf16), augmented, row_scores],
        2 * flops,
        exps,
    )
    half = shape((depth // 2, depth), f32)
    keep, send = call(
        functools.partial(moment_kernel, ns, rows_total),
        [half, half],
        pieces + exchange(lse, "col") + [carried],
        [small, pltpu.VMEM((depth, depth), f32)],
        6 * rows * depth * depth,
    )
    part = combine(add_kernel, [keep, swap(send, "row", 1)])
    part = combine(add_kernel, exchange(part, "col"))
    part = combine(add_kernel, exchange_chips(part))
    moment, a, lse, top, e = call(
        functools.partial(first_rows_kernel, ns),
        [shape((depth, depth), f32), projected, tile, tile, shape((rows, cols), bf16)],
        pieces + [t, pot, part, swap(part, "row", 1)],
        [small, augmented, row_scores],
        flops,
        exps,
    )
    for iteration in range(ITERS):
        last = iteration == ITERS - 1
        if iteration > 0:
            both = combine(log_sum_kernel, [column, swap(column, "row", 1)])
            lse, = call(
                functools.partial(rows_kernel, rows_total),
                [tile],
                [a, e, top, t, pot] + exchange_chips(both),
                [pltpu.VMEM((nt, width), f32), pltpu.VMEM((SUB, cols), bf16), row_scores],
                16 * rows * cols,
            )
        halves = shape((nt // 2, 1, width), f32)
        column, *sent, source_potential = call(
            functools.partial(columns_kernel, ns, cols_total, last),
            ([halves, halves] if last else [shape((nt, width), f32)]) + [tile],
            [a, e, top, t, pot] + exchange(lse, "col"),
            [
                small,
                pltpu.VMEM((SUB, rows), bf16),
                pltpu.VMEM((rows, LANES), f32),
                pltpu.VMEM((rows, width), f32),
            ],
            16 * rows * cols,
        )
    one = shape((1, width), f32)
    parts = call(split_kernel, [one] * (nt // 2), [column, swap(sent[0], "row", 1)])
    parts = [parts[0]] + [swap(x, "row", 2 * k) for k, x in enumerate(parts) if k > 0]
    update, = call(functools.partial(update_kernel, rows_total), [one], parts)
    return moment, source_potential.reshape(rows), update.reshape(width)


def solution(mesh):
    placed = (P(("row", "col"), None), P(("col", "row"), None), P(("col", "row")), P())
    return jax.shard_map(
        per_device,
        mesh=mesh,
        in_specs=placed,
        out_specs=(P(), P("row"), P(("col", "row"))),
        check_vma=False,
    )
```

```python
import functools
import math

import jax
import jax.numpy as jnp
from jax import lax
from jax.experimental import pallas as pl
from jax.experimental.pallas import tpu as pltpu
from jax.sharding import PartitionSpec as P

ITERS = 2
LANES = 128
SUB = 16
SMALLEST = 1e-16
LARGEST = 1e12
NT_DIMS = (((1,), (1,)), ((), ()))
TN_DIMS = (((0,), (0,)), ((), ()))


def split3(x):
    high = x.astype(jnp.bfloat16)
    rest = x - high.astype(jnp.float32)
    mid = rest.astype(jnp.bfloat16)
    low = (rest - mid.astype(jnp.float32)).astype(jnp.bfloat16)
    return high, mid, low


def project4(rows, matrix_parts):
    total = None
    for part in reversed(matrix_parts):
        term = jnp.dot(rows, part, preferred_element_type=jnp.float32)
        total = term if total is None else total + term
    return (total.astype(jnp.bfloat16).astype(jnp.float32) * 4.0).astype(jnp.bfloat16)


def lane_fold(op, x):
    parts = [x[:, i : i + LANES] for i in range(0, x.shape[1], LANES)]
    return functools.reduce(op, parts)


def as_lanes(column):
    return jnp.broadcast_to(column, (LANES, LANES)).T[0:1, :]


def as_rows(lanes):
    return jnp.broadcast_to(lanes, (LANES, LANES)).T


def tree(op, parts):
    while len(parts) > 1:
        parts = [op(parts[i], parts[i + 1]) for i in range(0, len(parts), 2)]
    return parts[0]


def log_sum(parts):
    top = functools.reduce(jnp.maximum, parts)
    return top + jnp.log(tree(jnp.add, [jnp.exp(p - top) for p in parts]))


def within(masses):
    low = jnp.min(functools.reduce(jnp.minimum, masses))
    high = jnp.max(functools.reduce(jnp.maximum, masses))
    return jnp.logical_and(low > SMALLEST, high < LARGEST)


def block_of(t_ref, g, width):
    return t_ref[g * width : (g + 1) * width, :LANES]


def shifted_rows(a_ref, t_ref, pot_ref, aug_ref, lse_ref, top_ref, mass_ref, scores, e_ref=None, carried_ref=None):
    c = lax.axis_index("col")
    width = pot_ref.shape[1]
    blocks = pot_ref.shape[0]
    steps = a_ref.shape[0] // LANES
    per = steps // lax.axis_size("col")
    lane = lax.broadcasted_iota(jnp.int32, (LANES, LANES), 1)

    def row(i):
        return pl.ds((c ^ (i // per)) * per + i % per, 1)

    for i in range(steps):
        at = slice(i * LANES, (i + 1) * LANES)
        a = a_ref[at, :]
        s = lax.dot_general(a, block_of(t_ref, 0, width), NT_DIMS, preferred_element_type=jnp.float32)
        top = jnp.max(lane_fold(jnp.maximum, s + pot_ref[0:1, :]), axis=1, keepdims=True)
        top = top.astype(jnp.bfloat16).astype(jnp.float32)
        aug_ref[at, :LANES] = a
        aug_ref[at, LANES:] = jnp.where(lane == 0, 1.0, jnp.where(lane == 1, -top, 0.0)).astype(jnp.bfloat16)
        top_ref[row(i), :] = as_lanes(top)
    rows = a_ref.shape[0]
    half = rows // 2
    for g in range(blocks + 1):
        for h in range(0, rows, half):
            at = slice(h, h + half)
            if g < blocks:
                t = t_ref[g * width : (g + 1) * width, :]
                scores[g % 2, at, :] = lax.dot_general(aug_ref[at, :], t, NT_DIMS, preferred_element_type=jnp.float32)
            if g > 0:
                e = jnp.exp(scores[(g - 1) % 2, at, :])
                m = lane_fold(jnp.add, e)
                mass_ref[at, :] = m if g == 1 else mass_ref[at, :] + m
                e = e.astype(jnp.bfloat16)
                if e_ref is not None:
                    e_ref[at, (g - 1) * width : g * width] = e
                if carried_ref is not None:
                    d = jnp.dot(e, block_of(t_ref, g - 1, width), preferred_element_type=jnp.float32)
                    carried_ref[at, :] = d if g == 1 else carried_ref[at, :] + d
    masses = []
    for i in range(steps):
        at = slice(i * LANES, (i + 1) * LANES)
        mass = jnp.sum(mass_ref[at, :], axis=1, keepdims=True)
        masses.append(as_lanes(mass))
        lse_ref[row(i), :] = top_ref[row(i), :] + jnp.log(masses[i])
        if carried_ref is not None:
            carried_ref[at, :] = carried_ref[at, :] / mass
    return within(masses)


def exact_rows(a_ref, t_ref, column, scores, lse_ref, top_ref=None, e_ref=None, carried_ref=None):
    c = lax.axis_index("col")
    steps = a_ref.shape[0] // LANES
    per = steps // lax.axis_size("col")
    width = column[0].shape[1]

    @pl.loop(0, steps)
    def _(i):
        rows = pl.ds(pl.multiple_of(i * LANES, LANES), LANES)
        top = None
        for g in range(len(column)):
            t = block_of(t_ref, g, width)
            s = column[g] + lax.dot_general(a_ref[rows, :], t, NT_DIMS, preferred_element_type=jnp.float32)
            scores[:, g * width : (g + 1) * width] = s
            m = lane_fold(jnp.maximum, s)
            top = m if top is None else jnp.maximum(top, m)
        top = jnp.max(top, axis=1, keepdims=True)
        mass, carried = None, None
        for g in range(len(column)):
            cols = slice(g * width, (g + 1) * width)
            e = jnp.exp(scores[:, cols] - top)
            m = lane_fold(jnp.add, e)
            mass = m if mass is None else mass + m
            if e_ref is not None:
                e_ref[rows, cols] = e.astype(jnp.bfloat16)
            if carried_ref is not None:
                t = block_of(t_ref, g, width)
                d = jnp.dot(e.astype(jnp.bfloat16), t, preferred_element_type=jnp.float32)
                carried = d if carried is None else carried + d
        mass = jnp.sum(mass, axis=1, keepdims=True)
        row = pl.ds((c ^ (i // per)) * per + i % per, 1)
        lse_ref[row, :] = as_lanes(top + jnp.log(mass))
        if top_ref is not None:
            top_ref[row, :] = as_lanes(top)
        if carried_ref is not None:
            carried_ref[rows, :] = carried / mass


def own_kernel(own_ref, moment_ref, s_ref, a_ref, parts_ref):
    s_ref[...] = own_ref[...]
    for k, part in enumerate(split3(moment_ref[...])):
        parts_ref[k] = part
    a_ref[...] = project4(own_ref[...], split3(moment_ref[...]))


def project_kernel(ns, *refs):
    s_refs, a_own_ref, parts_ref, s_ref, a_ref = refs[:ns], *refs[ns:]
    piece = a_own_ref.shape[0]
    a_ref[:piece, :] = a_own_ref[...]
    for k in range(ns):
        at = slice(k * piece, (k + 1) * piece)
        s_ref[at, :] = s_refs[k][...]
        if k > 0:
            a_ref[at, :] = project4(s_refs[k][...], [parts_ref[i] for i in range(3)])


def couple_kernel(nt, width, *refs):
    a_ref, t_refs = refs[0], refs[1 : 1 + nt]
    lse_ref, carried_ref, t_ref, pot_ref, top_ref, mass_ref, aug_ref, ahead, scores = refs[1 + nt :]
    lane = lax.broadcasted_iota(jnp.int32, (LANES, LANES), 1)
    for g in range(nt):
        t_ref[g * width : (g + 1) * width, :LANES] = t_refs[g][:width, :]
        potential = t_refs[g][width:, :].astype(jnp.float32)
        for j in range(width // LANES):
            row = potential[j : j + 1, :]
            at = g * width + j * LANES
            added = jnp.where(lane == 0, as_rows(row), jnp.where(lane == 1, 1.0, 0.0))
            t_ref[at : at + LANES, LANES:] = added.astype(jnp.bfloat16)
            pot_ref[g : g + 1, j * LANES : (j + 1) * LANES] = row
    fine = shifted_rows(a_ref, t_ref, pot_ref, aug_ref, lse_ref, top_ref, mass_ref, ahead, None, carried_ref)

    @pl.when(jnp.logical_not(fine))
    def _():
        column = [pot_ref[g : g + 1, :] for g in range(nt)]
        exact_rows(a_ref, t_ref, column, scores, lse_ref, None, None, carried_ref)


def moment_kernel(ns, rows_total, *refs):
    s_ref, l_refs, carried_ref = refs[0], refs[1 : 1 + ns], refs[1 + ns]
    keep_ref, send_ref, weight_ref, total_ref = refs[2 + ns :]
    c, r = lax.axis_index("col"), lax.axis_index("row")
    per = s_ref.shape[0] // ns // LANES
    shift = log_sum([l[...] for l in l_refs])
    weight_ref[...] = jnp.exp(l_refs[0][...] - shift) * (1.0 / rows_total)
    total = None
    for k in range(ns):
        for j in range(per):
            w = as_rows(weight_ref[pl.ds((c ^ k) * per + j, 1), :])
            at = (k * per + j) * LANES
            x = carried_ref[at : at + LANES, :] * w
            s = s_ref[at : at + LANES, :]
            for part in reversed(split3(x)):
                term = lax.dot_general(s, part, TN_DIMS, preferred_element_type=jnp.float32)
                total = term if total is None else total + term
    total_ref[...] = total
    half = keep_ref.shape[0]
    keep_ref[...] = total_ref[pl.ds(pl.multiple_of((r % 2) * half, half), half), :]
    send_ref[...] = total_ref[pl.ds(pl.multiple_of((1 - r % 2) * half, half), half), :]


def add_kernel(*refs):
    refs[-1][...] = tree(jnp.add, [r[...] for r in refs[:-1]])


def log_sum_kernel(*refs):
    refs[-1][...] = log_sum([r[...] for r in refs[:-1]])


def first_rows_kernel(*refs):
    s_ref, t_ref, pot_ref, m_refs = refs[0], refs[1], refs[2], refs[3:5]
    moment_ref, a_ref, lse_ref, top_ref, e_ref, mass_ref, aug_ref, ahead, scores = refs[5:]
    r = lax.axis_index("row")
    half = m_refs[0].shape[0]
    for k in range(2):
        moment_ref[pl.ds(pl.multiple_of((k ^ (r % 2)) * half, half), half), :] = m_refs[k][...]
    a_ref[...] = project4(s_ref[...], split3(moment_ref[...]))
    fine = shifted_rows(a_ref, t_ref, pot_ref, aug_ref, lse_ref, top_ref, mass_ref, ahead, e_ref)

    @pl.when(jnp.logical_not(fine))
    def _():
        column = [pot_ref[g : g + 1, :] for g in range(pot_ref.shape[0])]
        exact_rows(a_ref, t_ref, column, scores, lse_ref, top_ref, e_ref)


def high_low(x):
    high = x.astype(jnp.bfloat16).astype(jnp.float32)
    at = lax.broadcasted_iota(jnp.int32, (SUB, x.shape[1]), 0)
    return jnp.where(at == 0, high, jnp.where(at == 1, x - high, 0.0)).astype(jnp.bfloat16)


def rows_kernel(rows_total, *refs):
    a_ref, e_ref, top_ref, t_ref, pot_ref = refs[:5]
    l_refs, (lse_ref, column_ref, weights, scores) = refs[5:-4], refs[-4:]
    c, r = lax.axis_index("col"), lax.axis_index("row")
    nt, width = pot_ref.shape
    column_ref[...] = math.log(rows_total) - log_sum([l[...] for l in l_refs])
    column = [column_ref[pl.ds(r ^ k, 1), :] for k in range(nt)]
    change = [column[k] - pot_ref[k : k + 1, :] for k in range(nt)]
    top = jnp.max(functools.reduce(jnp.maximum, change), axis=1, keepdims=True)
    for k in range(nt):
        weights[:, k * width : (k + 1) * width] = high_low(jnp.exp(change[k] - top))
    steps = a_ref.shape[0] // LANES
    per = steps // lax.axis_size("col")
    masses = []
    for i in range(steps):
        e = e_ref[i * LANES : (i + 1) * LANES, :]
        sums = lax.dot_general(weights[...], e, NT_DIMS, preferred_element_type=jnp.float32)
        masses.append(sums[0:1, :] + sums[1:2, :])
        row = pl.ds((c ^ (i // per)) * per + i % per, 1)
        lse_ref[row, :] = top + top_ref[row, :] + jnp.log(masses[i])

    @pl.when(jnp.logical_not(within(masses)))
    def _():
        exact_rows(a_ref, t_ref, column, scores, lse_ref)


def columns_kernel(ns, cols_total, last, *refs):
    a_ref, e_ref, top_ref, t_ref, pot_ref, l_refs = *refs[:5], refs[5 : 5 + ns]
    out_refs, (sp_ref, weight_rows, weights, spread_rows, scores) = refs[5 + ns : -5], refs[-5:]
    c, r = lax.axis_index("col"), lax.axis_index("row")
    nt, width = pot_ref.shape
    rows = a_ref.shape[0]
    per = rows // ns // LANES
    potential = math.log(cols_total) - log_sum([l[...] for l in l_refs])
    sp_ref[...] = potential
    shift = potential + top_ref[...]
    top = jnp.max(jnp.max(shift, axis=1, keepdims=True), axis=0, keepdims=True)
    weight_rows[...] = jnp.exp(shift - top)
    for k in range(ns):
        for j in range(per):
            at = (k * per + j) * LANES
            weights[:, at : at + LANES] = high_low(weight_rows[pl.ds((c ^ k) * per + j, 1), :])

    def store(g, lse):
        if last:
            out_refs[g % 2][g // 2] = lse
        else:
            out_refs[0][pl.ds(r ^ g, 1), :] = lse

    masses = []
    for g in range(nt):
        e = e_ref[:, g * width : (g + 1) * width]
        sums = jnp.dot(weights[...], e, preferred_element_type=jnp.float32)
        masses.append(sums[0:1, :] + sums[1:2, :])
        store(g, top - pot_ref[g : g + 1, :] + jnp.log(masses[g]))

    @pl.when(jnp.logical_not(within(masses)))
    def _():
        exact_columns(ns, a_ref, t_ref, sp_ref, spread_rows, scores, store)


def exact_columns(ns, a_ref, t_ref, sp_ref, spread_rows, scores, store):
    c = lax.axis_index("col")
    rows, width = scores.shape
    per = rows // ns // LANES
    for k in range(ns):
        for j in range(per):
            at = (k * per + j) * LANES
            spread_rows[at : at + LANES, :] = as_rows(sp_ref[pl.ds((c ^ k) * per + j, 1), :])
    for g in range(t_ref.shape[0] // width):
        top = None
        for at in range(0, rows, LANES):
            a = a_ref[at : at + LANES, :]
            s = lax.dot_general(a, block_of(t_ref, g, width), NT_DIMS, preferred_element_type=jnp.float32)
            s = s + jnp.concatenate([spread_rows[at : at + LANES, :]] * (width // LANES), axis=1)
            scores[at : at + LANES, :] = s
            m = jnp.max(s.reshape(LANES // 8, 8, width), axis=0)
            top = m if top is None else jnp.maximum(top, m)
        top = jnp.max(top, axis=0, keepdims=True)
        mass = None
        for at in range(0, rows, LANES):
            e = jnp.exp(scores[at : at + LANES, :] - top)
            m = jnp.sum(e.reshape(LANES // 8, 8, width), axis=0)
            mass = m if mass is None else mass + m
        store(g, top + jnp.log(jnp.sum(mass, axis=0, keepdims=True)))


def split_kernel(x_ref, y_ref, *out_refs):
    for k, out_ref in enumerate(out_refs):
        out_ref[...] = log_sum([x_ref[k], y_ref[k]])


def update_kernel(rows_total, *refs):
    refs[-1][...] = math.log(rows_total) - log_sum([l[...] for l in refs[:-1]])


def call(kernel, out, args, scratch=(), flops=0, exps=0):
    vmem = pl.BlockSpec(memory_space=pltpu.VMEM)
    bytes_accessed = sum(x.size * x.dtype.itemsize for x in list(args) + list(out))
    return pl.pallas_call(
        kernel,
        out_shape=list(out),
        in_specs=[vmem] * len(args),
        out_specs=[vmem] * len(out),
        scratch_shapes=list(scratch),
        compiler_params=pltpu.CompilerParams(vmem_limit_bytes=24 << 20),
        cost_estimate=pl.CostEstimate(flops=flops, bytes_accessed=bytes_accessed, transcendentals=exps),
    )(*args)


def swap(x, axis, k):
    return lax.ppermute(x, axis, [(i, i ^ k) for i in range(lax.axis_size(axis))])


def exchange(x, axis):
    return [x] + [swap(x, axis, k) for k in range(1, lax.axis_size(axis))]


def exchange_chips(x):
    return [x] + [swap(x, "row", k) for k in range(2, lax.axis_size("row"), 2)]


def combine(kernel, parts):
    return call(kernel, [jax.ShapeDtypeStruct(parts[0].shape, parts[0].dtype)], parts)[0]


def per_device(source, target, target_potential, prev_moment):
    f32, bf16, shape = jnp.float32, jnp.bfloat16, jax.ShapeDtypeStruct
    ns, nt = lax.axis_size("col"), lax.axis_size("row")
    piece, width = source.shape[0], target.shape[0]
    depth = source.shape[1]
    rows, cols = piece * ns, width * nt
    rows_total, cols_total = rows * nt, cols * ns
    tile = shape((rows // LANES, LANES), f32)
    projected = shape((rows, depth), bf16)
    flops, exps = 2 * rows * cols * depth, rows * cols
    row_scores = pltpu.VMEM((LANES, cols), f32)
    small = pltpu.VMEM(tile.shape, f32)
    sums = pltpu.VMEM((rows, LANES), f32)
    ahead = pltpu.VMEM((2, rows, width), f32)
    augmented = pltpu.VMEM((rows, 2 * depth), bf16)

    groups = width // LANES
    tail = jnp.pad(target_potential.reshape(groups, LANES), ((0, SUB - groups), (0, 0)))
    block = jnp.concatenate([target, tail], axis=0)
    far = exchange_chips(block)
    pieces = exchange(source, "col")
    own = shape((piece, depth), bf16)
    s_own, a_own, moment_parts = call(
        own_kernel, [own, own, shape((3, depth, depth), bf16)], [source, prev_moment], flops=6 * piece * depth * depth
    )
    s, a = call(
        functools.partial(project_kernel, ns),
        [projected, projected],
        [s_own] + pieces[1:] + [a_own, moment_parts],
        flops=6 * rows * depth * depth,
    )
    far, a = lax.optimization_barrier((far, a))
    blocks = [x for pair in zip(far, [swap(x, "row", 1) for x in far]) for x in pair]
    lse, carried, t, pot = call(
        functools.partial(couple_kernel, nt, width),
        [tile, shape((rows, depth), f32), shape((cols, 2 * depth), bf16), shape((nt, width), f32)],
        [a] + blocks,
        [small, sums, augmented, ahead, row_scores],
        2 * flops,
        exps,
    )
    half = shape((depth // 2, depth), f32)
    keep, send = call(
        functools.partial(moment_kernel, ns, rows_total),
        [half, half],
        [s] + exchange(lse, "col") + [carried],
        [small, pltpu.VMEM((depth, depth), f32)],
        6 * rows * depth * depth,
    )
    part = combine(add_kernel, [keep, swap(send, "row", 1)])
    part = combine(add_kernel, exchange(part, "col"))
    part = combine(add_kernel, exchange_chips(part))
    moment, a, lse, top, e = call(
        first_rows_kernel,
        [shape((depth, depth), f32), projected, tile, tile, shape((rows, cols), bf16)],
        [s, t, pot, part, swap(part, "row", 1)],
        [sums, augmented, ahead, row_scores],
        flops,
        exps,
    )
    for iteration in range(ITERS):
        last = iteration == ITERS - 1
        if iteration > 0:
            both = combine(log_sum_kernel, [column, swap(column, "row", 1)])
            lse, = call(
                functools.partial(rows_kernel, rows_total),
                [tile],
                [a, e, top, t, pot] + exchange_chips(both),
                [pltpu.VMEM((nt, width), f32), pltpu.VMEM((SUB, cols), bf16), row_scores],
                16 * rows * cols,
            )
        halves = shape((nt // 2, 1, width), f32)
        column, *sent, source_potential = call(
            functools.partial(columns_kernel, ns, cols_total, last),
            ([halves, halves] if last else [shape((nt, width), f32)]) + [tile],
            [a, e, top, t, pot] + exchange(lse, "col"),
            [
                small,
                pltpu.VMEM((SUB, rows), bf16),
                pltpu.VMEM((rows, LANES), f32),
                pltpu.VMEM((rows, width), f32),
            ],
            16 * rows * cols,
        )
    one = shape((1, width), f32)
    parts = call(split_kernel, [one] * (nt // 2), [column, swap(sent[0], "row", 1)])
    parts = [parts[0]] + [swap(x, "row", 2 * k) for k, x in enumerate(parts) if k > 0]
    update, = call(functools.partial(update_kernel, rows_total), [one], parts)
    return moment, source_potential.reshape(rows), update.reshape(width)


def solution(mesh):
    placed = (P(("row", "col"), None), P(("col", "row"), None), P(("col", "row")), P())
    return jax.shard_map(
        per_device,
        mesh=mesh,
        in_specs=placed,
        out_specs=(P(), P("row"), P(("col", "row"))),
        check_vma=False,
    )
```

```python
import functools
import math

import jax
import jax.numpy as jnp
from jax import lax
from jax.experimental import pallas as pl
from jax.experimental.pallas import tpu as pltpu
from jax.sharding import PartitionSpec as P

ITERS = 2
LANES = 128
SUB = 16
SMALLEST = 1e-16
LARGEST = 1e12
NT_DIMS = (((1,), (1,)), ((), ()))
TN_DIMS = (((0,), (0,)), ((), ()))


def split3(x):
    high = x.astype(jnp.bfloat16)
    rest = x - high.astype(jnp.float32)
    mid = rest.astype(jnp.bfloat16)
    low = (rest - mid.astype(jnp.float32)).astype(jnp.bfloat16)
    return high, mid, low


def project4(rows, matrix_parts):
    total = None
    for part in reversed(matrix_parts):
        term = jnp.dot(rows, part, preferred_element_type=jnp.float32)
        total = term if total is None else total + term
    return (total.astype(jnp.bfloat16).astype(jnp.float32) * 4.0).astype(jnp.bfloat16)


def lane_fold(op, x):
    parts = [x[:, i : i + LANES] for i in range(0, x.shape[1], LANES)]
    return functools.reduce(op, parts)


def as_lanes(column):
    return jnp.broadcast_to(column, (LANES, LANES)).T[0:1, :]


def as_rows(lanes):
    return jnp.broadcast_to(lanes, (LANES, LANES)).T


def tree(op, parts):
    while len(parts) > 1:
        parts = [op(parts[i], parts[i + 1]) for i in range(0, len(parts), 2)]
    return parts[0]


def log_sum(parts):
    top = functools.reduce(jnp.maximum, parts)
    return top + jnp.log(tree(jnp.add, [jnp.exp(p - top) for p in parts]))


def within(masses):
    low = jnp.min(functools.reduce(jnp.minimum, masses))
    high = jnp.max(functools.reduce(jnp.maximum, masses))
    return jnp.logical_and(low > SMALLEST, high < LARGEST)


def block_of(t_ref, g, width):
    return t_ref[g * width : (g + 1) * width, :LANES]


def row_of(i, steps):
    per = steps // lax.axis_size("col")
    return pl.ds((lax.axis_index("col") ^ (i // per)) * per + i % per, 1)


def add_shifts(a_ref, t_ref, potential, aug_ref, top_ref):
    steps = a_ref.shape[0] // LANES
    lane = lax.broadcasted_iota(jnp.int32, (LANES, LANES), 1)
    for i in range(steps):
        at = slice(i * LANES, (i + 1) * LANES)
        a = a_ref[at, :]
        s = lax.dot_general(a, t_ref[: potential.shape[1], :LANES], NT_DIMS, preferred_element_type=jnp.float32)
        top = jnp.max(lane_fold(jnp.maximum, s + potential), axis=1, keepdims=True)
        top = top.astype(jnp.bfloat16).astype(jnp.float32)
        aug_ref[at, :LANES] = a
        aug_ref[at, LANES:] = jnp.where(lane == 0, 1.0, jnp.where(lane == 1, -top, 0.0)).astype(jnp.bfloat16)
        top_ref[row_of(i, steps), :] = as_lanes(top)


def shifted_rows(aug_ref, t_ref, width, lse_ref, top_ref, mass_ref, e_ref=None, carried_ref=None):
    rows = aug_ref.shape[0]
    steps = rows // LANES
    for g in range(t_ref.shape[0] // width):
        cols = slice(g * width, (g + 1) * width)
        for h in range(0, rows, 2 * LANES):
            at = slice(h, h + 2 * LANES)
            s = lax.dot_general(aug_ref[at, :], t_ref[cols, :], NT_DIMS, preferred_element_type=jnp.float32)
            e = jnp.exp(s)
            m = lane_fold(jnp.add, e)
            mass_ref[at, :] = m if g == 0 else mass_ref[at, :] + m
            e = e.astype(jnp.bfloat16)
            if e_ref is not None:
                e_ref[at, cols] = e
            if carried_ref is not None:
                d = jnp.dot(e, block_of(t_ref, g, width), preferred_element_type=jnp.float32)
                carried_ref[at, :] = d if g == 0 else carried_ref[at, :] + d
    masses = []
    for i in range(steps):
        at = slice(i * LANES, (i + 1) * LANES)
        mass = jnp.sum(mass_ref[at, :], axis=1, keepdims=True)
        masses.append(as_lanes(mass))
        row = row_of(i, steps)
        lse_ref[row, :] = top_ref[row, :] + jnp.log(masses[i])
        if carried_ref is not None:
            carried_ref[at, :] = carried_ref[at, :] / mass
    return within(masses)


def exact_rows(a_ref, t_ref, column, scores, lse_ref, top_ref=None, e_ref=None, carried_ref=None):
    steps = a_ref.shape[0] // LANES
    width = column[0].shape[1]

    @pl.loop(0, steps)
    def _(i):
        rows = pl.ds(pl.multiple_of(i * LANES, LANES), LANES)
        top = None
        for g in range(len(column)):
            t = block_of(t_ref, g, width)
            s = column[g] + lax.dot_general(a_ref[rows, :], t, NT_DIMS, preferred_element_type=jnp.float32)
            scores[:, g * width : (g + 1) * width] = s
            m = lane_fold(jnp.maximum, s)
            top = m if top is None else jnp.maximum(top, m)
        top = jnp.max(top, axis=1, keepdims=True)
        mass, carried = None, None
        for g in range(len(column)):
            cols = slice(g * width, (g + 1) * width)
            e = jnp.exp(scores[:, cols] - top)
            m = lane_fold(jnp.add, e)
            mass = m if mass is None else mass + m
            if e_ref is not None:
                e_ref[rows, cols] = e.astype(jnp.bfloat16)
            if carried_ref is not None:
                t = block_of(t_ref, g, width)
                d = jnp.dot(e.astype(jnp.bfloat16), t, preferred_element_type=jnp.float32)
                carried = d if carried is None else carried + d
        mass = jnp.sum(mass, axis=1, keepdims=True)
        row = row_of(i, steps)
        lse_ref[row, :] = as_lanes(top + jnp.log(mass))
        if top_ref is not None:
            top_ref[row, :] = as_lanes(top)
        if carried_ref is not None:
            carried_ref[rows, :] = carried / mass


def own_kernel(own_ref, moment_ref, s_ref, a_ref, parts_ref):
    s_ref[...] = own_ref[...]
    for k, part in enumerate(split3(moment_ref[...])):
        parts_ref[k] = part
    a_ref[...] = project4(own_ref[...], split3(moment_ref[...]))


def project_kernel(ns, *refs):
    s_refs, a_own_ref, parts_ref, s_ref, a_ref = refs[:ns], *refs[ns:]
    piece = a_own_ref.shape[0]
    a_ref[:piece, :] = a_own_ref[...]
    for k in range(ns):
        at = slice(k * piece, (k + 1) * piece)
        s_ref[at, :] = s_refs[k][...]
        if k > 0:
            a_ref[at, :] = project4(s_refs[k][...], [parts_ref[i] for i in range(3)])


def potential_of(block_ref, width):
    tail = block_ref[width:, :].astype(jnp.float32)
    return jnp.concatenate([tail[j : j + 1, :] for j in range(width // LANES)], axis=1)


def shift_kernel(width, a_ref, block_ref, aug_ref, top_ref):
    add_shifts(a_ref, block_ref, potential_of(block_ref, width), aug_ref, top_ref)


def couple_kernel(nt, width, *refs):
    a_ref, aug_ref, top_ref, t_refs = refs[0], refs[1], refs[2], refs[3 : 3 + nt]
    lse_ref, carried_ref, t_ref, pot_ref, mass_ref, scores = refs[3 + nt :]
    lane = lax.broadcasted_iota(jnp.int32, (LANES, LANES), 1)
    for g in range(nt):
        t_ref[g * width : (g + 1) * width, :LANES] = t_refs[g][:width, :]
        pot_ref[g : g + 1, :] = potential_of(t_refs[g], width)
        for j in range(0, width, LANES):
            potential = as_rows(pot_ref[g : g + 1, j : j + LANES])
            added = jnp.where(lane == 0, potential, jnp.where(lane == 1, 1.0, 0.0))
            at = g * width + j
            t_ref[at : at + LANES, LANES:] = added.astype(jnp.bfloat16)
    fine = shifted_rows(aug_ref, t_ref, width, lse_ref, top_ref, mass_ref, None, carried_ref)

    @pl.when(jnp.logical_not(fine))
    def _():
        column = [pot_ref[g : g + 1, :] for g in range(nt)]
        exact_rows(a_ref, t_ref, column, scores, lse_ref, None, None, carried_ref)


def moment_kernel(ns, rows_total, *refs):
    s_ref, l_refs, carried_ref = refs[0], refs[1 : 1 + ns], refs[1 + ns]
    keep_ref, send_ref, weight_ref, total_ref = refs[2 + ns :]
    c, r = lax.axis_index("col"), lax.axis_index("row")
    per = s_ref.shape[0] // ns // LANES
    shift = log_sum([l[...] for l in l_refs])
    weight_ref[...] = jnp.exp(l_refs[0][...] - shift) * (1.0 / rows_total)
    total = None
    for k in range(ns):
        for j in range(per):
            w = as_rows(weight_ref[pl.ds((c ^ k) * per + j, 1), :])
            at = (k * per + j) * LANES
            x = carried_ref[at : at + LANES, :] * w
            s = s_ref[at : at + LANES, :]
            for part in reversed(split3(x)):
                term = lax.dot_general(s, part, TN_DIMS, preferred_element_type=jnp.float32)
                total = term if total is None else total + term
    total_ref[...] = total
    half = keep_ref.shape[0]
    keep_ref[...] = total_ref[pl.ds(pl.multiple_of((r % 2) * half, half), half), :]
    send_ref[...] = total_ref[pl.ds(pl.multiple_of((1 - r % 2) * half, half), half), :]


def add_kernel(*refs):
    refs[-1][...] = tree(jnp.add, [r[...] for r in refs[:-1]])


def log_sum_kernel(*refs):
    refs[-1][...] = log_sum([r[...] for r in refs[:-1]])


def first_rows_kernel(*refs):
    s_ref, t_ref, pot_ref, m_refs = refs[0], refs[1], refs[2], refs[3:5]
    moment_ref, a_ref, lse_ref, top_ref, e_ref, mass_ref, aug_ref, scores = refs[5:]
    r = lax.axis_index("row")
    half = m_refs[0].shape[0]
    for k in range(2):
        moment_ref[pl.ds(pl.multiple_of((k ^ (r % 2)) * half, half), half), :] = m_refs[k][...]
    a_ref[...] = project4(s_ref[...], split3(moment_ref[...]))
    add_shifts(a_ref, t_ref, pot_ref[0:1, :], aug_ref, top_ref)
    fine = shifted_rows(aug_ref, t_ref, pot_ref.shape[1], lse_ref, top_ref, mass_ref, e_ref)

    @pl.when(jnp.logical_not(fine))
    def _():
        column = [pot_ref[g : g + 1, :] for g in range(pot_ref.shape[0])]
        exact_rows(a_ref, t_ref, column, scores, lse_ref, top_ref, e_ref)


def high_low(x):
    high = x.astype(jnp.bfloat16).astype(jnp.float32)
    at = lax.broadcasted_iota(jnp.int32, (SUB, x.shape[1]), 0)
    return jnp.where(at == 0, high, jnp.where(at == 1, x - high, 0.0)).astype(jnp.bfloat16)


def rows_kernel(rows_total, *refs):
    a_ref, e_ref, top_ref, t_ref, pot_ref = refs[:5]
    l_refs, (lse_ref, column_ref, weights, scores) = refs[5:-4], refs[-4:]
    r = lax.axis_index("row")
    nt, width = pot_ref.shape
    column_ref[...] = math.log(rows_total) - log_sum([l[...] for l in l_refs])
    column = [column_ref[pl.ds(r ^ k, 1), :] for k in range(nt)]
    change = [column[k] - pot_ref[k : k + 1, :] for k in range(nt)]
    top = jnp.max(functools.reduce(jnp.maximum, change), axis=1, keepdims=True)
    for k in range(nt):
        weights[:, k * width : (k + 1) * width] = high_low(jnp.exp(change[k] - top))
    steps = a_ref.shape[0] // LANES
    masses = []
    for i in range(steps):
        e = e_ref[i * LANES : (i + 1) * LANES, :]
        sums = lax.dot_general(weights[...], e, NT_DIMS, preferred_element_type=jnp.float32)
        masses.append(sums[0:1, :] + sums[1:2, :])
        row = row_of(i, steps)
        lse_ref[row, :] = top + top_ref[row, :] + jnp.log(masses[i])

    @pl.when(jnp.logical_not(within(masses)))
    def _():
        exact_rows(a_ref, t_ref, column, scores, lse_ref)


def columns_kernel(ns, cols_total, last, *refs):
    a_ref, e_ref, top_ref, t_ref, pot_ref, l_refs = *refs[:5], refs[5 : 5 + ns]
    out_refs, (sp_ref, weight_rows, weights, spread_rows, scores) = refs[5 + ns : -5], refs[-5:]
    c, r = lax.axis_index("col"), lax.axis_index("row")
    nt, width = pot_ref.shape
    rows = a_ref.shape[0]
    per = rows // ns // LANES
    potential = math.log(cols_total) - log_sum([l[...] for l in l_refs])
    sp_ref[...] = potential
    shift = potential + top_ref[...]
    top = jnp.max(jnp.max(shift, axis=1, keepdims=True), axis=0, keepdims=True)
    weight_rows[...] = jnp.exp(shift - top)
    for k in range(ns):
        for j in range(per):
            at = (k * per + j) * LANES
            weights[:, at : at + LANES] = high_low(weight_rows[pl.ds((c ^ k) * per + j, 1), :])

    def store(g, lse):
        if last:
            out_refs[g % 2][g // 2] = lse
        else:
            out_refs[0][pl.ds(r ^ g, 1), :] = lse

    masses = []
    for g in range(nt):
        e = e_ref[:, g * width : (g + 1) * width]
        sums = jnp.dot(weights[...], e, preferred_element_type=jnp.float32)
        masses.append(sums[0:1, :] + sums[1:2, :])
        store(g, top - pot_ref[g : g + 1, :] + jnp.log(masses[g]))

    @pl.when(jnp.logical_not(within(masses)))
    def _():
        exact_columns(ns, a_ref, t_ref, sp_ref, spread_rows, scores, store)


def exact_columns(ns, a_ref, t_ref, sp_ref, spread_rows, scores, store):
    c = lax.axis_index("col")
    rows, width = scores.shape
    per = rows // ns // LANES
    for k in range(ns):
        for j in range(per):
            at = (k * per + j) * LANES
            spread_rows[at : at + LANES, :] = as_rows(sp_ref[pl.ds((c ^ k) * per + j, 1), :])
    for g in range(t_ref.shape[0] // width):
        top = None
        for at in range(0, rows, LANES):
            a = a_ref[at : at + LANES, :]
            s = lax.dot_general(a, block_of(t_ref, g, width), NT_DIMS, preferred_element_type=jnp.float32)
            s = s + jnp.concatenate([spread_rows[at : at + LANES, :]] * (width // LANES), axis=1)
            scores[at : at + LANES, :] = s
            m = jnp.max(s.reshape(LANES // 8, 8, width), axis=0)
            top = m if top is None else jnp.maximum(top, m)
        top = jnp.max(top, axis=0, keepdims=True)
        mass = None
        for at in range(0, rows, LANES):
            e = jnp.exp(scores[at : at + LANES, :] - top)
            m = jnp.sum(e.reshape(LANES // 8, 8, width), axis=0)
            mass = m if mass is None else mass + m
        store(g, top + jnp.log(jnp.sum(mass, axis=0, keepdims=True)))


def split_kernel(x_ref, y_ref, *out_refs):
    for k, out_ref in enumerate(out_refs):
        out_ref[...] = log_sum([x_ref[k], y_ref[k]])


def update_kernel(rows_total, *refs):
    refs[-1][...] = math.log(rows_total) - log_sum([l[...] for l in refs[:-1]])


def call(kernel, out, args, scratch=(), flops=0, exps=0):
    vmem = pl.BlockSpec(memory_space=pltpu.VMEM)
    bytes_accessed = sum(x.size * x.dtype.itemsize for x in list(args) + list(out))
    return pl.pallas_call(
        kernel,
        out_shape=list(out),
        in_specs=[vmem] * len(args),
        out_specs=[vmem] * len(out),
        scratch_shapes=list(scratch),
        compiler_params=pltpu.CompilerParams(vmem_limit_bytes=24 << 20),
        cost_estimate=pl.CostEstimate(flops=flops, bytes_accessed=bytes_accessed, transcendentals=exps),
    )(*args)


def swap(x, axis, k):
    return lax.ppermute(x, axis, [(i, i ^ k) for i in range(lax.axis_size(axis))])


def exchange(x, axis):
    return [x] + [swap(x, axis, k) for k in range(1, lax.axis_size(axis))]


def exchange_chips(x):
    return [x] + [swap(x, "row", k) for k in range(2, lax.axis_size("row"), 2)]


def combine(kernel, parts):
    return call(kernel, [jax.ShapeDtypeStruct(parts[0].shape, parts[0].dtype)], parts)[0]


def per_device(source, target, target_potential, prev_moment):
    f32, bf16, shape = jnp.float32, jnp.bfloat16, jax.ShapeDtypeStruct
    ns, nt = lax.axis_size("col"), lax.axis_size("row")
    piece, width = source.shape[0], target.shape[0]
    depth = source.shape[1]
    rows, cols = piece * ns, width * nt
    rows_total, cols_total = rows * nt, cols * ns
    tile = shape((rows // LANES, LANES), f32)
    projected = shape((rows, depth), bf16)
    flops, exps = 2 * rows * cols * depth, rows * cols
    row_scores = pltpu.VMEM((LANES, cols), f32)
    small = pltpu.VMEM(tile.shape, f32)
    sums = pltpu.VMEM((rows, LANES), f32)

    groups = width // LANES
    tail = jnp.pad(target_potential.reshape(groups, LANES), ((0, SUB - groups), (0, 0)))
    block = jnp.concatenate([target, tail], axis=0)
    far = exchange_chips(block)
    pieces = exchange(source, "col")
    own = shape((piece, depth), bf16)
    s_own, a_own, moment_parts = call(
        own_kernel, [own, own, shape((3, depth, depth), bf16)], [source, prev_moment], flops=6 * piece * depth * depth
    )
    s, a = call(
        functools.partial(project_kernel, ns),
        [projected, projected],
        [s_own] + pieces[1:] + [a_own, moment_parts],
        flops=6 * rows * depth * depth,
    )
    far, a = lax.optimization_barrier((far, a))
    blocks = [x for pair in zip(far, [swap(x, "row", 1) for x in far]) for x in pair]
    augmented = shape((rows, 2 * depth), bf16)
    aug, top = call(
        functools.partial(shift_kernel, width), [augmented, tile], [a, far[0]], flops=2 * rows * width * depth
    )
    lse, carried, t, pot = call(
        functools.partial(couple_kernel, nt, width),
        [tile, shape((rows, depth), f32), shape((cols, 2 * depth), bf16), shape((nt, width), f32)],
        [a, aug, top] + blocks,
        [sums, row_scores],
        2 * flops,
        exps,
    )
    half = shape((depth // 2, depth), f32)
    keep, send = call(
        functools.partial(moment_kernel, ns, rows_total),
        [half, half],
        [s] + exchange(lse, "col") + [carried],
        [small, pltpu.VMEM((depth, depth), f32)],
        6 * rows * depth * depth,
    )
    part = combine(add_kernel, [keep, swap(send, "row", 1)])
    part = combine(add_kernel, exchange(part, "col"))
    part = combine(add_kernel, exchange_chips(part))
    moment, a, lse, top, e = call(
        first_rows_kernel,
        [shape((depth, depth), f32), projected, tile, tile, shape((rows, cols), bf16)],
        [s, t, pot, part, swap(part, "row", 1)],
        [sums, pltpu.VMEM(augmented.shape, bf16), row_scores],
        flops,
        exps,
    )
    for iteration in range(ITERS):
        last = iteration == ITERS - 1
        if iteration > 0:
            both = combine(log_sum_kernel, [column, swap(column, "row", 1)])
            lse, = call(
                functools.partial(rows_kernel, rows_total),
                [tile],
                [a, e, top, t, pot] + exchange_chips(both),
                [pltpu.VMEM((nt, width), f32), pltpu.VMEM((SUB, cols), bf16), row_scores],
                16 * rows * cols,
            )
        halves = shape((nt // 2, 1, width), f32)
        column, *sent, source_potential = call(
            functools.partial(columns_kernel, ns, cols_total, last),
            ([halves, halves] if last else [shape((nt, width), f32)]) + [tile],
            [a, e, top, t, pot] + exchange(lse, "col"),
            [
                small,
                pltpu.VMEM((SUB, rows), bf16),
                pltpu.VMEM((rows, LANES), f32),
                pltpu.VMEM((rows, width), f32),
            ],
            16 * rows * cols,
        )
    one = shape((1, width), f32)
    parts = call(split_kernel, [one] * (nt // 2), [column, swap(sent[0], "row", 1)])
    parts = [parts[0]] + [swap(x, "row", 2 * k) for k, x in enumerate(parts) if k > 0]
    update, = call(functools.partial(update_kernel, rows_total), [one], parts)
    return moment, source_potential.reshape(rows), update.reshape(width)


def solution(mesh):
    placed = (P(("row", "col"), None), P(("col", "row"), None), P(("col", "row")), P())
    return jax.shard_map(
        per_device,
        mesh=mesh,
        in_specs=placed,
        out_specs=(P(), P("row"), P(("col", "row"))),
        check_vma=False,
    )
```

```python
import functools
import math

import jax
import jax.numpy as jnp
from jax import lax
from jax.experimental import pallas as pl
from jax.experimental.pallas import tpu as pltpu
from jax.sharding import PartitionSpec as P

ITERS = 2
LANES = 128
SUB = 16
SMALLEST = 1e-16
LARGEST = 1e12
NT_DIMS = (((1,), (1,)), ((), ()))
TN_DIMS = (((0,), (0,)), ((), ()))


def split3(x):
    high = x.astype(jnp.bfloat16)
    rest = x - high.astype(jnp.float32)
    mid = rest.astype(jnp.bfloat16)
    low = (rest - mid.astype(jnp.float32)).astype(jnp.bfloat16)
    return high, mid, low


def project4(rows, matrix_parts):
    total = None
    for part in reversed(matrix_parts):
        term = jnp.dot(rows, part, preferred_element_type=jnp.float32)
        total = term if total is None else total + term
    return (total.astype(jnp.bfloat16).astype(jnp.float32) * 4.0).astype(jnp.bfloat16)


def lane_fold(op, x):
    parts = [x[:, i : i + LANES] for i in range(0, x.shape[1], LANES)]
    return functools.reduce(op, parts)


def as_lanes(column):
    return jnp.broadcast_to(column, (LANES, LANES)).T[0:1, :]


def as_rows(lanes):
    return jnp.broadcast_to(lanes, (LANES, LANES)).T


def tree(op, parts):
    while len(parts) > 1:
        parts = [op(parts[i], parts[i + 1]) for i in range(0, len(parts), 2)]
    return parts[0]


def log_sum(parts):
    top = functools.reduce(jnp.maximum, parts)
    return top + jnp.log(tree(jnp.add, [jnp.exp(p - top) for p in parts]))


def within(masses):
    low = jnp.min(functools.reduce(jnp.minimum, masses))
    high = jnp.max(functools.reduce(jnp.maximum, masses))
    return jnp.logical_and(low > SMALLEST, high < LARGEST)


def block_of(t_ref, g, width):
    return t_ref[g * width : (g + 1) * width, :LANES]


def row_of(i, steps):
    per = steps // lax.axis_size("col")
    return pl.ds((lax.axis_index("col") ^ (i // per)) * per + i % per, 1)


def add_shifts(a_ref, t_ref, potential, aug_ref, top_ref):
    steps = a_ref.shape[0] // LANES
    lane = lax.broadcasted_iota(jnp.int32, (LANES, LANES), 1)
    for i in range(steps):
        at = slice(i * LANES, (i + 1) * LANES)
        a = a_ref[at, :]
        s = lax.dot_general(a, t_ref[: potential.shape[1], :LANES], NT_DIMS, preferred_element_type=jnp.float32)
        top = jnp.max(lane_fold(jnp.maximum, s + potential), axis=1, keepdims=True)
        top = top.astype(jnp.bfloat16).astype(jnp.float32)
        aug_ref[at, :LANES] = a
        aug_ref[at, LANES:] = jnp.where(lane == 0, 1.0, jnp.where(lane == 1, -top, 0.0)).astype(jnp.bfloat16)
        top_ref[row_of(i, steps), :] = as_lanes(top)


def shifted_rows(aug_ref, t_ref, width, lse_ref, top_ref, mass_ref, scores, e_ref, carried_ref=None):
    rows = aug_ref.shape[0]
    steps = rows // LANES
    blocks = t_ref.shape[0] // width
    keep = e_ref.shape[1] // width
    for g in range(blocks + 2):
        if g < blocks:
            t = t_ref[g * width : (g + 1) * width, :]
            scores[g % 2] = lax.dot_general(aug_ref[...], t, NT_DIMS, preferred_element_type=jnp.float32)
        if g > 1 and carried_ref is not None:
            e = e_ref[:, (g - 2) % keep * width : ((g - 2) % keep + 1) * width]
            d = jnp.dot(e, block_of(t_ref, g - 2, width), preferred_element_type=jnp.float32)
            carried_ref[...] = d if g == 2 else carried_ref[...] + d
        if 0 < g <= blocks:
            cols = slice((g - 1) % keep * width, ((g - 1) % keep + 1) * width)
            for h in range(0, rows, LANES):
                at = slice(h, h + LANES)
                e = jnp.exp(scores[(g - 1) % 2, at, :])
                m = lane_fold(jnp.add, e)
                mass_ref[at, :] = m if g == 1 else mass_ref[at, :] + m
                e_ref[at, cols] = e.astype(jnp.bfloat16)
    masses = []
    for i in range(steps):
        at = slice(i * LANES, (i + 1) * LANES)
        mass = jnp.sum(mass_ref[at, :], axis=1, keepdims=True)
        masses.append(as_lanes(mass))
        row = row_of(i, steps)
        lse_ref[row, :] = top_ref[row, :] + jnp.log(masses[i])
        if carried_ref is not None:
            carried_ref[at, :] = carried_ref[at, :] / mass
    return within(masses)


def exact_rows(a_ref, t_ref, column, scores, lse_ref, top_ref=None, e_ref=None, carried_ref=None):
    steps = a_ref.shape[0] // LANES
    width = column[0].shape[1]

    @pl.loop(0, steps)
    def _(i):
        rows = pl.ds(pl.multiple_of(i * LANES, LANES), LANES)
        top = None
        for g in range(len(column)):
            t = block_of(t_ref, g, width)
            s = column[g] + lax.dot_general(a_ref[rows, :], t, NT_DIMS, preferred_element_type=jnp.float32)
            scores[:, g * width : (g + 1) * width] = s
            m = lane_fold(jnp.maximum, s)
            top = m if top is None else jnp.maximum(top, m)
        top = jnp.max(top, axis=1, keepdims=True)
        mass, carried = None, None
        for g in range(len(column)):
            cols = slice(g * width, (g + 1) * width)
            e = jnp.exp(scores[:, cols] - top)
            m = lane_fold(jnp.add, e)
            mass = m if mass is None else mass + m
            if e_ref is not None:
                e_ref[rows, cols] = e.astype(jnp.bfloat16)
            if carried_ref is not None:
                t = block_of(t_ref, g, width)
                d = jnp.dot(e.astype(jnp.bfloat16), t, preferred_element_type=jnp.float32)
                carried = d if carried is None else carried + d
        mass = jnp.sum(mass, axis=1, keepdims=True)
        row = row_of(i, steps)
        lse_ref[row, :] = as_lanes(top + jnp.log(mass))
        if top_ref is not None:
            top_ref[row, :] = as_lanes(top)
        if carried_ref is not None:
            carried_ref[rows, :] = carried / mass


def own_kernel(own_ref, moment_ref, s_ref, a_ref, parts_ref):
    s_ref[...] = own_ref[...]
    for k, part in enumerate(split3(moment_ref[...])):
        parts_ref[k] = part
    a_ref[...] = project4(own_ref[...], split3(moment_ref[...]))


def project_kernel(ns, *refs):
    s_refs, a_own_ref, parts_ref, s_ref, a_ref = refs[:ns], *refs[ns:]
    piece = a_own_ref.shape[0]
    a_ref[:piece, :] = a_own_ref[...]
    for k in range(ns):
        at = slice(k * piece, (k + 1) * piece)
        s_ref[at, :] = s_refs[k][...]
        if k > 0:
            a_ref[at, :] = project4(s_refs[k][...], [parts_ref[i] for i in range(3)])


def potential_of(block_ref, width):
    tail = block_ref[width:, :].astype(jnp.float32)
    return jnp.concatenate([tail[j : j + 1, :] for j in range(width // LANES)], axis=1)


def shift_kernel(width, a_ref, block_ref, aug_ref, top_ref):
    add_shifts(a_ref, block_ref, potential_of(block_ref, width), aug_ref, top_ref)


def couple_kernel(nt, width, *refs):
    a_ref, aug_ref, top_ref, t_refs = refs[0], refs[1], refs[2], refs[3 : 3 + nt]
    lse_ref, carried_ref, t_ref, pot_ref, mass_ref, ahead, e_ref, scores = refs[3 + nt :]
    lane = lax.broadcasted_iota(jnp.int32, (LANES, LANES), 1)
    for g in range(nt):
        t_ref[g * width : (g + 1) * width, :LANES] = t_refs[g][:width, :]
        pot_ref[g : g + 1, :] = potential_of(t_refs[g], width)
        for j in range(0, width, LANES):
            potential = as_rows(pot_ref[g : g + 1, j : j + LANES])
            added = jnp.where(lane == 0, potential, jnp.where(lane == 1, 1.0, 0.0))
            at = g * width + j
            t_ref[at : at + LANES, LANES:] = added.astype(jnp.bfloat16)
    fine = shifted_rows(aug_ref, t_ref, width, lse_ref, top_ref, mass_ref, ahead, e_ref, carried_ref)

    @pl.when(jnp.logical_not(fine))
    def _():
        column = [pot_ref[g : g + 1, :] for g in range(nt)]
        exact_rows(a_ref, t_ref, column, scores, lse_ref, None, None, carried_ref)


def moment_kernel(ns, rows_total, *refs):
    s_ref, l_refs, carried_ref = refs[0], refs[1 : 1 + ns], refs[1 + ns]
    keep_ref, send_ref, weight_ref, total_ref = refs[2 + ns :]
    c, r = lax.axis_index("col"), lax.axis_index("row")
    per = s_ref.shape[0] // ns // LANES
    shift = log_sum([l[...] for l in l_refs])
    weight_ref[...] = jnp.exp(l_refs[0][...] - shift) * (1.0 / rows_total)
    total = None
    for k in range(ns):
        for j in range(per):
            w = as_rows(weight_ref[pl.ds((c ^ k) * per + j, 1), :])
            at = (k * per + j) * LANES
            x = carried_ref[at : at + LANES, :] * w
            s = s_ref[at : at + LANES, :]
            for part in reversed(split3(x)):
                term = lax.dot_general(s, part, TN_DIMS, preferred_element_type=jnp.float32)
                total = term if total is None else total + term
    total_ref[...] = total
    half = keep_ref.shape[0]
    keep_ref[...] = total_ref[pl.ds(pl.multiple_of((r % 2) * half, half), half), :]
    send_ref[...] = total_ref[pl.ds(pl.multiple_of((1 - r % 2) * half, half), half), :]


def add_kernel(*refs):
    refs[-1][...] = tree(jnp.add, [r[...] for r in refs[:-1]])


def log_sum_kernel(*refs):
    refs[-1][...] = log_sum([r[...] for r in refs[:-1]])


def first_rows_kernel(*refs):
    s_ref, t_ref, pot_ref, m_refs = refs[0], refs[1], refs[2], refs[3:5]
    moment_ref, a_ref, lse_ref, top_ref, e_ref, mass_ref, aug_ref, ahead, scores = refs[5:]
    r = lax.axis_index("row")
    half = m_refs[0].shape[0]
    for k in range(2):
        moment_ref[pl.ds(pl.multiple_of((k ^ (r % 2)) * half, half), half), :] = m_refs[k][...]
    a_ref[...] = project4(s_ref[...], split3(moment_ref[...]))
    add_shifts(a_ref, t_ref, pot_ref[0:1, :], aug_ref, top_ref)
    fine = shifted_rows(aug_ref, t_ref, pot_ref.shape[1], lse_ref, top_ref, mass_ref, ahead, e_ref)

    @pl.when(jnp.logical_not(fine))
    def _():
        column = [pot_ref[g : g + 1, :] for g in range(pot_ref.shape[0])]
        exact_rows(a_ref, t_ref, column, scores, lse_ref, top_ref, e_ref)


def high_low(x):
    high = x.astype(jnp.bfloat16).astype(jnp.float32)
    at = lax.broadcasted_iota(jnp.int32, (SUB, x.shape[1]), 0)
    return jnp.where(at == 0, high, jnp.where(at == 1, x - high, 0.0)).astype(jnp.bfloat16)


def on_vector_unit(part):
    return part % 8 in (2, 4, 6)


def rows_kernel(rows_total, *refs):
    a_ref, e_ref, top_ref, t_ref, pot_ref = refs[:5]
    l_refs, (lse_ref, column_ref, weights, scores) = refs[5:-4], refs[-4:]
    r = lax.axis_index("row")
    nt, width = pot_ref.shape
    column_ref[...] = math.log(rows_total) - log_sum([l[...] for l in l_refs])
    column = [column_ref[pl.ds(r ^ k, 1), :] for k in range(nt)]
    change = [column[k] - pot_ref[k : k + 1, :] for k in range(nt)]
    top = jnp.max(functools.reduce(jnp.maximum, change), axis=1, keepdims=True)
    for k in range(nt):
        weights[:, k * width : (k + 1) * width] = high_low(jnp.exp(change[k] - top))
    steps = a_ref.shape[0] // LANES
    masses = []
    for i in range(steps):
        at = slice(i * LANES, (i + 1) * LANES)
        if on_vector_unit(i):
            total = None
            for k in range(nt):
                e = e_ref[at, k * width : (k + 1) * width].astype(jnp.float32)
                m = lane_fold(jnp.add, e * jnp.exp(change[k] - top))
                total = m if total is None else total + m
            masses.append(as_lanes(jnp.sum(total, axis=1, keepdims=True)))
        else:
            sums = lax.dot_general(weights[...], e_ref[at, :], NT_DIMS, preferred_element_type=jnp.float32)
            masses.append(sums[0:1, :] + sums[1:2, :])
        row = row_of(i, steps)
        lse_ref[row, :] = top + top_ref[row, :] + jnp.log(masses[i])

    @pl.when(jnp.logical_not(within(masses)))
    def _():
        exact_rows(a_ref, t_ref, column, scores, lse_ref)


def columns_kernel(ns, cols_total, last, *refs):
    a_ref, e_ref, top_ref, t_ref, pot_ref, l_refs = *refs[:5], refs[5 : 5 + ns]
    out_refs, (sp_ref, weight_rows, weights, spread_rows, scores) = refs[5 + ns : -5], refs[-5:]
    c, r = lax.axis_index("col"), lax.axis_index("row")
    nt, width = pot_ref.shape
    rows = a_ref.shape[0]
    per = rows // ns // LANES
    potential = math.log(cols_total) - log_sum([l[...] for l in l_refs])
    sp_ref[...] = potential
    shift = potential + top_ref[...]
    top = jnp.max(jnp.max(shift, axis=1, keepdims=True), axis=0, keepdims=True)
    weight_rows[...] = jnp.exp(shift - top)
    for k in range(ns):
        for j in range(per):
            at = (k * per + j) * LANES
            row = weight_rows[pl.ds((c ^ k) * per + j, 1), :]
            weights[:, at : at + LANES] = high_low(row)
            spread_rows[at : at + LANES, :] = as_rows(row)

    def store(g, lse):
        if last:
            out_refs[g % 2][g // 2] = lse
        else:
            out_refs[0][pl.ds(r ^ g, 1), :] = lse

    masses = []
    for g in range(nt):
        cols = slice(g * width, (g + 1) * width)
        if on_vector_unit(g):
            total = None
            for at in range(0, rows, LANES):
                e = e_ref[at : at + LANES, cols].astype(jnp.float32)
                e = e * jnp.concatenate([spread_rows[at : at + LANES, :]] * (width // LANES), axis=1)
                m = jnp.sum(e.reshape(LANES // 8, 8, width), axis=0)
                total = m if total is None else total + m
            masses.append(jnp.sum(total, axis=0, keepdims=True))
        else:
            sums = jnp.dot(weights[...], e_ref[:, cols], preferred_element_type=jnp.float32)
            masses.append(sums[0:1, :] + sums[1:2, :])
        store(g, top - pot_ref[g : g + 1, :] + jnp.log(masses[g]))

    @pl.when(jnp.logical_not(within(masses)))
    def _():
        exact_columns(ns, a_ref, t_ref, sp_ref, spread_rows, scores, store)


def exact_columns(ns, a_ref, t_ref, sp_ref, spread_rows, scores, store):
    c = lax.axis_index("col")
    rows, width = scores.shape
    per = rows // ns // LANES
    for k in range(ns):
        for j in range(per):
            at = (k * per + j) * LANES
            spread_rows[at : at + LANES, :] = as_rows(sp_ref[pl.ds((c ^ k) * per + j, 1), :])
    for g in range(t_ref.shape[0] // width):
        top = None
        for at in range(0, rows, LANES):
            a = a_ref[at : at + LANES, :]
            s = lax.dot_general(a, block_of(t_ref, g, width), NT_DIMS, preferred_element_type=jnp.float32)
            s = s + jnp.concatenate([spread_rows[at : at + LANES, :]] * (width // LANES), axis=1)
            scores[at : at + LANES, :] = s
            m = jnp.max(s.reshape(LANES // 8, 8, width), axis=0)
            top = m if top is None else jnp.maximum(top, m)
        top = jnp.max(top, axis=0, keepdims=True)
        mass = None
        for at in range(0, rows, LANES):
            e = jnp.exp(scores[at : at + LANES, :] - top)
            m = jnp.sum(e.reshape(LANES // 8, 8, width), axis=0)
            mass = m if mass is None else mass + m
        store(g, top + jnp.log(jnp.sum(mass, axis=0, keepdims=True)))


def split_kernel(x_ref, y_ref, *out_refs):
    for k, out_ref in enumerate(out_refs):
        out_ref[...] = log_sum([x_ref[k], y_ref[k]])


def update_kernel(rows_total, *refs):
    refs[-1][...] = math.log(rows_total) - log_sum([l[...] for l in refs[:-1]])


def call(kernel, out, args, scratch=(), flops=0, exps=0):
    vmem = pl.BlockSpec(memory_space=pltpu.VMEM)
    bytes_accessed = sum(x.size * x.dtype.itemsize for x in list(args) + list(out))
    return pl.pallas_call(
        kernel,
        out_shape=list(out),
        in_specs=[vmem] * len(args),
        out_specs=[vmem] * len(out),
        scratch_shapes=list(scratch),
        compiler_params=pltpu.CompilerParams(vmem_limit_bytes=24 << 20),
        cost_estimate=pl.CostEstimate(flops=flops, bytes_accessed=bytes_accessed, transcendentals=exps),
    )(*args)


def swap(x, axis, k):
    return lax.ppermute(x, axis, [(i, i ^ k) for i in range(lax.axis_size(axis))])


def exchange(x, axis):
    return [x] + [swap(x, axis, k) for k in range(1, lax.axis_size(axis))]


def exchange_chips(x):
    return [x] + [swap(x, "row", k) for k in range(2, lax.axis_size("row"), 2)]


def combine(kernel, parts):
    return call(kernel, [jax.ShapeDtypeStruct(parts[0].shape, parts[0].dtype)], parts)[0]


def per_device(source, target, target_potential, prev_moment):
    f32, bf16, shape = jnp.float32, jnp.bfloat16, jax.ShapeDtypeStruct
    ns, nt = lax.axis_size("col"), lax.axis_size("row")
    piece, width = source.shape[0], target.shape[0]
    depth = source.shape[1]
    rows, cols = piece * ns, width * nt
    rows_total, cols_total = rows * nt, cols * ns
    tile = shape((rows // LANES, LANES), f32)
    projected = shape((rows, depth), bf16)
    flops, exps = 2 * rows * cols * depth, rows * cols
    row_scores = pltpu.VMEM((LANES, cols), f32)
    small = pltpu.VMEM(tile.shape, f32)
    sums = pltpu.VMEM((rows, LANES), f32)
    ahead = pltpu.VMEM((2, rows, width), f32)

    groups = width // LANES
    tail = jnp.pad(target_potential.reshape(groups, LANES), ((0, SUB - groups), (0, 0)))
    block = jnp.concatenate([target, tail], axis=0)
    far = exchange_chips(block)
    pieces = exchange(source, "col")
    own = shape((piece, depth), bf16)
    s_own, a_own, moment_parts = call(
        own_kernel, [own, own, shape((3, depth, depth), bf16)], [source, prev_moment], flops=6 * piece * depth * depth
    )
    s, a = call(
        functools.partial(project_kernel, ns),
        [projected, projected],
        [s_own] + pieces[1:] + [a_own, moment_parts],
        flops=6 * rows * depth * depth,
    )
    far, a = lax.optimization_barrier((far, a))
    blocks = [x for pair in zip(far, [swap(x, "row", 1) for x in far]) for x in pair]
    augmented = shape((rows, 2 * depth), bf16)
    aug, top = call(
        functools.partial(shift_kernel, width), [augmented, tile], [a, far[0]], flops=2 * rows * width * depth
    )
    lse, carried, t, pot = call(
        functools.partial(couple_kernel, nt, width),
        [tile, shape((rows, depth), f32), shape((cols, 2 * depth), bf16), shape((nt, width), f32)],
        [a, aug, top] + blocks,
        [sums, ahead, pltpu.VMEM((rows, 3 * width), bf16), row_scores],
        2 * flops,
        exps,
    )
    half = shape((depth // 2, depth), f32)
    keep, send = call(
        functools.partial(moment_kernel, ns, rows_total),
        [half, half],
        [s] + exchange(lse, "col") + [carried],
        [small, pltpu.VMEM((depth, depth), f32)],
        6 * rows * depth * depth,
    )
    part = combine(add_kernel, [keep, swap(send, "row", 1)])
    part = combine(add_kernel, exchange(part, "col"))
    part = combine(add_kernel, exchange_chips(part))
    moment, a, lse, top, e = call(
        first_rows_kernel,
        [shape((depth, depth), f32), projected, tile, tile, shape((rows, cols), bf16)],
        [s, t, pot, part, swap(part, "row", 1)],
        [sums, pltpu.VMEM(augmented.shape, bf16), ahead, row_scores],
        flops,
        exps,
    )
    for iteration in range(ITERS):
        last = iteration == ITERS - 1
        if iteration > 0:
            both = combine(log_sum_kernel, [column, swap(column, "row", 1)])
            lse, = call(
                functools.partial(rows_kernel, rows_total),
                [tile],
                [a, e, top, t, pot] + exchange_chips(both),
                [pltpu.VMEM((nt, width), f32), pltpu.VMEM((SUB, cols), bf16), row_scores],
                16 * rows * cols,
            )
        halves = shape((nt // 2, 1, width), f32)
        column, *sent, source_potential = call(
            functools.partial(columns_kernel, ns, cols_total, last),
            ([halves, halves] if last else [shape((nt, width), f32)]) + [tile],
            [a, e, top, t, pot] + exchange(lse, "col"),
            [
                small,
                pltpu.VMEM((SUB, rows), bf16),
                pltpu.VMEM((rows, LANES), f32),
                pltpu.VMEM((rows, width), f32),
            ],
            16 * rows * cols,
        )
    one = shape((1, width), f32)
    parts = call(split_kernel, [one] * (nt // 2), [column, swap(sent[0], "row", 1)])
    parts = [parts[0]] + [swap(x, "row", 2 * k) for k, x in enumerate(parts) if k > 0]
    update, = call(functools.partial(update_kernel, rows_total), [one], parts)
    return moment, source_potential.reshape(rows), update.reshape(width)


def solution(mesh):
    placed = (P(("row", "col"), None), P(("col", "row"), None), P(("col", "row")), P())
    return jax.shard_map(
        per_device,
        mesh=mesh,
        in_specs=placed,
        out_specs=(P(), P("row"), P(("col", "row"))),
        check_vma=False,
    )
```

```python
import functools
import math

import jax
import jax.numpy as jnp
from jax import lax
from jax.experimental import pallas as pl
from jax.experimental.pallas import tpu as pltpu
from jax.sharding import PartitionSpec as P

ITERS = 2
LANES = 128
SUB = 16
STAGE = 256
SMALLEST = 1e-16
LARGEST = 1e12
NT_DIMS = (((1,), (1,)), ((), ()))
TN_DIMS = (((0,), (0,)), ((), ()))


def split3(x):
    high = x.astype(jnp.bfloat16)
    rest = x - high.astype(jnp.float32)
    mid = rest.astype(jnp.bfloat16)
    low = (rest - mid.astype(jnp.float32)).astype(jnp.bfloat16)
    return high, mid, low


def project4(rows, matrix_parts):
    total = None
    for part in reversed(matrix_parts):
        term = jnp.dot(rows, part, preferred_element_type=jnp.float32)
        total = term if total is None else total + term
    return (total.astype(jnp.bfloat16).astype(jnp.float32) * 4.0).astype(jnp.bfloat16)


def lane_fold(op, x):
    parts = [x[:, i : i + LANES] for i in range(0, x.shape[1], LANES)]
    return functools.reduce(op, parts)


def as_lanes(column):
    return jnp.broadcast_to(column, (LANES, LANES)).T[0:1, :]


def as_rows(lanes):
    return jnp.broadcast_to(lanes, (LANES, LANES)).T


def tree(op, parts):
    while len(parts) > 1:
        parts = [op(parts[i], parts[i + 1]) for i in range(0, len(parts), 2)]
    return parts[0]


def log_sum(parts):
    top = functools.reduce(jnp.maximum, parts)
    return top + jnp.log(tree(jnp.add, [jnp.exp(p - top) for p in parts]))


def within(masses):
    low = jnp.min(functools.reduce(jnp.minimum, masses))
    high = jnp.max(functools.reduce(jnp.maximum, masses))
    return jnp.logical_and(low > SMALLEST, high < LARGEST)


def block_of(t_ref, g, width):
    return t_ref[g * width : (g + 1) * width, :LANES]


def row_of(i, steps):
    per = steps // lax.axis_size("col")
    return pl.ds((lax.axis_index("col") ^ (i // per)) * per + i % per, 1)


def add_shifts(a_ref, t_ref, potential, aug_ref, top_ref):
    steps = a_ref.shape[0] // LANES
    lane = lax.broadcasted_iota(jnp.int32, (LANES, LANES), 1)
    for i in range(steps):
        at = slice(i * LANES, (i + 1) * LANES)
        a = a_ref[at, :]
        s = lax.dot_general(a, t_ref[: potential.shape[1], :LANES], NT_DIMS, preferred_element_type=jnp.float32)
        top = jnp.max(lane_fold(jnp.maximum, s + potential), axis=1, keepdims=True)
        top = top.astype(jnp.bfloat16).astype(jnp.float32)
        aug_ref[at, :LANES] = a
        aug_ref[at, LANES:] = jnp.where(lane == 0, 1.0, jnp.where(lane == 1, -top, 0.0)).astype(jnp.bfloat16)
        top_ref[row_of(i, steps), :] = as_lanes(top)


def shifted_rows(aug_ref, t_ref, width, lse_ref, top_ref, mass_ref, e_ref, carried_ref=None):
    rows = aug_ref.shape[0]
    steps = rows // LANES
    stages = t_ref.shape[0] // width
    keep = e_ref.shape[1] // width
    for g in range(stages + 1):
        if g > 0 and carried_ref is not None:
            e = e_ref[:, (g - 1) % keep * width : ((g - 1) % keep + 1) * width]
            d = jnp.dot(e, block_of(t_ref, g - 1, width), preferred_element_type=jnp.float32)
            carried_ref[...] = d if g == 1 else carried_ref[...] + d
        if g < stages:
            t = t_ref[g * width : (g + 1) * width, :]
            e = jnp.exp(lax.dot_general(aug_ref[...], t, NT_DIMS, preferred_element_type=jnp.float32))
            m = lane_fold(jnp.add, e)
            mass_ref[...] = m if g == 0 else mass_ref[...] + m
            e_ref[:, g % keep * width : (g % keep + 1) * width] = e.astype(jnp.bfloat16)
    masses = []
    for i in range(steps):
        at = slice(i * LANES, (i + 1) * LANES)
        mass = jnp.sum(mass_ref[at, :], axis=1, keepdims=True)
        masses.append(as_lanes(mass))
        row = row_of(i, steps)
        lse_ref[row, :] = top_ref[row, :] + jnp.log(masses[i])
        if carried_ref is not None:
            carried_ref[at, :] = carried_ref[at, :] / mass
    return within(masses)


def exact_rows(a_ref, t_ref, column, scores, lse_ref, top_ref=None, e_ref=None, carried_ref=None):
    steps = a_ref.shape[0] // LANES
    width = column[0].shape[1]

    @pl.loop(0, steps)
    def _(i):
        rows = pl.ds(pl.multiple_of(i * LANES, LANES), LANES)
        top = None
        for g in range(len(column)):
            t = block_of(t_ref, g, width)
            s = column[g] + lax.dot_general(a_ref[rows, :], t, NT_DIMS, preferred_element_type=jnp.float32)
            scores[:, g * width : (g + 1) * width] = s
            m = lane_fold(jnp.maximum, s)
            top = m if top is None else jnp.maximum(top, m)
        top = jnp.max(top, axis=1, keepdims=True)
        mass, carried = None, None
        for g in range(len(column)):
            cols = slice(g * width, (g + 1) * width)
            e = jnp.exp(scores[:, cols] - top)
            m = lane_fold(jnp.add, e)
            mass = m if mass is None else mass + m
            if e_ref is not None:
                e_ref[rows, cols] = e.astype(jnp.bfloat16)
            if carried_ref is not None:
                t = block_of(t_ref, g, width)
                d = jnp.dot(e.astype(jnp.bfloat16), t, preferred_element_type=jnp.float32)
                carried = d if carried is None else carried + d
        mass = jnp.sum(mass, axis=1, keepdims=True)
        row = row_of(i, steps)
        lse_ref[row, :] = as_lanes(top + jnp.log(mass))
        if top_ref is not None:
            top_ref[row, :] = as_lanes(top)
        if carried_ref is not None:
            carried_ref[rows, :] = carried / mass


def own_kernel(own_ref, moment_ref, s_ref, a_ref, parts_ref):
    s_ref[...] = own_ref[...]
    for k, part in enumerate(split3(moment_ref[...])):
        parts_ref[k] = part
    a_ref[...] = project4(own_ref[...], split3(moment_ref[...]))


def project_kernel(ns, *refs):
    s_refs, a_own_ref, parts_ref, s_ref, a_ref = refs[:ns], *refs[ns:]
    piece = a_own_ref.shape[0]
    a_ref[:piece, :] = a_own_ref[...]
    for k in range(ns):
        at = slice(k * piece, (k + 1) * piece)
        s_ref[at, :] = s_refs[k][...]
        if k > 0:
            a_ref[at, :] = project4(s_refs[k][...], [parts_ref[i] for i in range(3)])


def potential_of(block_ref, width):
    tail = block_ref[width:, :].astype(jnp.float32)
    return jnp.concatenate([tail[j : j + 1, :] for j in range(width // LANES)], axis=1)


def shift_kernel(width, a_ref, block_ref, aug_ref, top_ref):
    add_shifts(a_ref, block_ref, potential_of(block_ref, width), aug_ref, top_ref)


def couple_kernel(nt, width, *refs):
    a_ref, aug_ref, top_ref, t_refs = refs[0], refs[1], refs[2], refs[3 : 3 + nt]
    lse_ref, carried_ref, t_ref, pot_ref, mass_ref, e_ref, scores = refs[3 + nt :]
    lane = lax.broadcasted_iota(jnp.int32, (LANES, LANES), 1)
    for g in range(nt):
        t_ref[g * width : (g + 1) * width, :LANES] = t_refs[g][:width, :]
        pot_ref[g : g + 1, :] = potential_of(t_refs[g], width)
        for j in range(0, width, LANES):
            potential = as_rows(pot_ref[g : g + 1, j : j + LANES])
            added = jnp.where(lane == 0, potential, jnp.where(lane == 1, 1.0, 0.0))
            at = g * width + j
            t_ref[at : at + LANES, LANES:] = added.astype(jnp.bfloat16)
    fine = shifted_rows(aug_ref, t_ref, STAGE, lse_ref, top_ref, mass_ref, e_ref, carried_ref)

    @pl.when(jnp.logical_not(fine))
    def _():
        column = [pot_ref[g : g + 1, :] for g in range(nt)]
        exact_rows(a_ref, t_ref, column, scores, lse_ref, None, None, carried_ref)


def moment_kernel(ns, rows_total, *refs):
    s_ref, l_refs, carried_ref = refs[0], refs[1 : 1 + ns], refs[1 + ns]
    keep_ref, send_ref, weight_ref, total_ref = refs[2 + ns :]
    c, r = lax.axis_index("col"), lax.axis_index("row")
    per = s_ref.shape[0] // ns // LANES
    shift = log_sum([l[...] for l in l_refs])
    weight_ref[...] = jnp.exp(l_refs[0][...] - shift) * (1.0 / rows_total)
    total = None
    for k in range(ns):
        for j in range(per):
            w = as_rows(weight_ref[pl.ds((c ^ k) * per + j, 1), :])
            at = (k * per + j) * LANES
            x = carried_ref[at : at + LANES, :] * w
            s = s_ref[at : at + LANES, :]
            for part in reversed(split3(x)):
                term = lax.dot_general(s, part, TN_DIMS, preferred_element_type=jnp.float32)
                total = term if total is None else total + term
    total_ref[...] = total
    half = keep_ref.shape[0]
    keep_ref[...] = total_ref[pl.ds(pl.multiple_of((r % 2) * half, half), half), :]
    send_ref[...] = total_ref[pl.ds(pl.multiple_of((1 - r % 2) * half, half), half), :]


def add_kernel(*refs):
    refs[-1][...] = tree(jnp.add, [r[...] for r in refs[:-1]])


def log_sum_kernel(*refs):
    refs[-1][...] = log_sum([r[...] for r in refs[:-1]])


def first_rows_kernel(*refs):
    s_ref, t_ref, pot_ref, m_refs = refs[0], refs[1], refs[2], refs[3:5]
    moment_ref, a_ref, lse_ref, top_ref, e_ref, mass_ref, aug_ref, scores = refs[5:]
    r = lax.axis_index("row")
    half = m_refs[0].shape[0]
    for k in range(2):
        moment_ref[pl.ds(pl.multiple_of((k ^ (r % 2)) * half, half), half), :] = m_refs[k][...]
    a_ref[...] = project4(s_ref[...], split3(moment_ref[...]))
    add_shifts(a_ref, t_ref, pot_ref[0:1, :], aug_ref, top_ref)
    fine = shifted_rows(aug_ref, t_ref, STAGE, lse_ref, top_ref, mass_ref, e_ref)

    @pl.when(jnp.logical_not(fine))
    def _():
        column = [pot_ref[g : g + 1, :] for g in range(pot_ref.shape[0])]
        exact_rows(a_ref, t_ref, column, scores, lse_ref, top_ref, e_ref)


def high_low(x):
    high = x.astype(jnp.bfloat16).astype(jnp.float32)
    at = lax.broadcasted_iota(jnp.int32, (SUB, x.shape[1]), 0)
    return jnp.where(at == 0, high, jnp.where(at == 1, x - high, 0.0)).astype(jnp.bfloat16)


def on_vector_unit(part):
    return part % 8 in (2, 4, 6)


def rows_kernel(rows_total, *refs):
    a_ref, e_ref, top_ref, t_ref, pot_ref = refs[:5]
    l_refs, (lse_ref, column_ref, weights, scores) = refs[5:-4], refs[-4:]
    r = lax.axis_index("row")
    nt, width = pot_ref.shape
    column_ref[...] = math.log(rows_total) - log_sum([l[...] for l in l_refs])
    column = [column_ref[pl.ds(r ^ k, 1), :] for k in range(nt)]
    change = [column[k] - pot_ref[k : k + 1, :] for k in range(nt)]
    weight = [jnp.exp(x) for x in change]
    for k in range(nt):
        weights[:, k * width : (k + 1) * width] = high_low(weight[k])
    steps = a_ref.shape[0] // LANES
    masses = []
    for i in range(steps):
        at = slice(i * LANES, (i + 1) * LANES)
        if on_vector_unit(i):
            total = None
            for k in range(nt):
                e = e_ref[at, k * width : (k + 1) * width].astype(jnp.float32)
                m = lane_fold(jnp.add, e * weight[k])
                total = m if total is None else total + m
            masses.append(as_lanes(jnp.sum(total, axis=1, keepdims=True)))
        else:
            sums = lax.dot_general(weights[...], e_ref[at, :], NT_DIMS, preferred_element_type=jnp.float32)
            masses.append(sums[0:1, :] + sums[1:2, :])
        row = row_of(i, steps)
        lse_ref[row, :] = top_ref[row, :] + jnp.log(masses[i])

    @pl.when(jnp.logical_not(within(masses)))
    def _():
        exact_rows(a_ref, t_ref, column, scores, lse_ref)


def columns_kernel(ns, cols_total, last, *refs):
    a_ref, e_ref, top_ref, t_ref, pot_ref, l_refs = *refs[:5], refs[5 : 5 + ns]
    out_refs, (sp_ref, weight_rows, weights, spread_rows, scores) = refs[5 + ns : -5], refs[-5:]
    c, r = lax.axis_index("col"), lax.axis_index("row")
    nt, width = pot_ref.shape
    rows = a_ref.shape[0]
    per = rows // ns // LANES
    potential = math.log(cols_total) - log_sum([l[...] for l in l_refs])
    sp_ref[...] = potential
    weight_rows[...] = jnp.exp(potential + top_ref[...])
    for k in range(ns):
        for j in range(per):
            at = (k * per + j) * LANES
            weights[:, at : at + LANES] = high_low(weight_rows[pl.ds((c ^ k) * per + j, 1), :])

    def store(g, lse):
        if last:
            out_refs[g % 2][g // 2] = lse
        else:
            out_refs[0][pl.ds(r ^ g, 1), :] = lse

    sums = jnp.dot(weights[...], e_ref[...], preferred_element_type=jnp.float32)
    mass = sums[0:1, :] + sums[1:2, :]
    for g in range(nt):
        store(g, jnp.log(mass[:, g * width : (g + 1) * width]) - pot_ref[g : g + 1, :])

    @pl.when(jnp.logical_not(within([mass])))
    def _():
        exact_columns(ns, a_ref, t_ref, sp_ref, spread_rows, scores, store)


def exact_columns(ns, a_ref, t_ref, sp_ref, spread_rows, scores, store):
    c = lax.axis_index("col")
    rows, width = scores.shape
    per = rows // ns // LANES
    for k in range(ns):
        for j in range(per):
            at = (k * per + j) * LANES
            spread_rows[at : at + LANES, :] = as_rows(sp_ref[pl.ds((c ^ k) * per + j, 1), :])
    for g in range(t_ref.shape[0] // width):
        top = None
        for at in range(0, rows, LANES):
            a = a_ref[at : at + LANES, :]
            s = lax.dot_general(a, block_of(t_ref, g, width), NT_DIMS, preferred_element_type=jnp.float32)
            s = s + jnp.concatenate([spread_rows[at : at + LANES, :]] * (width // LANES), axis=1)
            scores[at : at + LANES, :] = s
            m = jnp.max(s.reshape(LANES // 8, 8, width), axis=0)
            top = m if top is None else jnp.maximum(top, m)
        top = jnp.max(top, axis=0, keepdims=True)
        mass = None
        for at in range(0, rows, LANES):
            e = jnp.exp(scores[at : at + LANES, :] - top)
            m = jnp.sum(e.reshape(LANES // 8, 8, width), axis=0)
            mass = m if mass is None else mass + m
        store(g, top + jnp.log(jnp.sum(mass, axis=0, keepdims=True)))


def split_kernel(x_ref, y_ref, *out_refs):
    for k, out_ref in enumerate(out_refs):
        out_ref[...] = log_sum([x_ref[k], y_ref[k]])


def update_kernel(rows_total, *refs):
    refs[-1][...] = math.log(rows_total) - log_sum([l[...] for l in refs[:-1]])


def call(kernel, out, args, scratch=(), flops=0, exps=0):
    vmem = pl.BlockSpec(memory_space=pltpu.VMEM)
    bytes_accessed = sum(x.size * x.dtype.itemsize for x in list(args) + list(out))
    return pl.pallas_call(
        kernel,
        out_shape=list(out),
        in_specs=[vmem] * len(args),
        out_specs=[vmem] * len(out),
        scratch_shapes=list(scratch),
        compiler_params=pltpu.CompilerParams(vmem_limit_bytes=24 << 20),
        cost_estimate=pl.CostEstimate(flops=flops, bytes_accessed=bytes_accessed, transcendentals=exps),
    )(*args)


def swap(x, axis, k):
    return lax.ppermute(x, axis, [(i, i ^ k) for i in range(lax.axis_size(axis))])


def exchange(x, axis):
    return [x] + [swap(x, axis, k) for k in range(1, lax.axis_size(axis))]


def exchange_chips(x):
    return [x] + [swap(x, "row", k) for k in range(2, lax.axis_size("row"), 2)]


def combine(kernel, parts):
    return call(kernel, [jax.ShapeDtypeStruct(parts[0].shape, parts[0].dtype)], parts)[0]


def per_device(source, target, target_potential, prev_moment):
    f32, bf16, shape = jnp.float32, jnp.bfloat16, jax.ShapeDtypeStruct
    ns, nt = lax.axis_size("col"), lax.axis_size("row")
    piece, width = source.shape[0], target.shape[0]
    depth = source.shape[1]
    rows, cols = piece * ns, width * nt
    rows_total, cols_total = rows * nt, cols * ns
    tile = shape((rows // LANES, LANES), f32)
    projected = shape((rows, depth), bf16)
    flops, exps = 2 * rows * cols * depth, rows * cols
    row_scores = pltpu.VMEM((LANES, cols), f32)
    small = pltpu.VMEM(tile.shape, f32)
    sums = pltpu.VMEM((rows, LANES), f32)

    groups = width // LANES
    tail = jnp.pad(target_potential.reshape(groups, LANES), ((0, SUB - groups), (0, 0)))
    block = jnp.concatenate([target, tail], axis=0)
    far = exchange_chips(block)
    pieces = exchange(source, "col")
    own = shape((piece, depth), bf16)
    s_own, a_own, moment_parts = call(
        own_kernel, [own, own, shape((3, depth, depth), bf16)], [source, prev_moment], flops=6 * piece * depth * depth
    )
    s, a = call(
        functools.partial(project_kernel, ns),
        [projected, projected],
        [s_own] + pieces[1:] + [a_own, moment_parts],
        flops=6 * rows * depth * depth,
    )
    far, a = lax.optimization_barrier((far, a))
    blocks = [x for pair in zip(far, [swap(x, "row", 1) for x in far]) for x in pair]
    augmented = shape((rows, 2 * depth), bf16)
    aug, top = call(
        functools.partial(shift_kernel, width), [augmented, tile], [a, far[0]], flops=2 * rows * width * depth
    )
    lse, carried, t, pot = call(
        functools.partial(couple_kernel, nt, width),
        [tile, shape((rows, depth), f32), shape((cols, 2 * depth), bf16), shape((nt, width), f32)],
        [a, aug, top] + blocks,
        [sums, pltpu.VMEM((rows, 2 * STAGE), bf16), row_scores],
        2 * flops,
        exps,
    )
    half = shape((depth // 2, depth), f32)
    keep, send = call(
        functools.partial(moment_kernel, ns, rows_total),
        [half, half],
        [s] + exchange(lse, "col") + [carried],
        [small, pltpu.VMEM((depth, depth), f32)],
        6 * rows * depth * depth,
    )
    part = combine(add_kernel, [keep, swap(send, "row", 1)])
    part = combine(add_kernel, exchange(part, "col"))
    part = combine(add_kernel, exchange_chips(part))
    moment, a, lse, top, e = call(
        first_rows_kernel,
        [shape((depth, depth), f32), projected, tile, tile, shape((rows, cols), bf16)],
        [s, t, pot, part, swap(part, "row", 1)],
        [sums, pltpu.VMEM(augmented.shape, bf16), row_scores],
        flops,
        exps,
    )
    for iteration in range(ITERS):
        last = iteration == ITERS - 1
        if iteration > 0:
            both = combine(log_sum_kernel, [column, swap(column, "row", 1)])
            lse, = call(
                functools.partial(rows_kernel, rows_total),
                [tile],
                [a, e, top, t, pot] + exchange_chips(both),
                [pltpu.VMEM((nt, width), f32), pltpu.VMEM((SUB, cols), bf16), row_scores],
                16 * rows * cols,
            )
        halves = shape((nt // 2, 1, width), f32)
        column, *sent, source_potential = call(
            functools.partial(columns_kernel, ns, cols_total, last),
            ([halves, halves] if last else [shape((nt, width), f32)]) + [tile],
            [a, e, top, t, pot] + exchange(lse, "col"),
            [
                small,
                pltpu.VMEM((SUB, rows), bf16),
                pltpu.VMEM((rows, LANES), f32),
                pltpu.VMEM((rows, width), f32),
            ],
            16 * rows * cols,
        )
    one = shape((1, width), f32)
    parts = call(split_kernel, [one] * (nt // 2), [column, swap(sent[0], "row", 1)])
    parts = [parts[0]] + [swap(x, "row", 2 * k) for k, x in enumerate(parts) if k > 0]
    update, = call(functools.partial(update_kernel, rows_total), [one], parts)
    return moment, source_potential.reshape(rows), update.reshape(width)


def solution(mesh):
    placed = (P(("row", "col"), None), P(("col", "row"), None), P(("col", "row")), P())
    return jax.shard_map(
        per_device,
        mesh=mesh,
        in_specs=placed,
        out_specs=(P(), P("row"), P(("col", "row"))),
        check_vma=False,
    )
```

```python
import functools
import math

import jax
import jax.numpy as jnp
from jax import lax
from jax.experimental import pallas as pl
from jax.experimental.pallas import tpu as pltpu
from jax.sharding import PartitionSpec as P

ITERS = 2
LANES = 128
SUB = 16
STAGE = 256
SMALLEST = 1e-16
LARGEST = 1e12
NT_DIMS = (((1,), (1,)), ((), ()))
TN_DIMS = (((0,), (0,)), ((), ()))


def split3(x):
    high = x.astype(jnp.bfloat16)
    rest = x - high.astype(jnp.float32)
    mid = rest.astype(jnp.bfloat16)
    low = (rest - mid.astype(jnp.float32)).astype(jnp.bfloat16)
    return high, mid, low


def project4(rows, matrix_parts):
    total = None
    for part in reversed(matrix_parts):
        term = jnp.dot(rows, part, preferred_element_type=jnp.float32)
        total = term if total is None else total + term
    return (total.astype(jnp.bfloat16).astype(jnp.float32) * 4.0).astype(jnp.bfloat16)


def lane_fold(op, x):
    parts = [x[:, i : i + LANES] for i in range(0, x.shape[1], LANES)]
    return functools.reduce(op, parts)


def as_lanes(column):
    return jnp.broadcast_to(column, (LANES, LANES)).T[0:1, :]


def as_rows(lanes):
    return jnp.broadcast_to(lanes, (LANES, LANES)).T


def tree(op, parts):
    while len(parts) > 1:
        parts = [op(parts[i], parts[i + 1]) for i in range(0, len(parts), 2)]
    return parts[0]


def log_sum(parts):
    top = functools.reduce(jnp.maximum, parts)
    return top + jnp.log(tree(jnp.add, [jnp.exp(p - top) for p in parts]))


def within(masses):
    low = jnp.min(functools.reduce(jnp.minimum, masses))
    high = jnp.max(functools.reduce(jnp.maximum, masses))
    return jnp.logical_and(low > SMALLEST, high < LARGEST)


def block_of(t_ref, g, width):
    return t_ref[g * width : (g + 1) * width, :LANES]


def row_of(i, steps):
    per = steps // lax.axis_size("col")
    return pl.ds((lax.axis_index("col") ^ (i // per)) * per + i % per, 1)


def add_shifts(a_ref, t_ref, potential, aug_ref, top_ref):
    rows = a_ref.shape[0]
    steps = rows // LANES
    lane = lax.broadcasted_iota(jnp.int32, (LANES, LANES), 1)
    s = lax.dot_general(a_ref[...], t_ref[: potential.shape[1], :LANES], NT_DIMS, preferred_element_type=jnp.float32)
    aug_ref[:, :LANES] = a_ref[...]
    top = jnp.max(lane_fold(jnp.maximum, s + potential), axis=1, keepdims=True)
    for i in range(steps):
        at = slice(i * LANES, (i + 1) * LANES)
        shift = top[at, :].astype(jnp.bfloat16).astype(jnp.float32)
        aug_ref[at, LANES:] = jnp.where(lane == 0, 1.0, jnp.where(lane == 1, -shift, 0.0)).astype(jnp.bfloat16)
        top_ref[row_of(i, steps), :] = as_lanes(shift)


def shifted_rows(aug_ref, t_ref, width, lse_ref, top_ref, mass_ref, e_ref, carried_ref=None):
    rows = aug_ref.shape[0]
    steps = rows // LANES
    stages = t_ref.shape[0] // width
    keep = e_ref.shape[1] // width
    for g in range(stages + 1):
        if g > 0 and carried_ref is not None:
            e = e_ref[:, (g - 1) % keep * width : ((g - 1) % keep + 1) * width]
            d = jnp.dot(e, block_of(t_ref, g - 1, width), preferred_element_type=jnp.float32)
            carried_ref[...] = d if g == 1 else carried_ref[...] + d
        if g < stages:
            t = t_ref[g * width : (g + 1) * width, :]
            e = jnp.exp(lax.dot_general(aug_ref[...], t, NT_DIMS, preferred_element_type=jnp.float32))
            m = lane_fold(jnp.add, e)
            mass_ref[...] = m if g == 0 else mass_ref[...] + m
            e_ref[:, g % keep * width : (g % keep + 1) * width] = e.astype(jnp.bfloat16)
    masses = []
    for i in range(steps):
        at = slice(i * LANES, (i + 1) * LANES)
        mass = jnp.sum(mass_ref[at, :], axis=1, keepdims=True)
        masses.append(as_lanes(mass))
        row = row_of(i, steps)
        lse_ref[row, :] = top_ref[row, :] + jnp.log(masses[i])
        if carried_ref is not None:
            carried_ref[at, :] = carried_ref[at, :] / mass
    return within(masses)


def exact_rows(a_ref, t_ref, column, scores, lse_ref, top_ref=None, e_ref=None, carried_ref=None):
    steps = a_ref.shape[0] // LANES
    width = column[0].shape[1]

    @pl.loop(0, steps)
    def _(i):
        rows = pl.ds(pl.multiple_of(i * LANES, LANES), LANES)
        top = None
        for g in range(len(column)):
            t = block_of(t_ref, g, width)
            s = column[g] + lax.dot_general(a_ref[rows, :], t, NT_DIMS, preferred_element_type=jnp.float32)
            scores[:, g * width : (g + 1) * width] = s
            m = lane_fold(jnp.maximum, s)
            top = m if top is None else jnp.maximum(top, m)
        top = jnp.max(top, axis=1, keepdims=True)
        mass, carried = None, None
        for g in range(len(column)):
            cols = slice(g * width, (g + 1) * width)
            e = jnp.exp(scores[:, cols] - top)
            m = lane_fold(jnp.add, e)
            mass = m if mass is None else mass + m
            if e_ref is not None:
                e_ref[rows, cols] = e.astype(jnp.bfloat16)
            if carried_ref is not None:
                t = block_of(t_ref, g, width)
                d = jnp.dot(e.astype(jnp.bfloat16), t, preferred_element_type=jnp.float32)
                carried = d if carried is None else carried + d
        mass = jnp.sum(mass, axis=1, keepdims=True)
        row = row_of(i, steps)
        lse_ref[row, :] = as_lanes(top + jnp.log(mass))
        if top_ref is not None:
            top_ref[row, :] = as_lanes(top)
        if carried_ref is not None:
            carried_ref[rows, :] = carried / mass


def own_kernel(own_ref, moment_ref, s_ref, a_ref, parts_ref):
    s_ref[...] = own_ref[...]
    for k, part in enumerate(split3(moment_ref[...])):
        parts_ref[k] = part
    a_ref[...] = project4(own_ref[...], split3(moment_ref[...]))


def project_kernel(ns, *refs):
    s_refs, a_own_ref, parts_ref, s_ref, a_ref = refs[:ns], *refs[ns:]
    piece = a_own_ref.shape[0]
    a_ref[:piece, :] = a_own_ref[...]
    for k in range(ns):
        at = slice(k * piece, (k + 1) * piece)
        s_ref[at, :] = s_refs[k][...]
        if k > 0:
            a_ref[at, :] = project4(s_refs[k][...], [parts_ref[i] for i in range(3)])


def potential_of(block_ref, width):
    tail = block_ref[width:, :].astype(jnp.float32)
    return jnp.concatenate([tail[j : j + 1, :] for j in range(width // LANES)], axis=1)


def shift_kernel(width, a_ref, block_ref, aug_ref, top_ref):
    add_shifts(a_ref, block_ref, potential_of(block_ref, width), aug_ref, top_ref)


def couple_kernel(nt, width, *refs):
    a_ref, aug_ref, top_ref, t_refs = refs[0], refs[1], refs[2], refs[3 : 3 + nt]
    lse_ref, carried_ref, t_ref, pot_ref, mass_ref, e_ref, scores = refs[3 + nt :]
    lane = lax.broadcasted_iota(jnp.int32, (LANES, LANES), 1)
    for g in range(nt):
        t_ref[g * width : (g + 1) * width, :LANES] = t_refs[g][:width, :]
        pot_ref[g : g + 1, :] = potential_of(t_refs[g], width)
        for j in range(0, width, LANES):
            potential = as_rows(pot_ref[g : g + 1, j : j + LANES])
            added = jnp.where(lane == 0, potential, jnp.where(lane == 1, 1.0, 0.0))
            at = g * width + j
            t_ref[at : at + LANES, LANES:] = added.astype(jnp.bfloat16)
    fine = shifted_rows(aug_ref, t_ref, STAGE, lse_ref, top_ref, mass_ref, e_ref, carried_ref)

    @pl.when(jnp.logical_not(fine))
    def _():
        column = [pot_ref[g : g + 1, :] for g in range(nt)]
        exact_rows(a_ref, t_ref, column, scores, lse_ref, None, None, carried_ref)


def moment_kernel(ns, rows_total, *refs):
    s_ref, l_refs, carried_ref = refs[0], refs[1 : 1 + ns], refs[1 + ns]
    keep_ref, send_ref, weight_ref, total_ref = refs[2 + ns :]
    c, r = lax.axis_index("col"), lax.axis_index("row")
    per = s_ref.shape[0] // ns // LANES
    shift = log_sum([l[...] for l in l_refs])
    weight_ref[...] = jnp.exp(l_refs[0][...] - shift) * (1.0 / rows_total)
    total = None
    for k in range(ns):
        for j in range(per):
            w = as_rows(weight_ref[pl.ds((c ^ k) * per + j, 1), :])
            at = (k * per + j) * LANES
            x = carried_ref[at : at + LANES, :] * w
            s = s_ref[at : at + LANES, :]
            for part in reversed(split3(x)):
                term = lax.dot_general(s, part, TN_DIMS, preferred_element_type=jnp.float32)
                total = term if total is None else total + term
    total_ref[...] = total
    half = keep_ref.shape[0]
    keep_ref[...] = total_ref[pl.ds(pl.multiple_of((r % 2) * half, half), half), :]
    send_ref[...] = total_ref[pl.ds(pl.multiple_of((1 - r % 2) * half, half), half), :]


def add_kernel(*refs):
    refs[-1][...] = tree(jnp.add, [r[...] for r in refs[:-1]])


def log_sum_kernel(*refs):
    refs[-1][...] = log_sum([r[...] for r in refs[:-1]])


def first_rows_kernel(*refs):
    s_ref, t_ref, pot_ref, m_refs = refs[0], refs[1], refs[2], refs[3:5]
    moment_ref, a_ref, lse_ref, top_ref, e_ref, mass_ref, aug_ref, scores = refs[5:]
    r = lax.axis_index("row")
    half = m_refs[0].shape[0]
    for k in range(2):
        moment_ref[pl.ds(pl.multiple_of((k ^ (r % 2)) * half, half), half), :] = m_refs[k][...]
    a_ref[...] = project4(s_ref[...], split3(moment_ref[...]))
    add_shifts(a_ref, t_ref, pot_ref[0:1, :], aug_ref, top_ref)
    fine = shifted_rows(aug_ref, t_ref, STAGE, lse_ref, top_ref, mass_ref, e_ref)

    @pl.when(jnp.logical_not(fine))
    def _():
        column = [pot_ref[g : g + 1, :] for g in range(pot_ref.shape[0])]
        exact_rows(a_ref, t_ref, column, scores, lse_ref, top_ref, e_ref)


def high_low(x):
    high = x.astype(jnp.bfloat16).astype(jnp.float32)
    at = lax.broadcasted_iota(jnp.int32, (SUB, x.shape[1]), 0)
    return jnp.where(at == 0, high, jnp.where(at == 1, x - high, 0.0)).astype(jnp.bfloat16)


def on_vector_unit(part):
    return part % 8 in (2, 4, 6)


def rows_kernel(rows_total, *refs):
    a_ref, e_ref, top_ref, t_ref, pot_ref = refs[:5]
    l_refs, (lse_ref, column_ref, weights, scores) = refs[5:-4], refs[-4:]
    r = lax.axis_index("row")
    nt, width = pot_ref.shape
    column_ref[...] = math.log(rows_total) - log_sum([l[...] for l in l_refs])
    column = [column_ref[pl.ds(r ^ k, 1), :] for k in range(nt)]
    change = [column[k] - pot_ref[k : k + 1, :] for k in range(nt)]
    weight = [jnp.exp(x) for x in change]
    for k in range(nt):
        weights[:, k * width : (k + 1) * width] = high_low(weight[k])
    steps = a_ref.shape[0] // LANES
    masses = []
    for i in range(steps):
        at = slice(i * LANES, (i + 1) * LANES)
        if on_vector_unit(i):
            total = None
            for k in range(nt):
                e = e_ref[at, k * width : (k + 1) * width].astype(jnp.float32)
                m = lane_fold(jnp.add, e * weight[k])
                total = m if total is None else total + m
            masses.append(as_lanes(jnp.sum(total, axis=1, keepdims=True)))
        else:
            sums = lax.dot_general(weights[...], e_ref[at, :], NT_DIMS, preferred_element_type=jnp.float32)
            masses.append(sums[0:1, :] + sums[1:2, :])
        row = row_of(i, steps)
        lse_ref[row, :] = top_ref[row, :] + jnp.log(masses[i])

    @pl.when(jnp.logical_not(within(masses)))
    def _():
        exact_rows(a_ref, t_ref, column, scores, lse_ref)


def columns_kernel(ns, cols_total, last, *refs):
    a_ref, e_ref, top_ref, t_ref, pot_ref, l_refs = *refs[:5], refs[5 : 5 + ns]
    out_refs, (sp_ref, weight_rows, weights, spread_rows, scores) = refs[5 + ns : -5], refs[-5:]
    c, r = lax.axis_index("col"), lax.axis_index("row")
    nt, width = pot_ref.shape
    rows = a_ref.shape[0]
    per = rows // ns // LANES
    potential = math.log(cols_total) - log_sum([l[...] for l in l_refs])
    sp_ref[...] = potential
    weight_rows[...] = jnp.exp(potential + top_ref[...])
    for k in range(ns):
        for j in range(per):
            at = (k * per + j) * LANES
            weights[:, at : at + LANES] = high_low(weight_rows[pl.ds((c ^ k) * per + j, 1), :])

    def store(g, lse):
        if last:
            out_refs[g % 2][g // 2] = lse
        else:
            out_refs[0][pl.ds(r ^ g, 1), :] = lse

    sums = jnp.dot(weights[...], e_ref[...], preferred_element_type=jnp.float32)
    mass = sums[0:1, :] + sums[1:2, :]
    for g in range(nt):
        store(g, jnp.log(mass[:, g * width : (g + 1) * width]) - pot_ref[g : g + 1, :])

    @pl.when(jnp.logical_not(within([mass])))
    def _():
        exact_columns(ns, a_ref, t_ref, sp_ref, spread_rows, scores, store)


def exact_columns(ns, a_ref, t_ref, sp_ref, spread_rows, scores, store):
    c = lax.axis_index("col")
    rows, width = scores.shape
    per = rows // ns // LANES
    for k in range(ns):
        for j in range(per):
            at = (k * per + j) * LANES
            spread_rows[at : at + LANES, :] = as_rows(sp_ref[pl.ds((c ^ k) * per + j, 1), :])
    for g in range(t_ref.shape[0] // width):
        top = None
        for at in range(0, rows, LANES):
            a = a_ref[at : at + LANES, :]
            s = lax.dot_general(a, block_of(t_ref, g, width), NT_DIMS, preferred_element_type=jnp.float32)
            s = s + jnp.concatenate([spread_rows[at : at + LANES, :]] * (width // LANES), axis=1)
            scores[at : at + LANES, :] = s
            m = jnp.max(s.reshape(LANES // 8, 8, width), axis=0)
            top = m if top is None else jnp.maximum(top, m)
        top = jnp.max(top, axis=0, keepdims=True)
        mass = None
        for at in range(0, rows, LANES):
            e = jnp.exp(scores[at : at + LANES, :] - top)
            m = jnp.sum(e.reshape(LANES // 8, 8, width), axis=0)
            mass = m if mass is None else mass + m
        store(g, top + jnp.log(jnp.sum(mass, axis=0, keepdims=True)))


def split_kernel(x_ref, y_ref, *out_refs):
    for k, out_ref in enumerate(reversed(out_refs)):
        out_ref[...] = log_sum([x_ref[k], y_ref[k]])


def update_kernel(rows_total, *refs):
    refs[-1][...] = math.log(rows_total) - log_sum([l[...] for l in refs[:-1]])


def call(kernel, out, args, scratch=(), flops=0, exps=0):
    vmem = pl.BlockSpec(memory_space=pltpu.VMEM)
    bytes_accessed = sum(x.size * x.dtype.itemsize for x in list(args) + list(out))
    return pl.pallas_call(
        kernel,
        out_shape=list(out),
        in_specs=[vmem] * len(args),
        out_specs=[vmem] * len(out),
        scratch_shapes=list(scratch),
        compiler_params=pltpu.CompilerParams(vmem_limit_bytes=24 << 20),
        cost_estimate=pl.CostEstimate(flops=flops, bytes_accessed=bytes_accessed, transcendentals=exps),
    )(*args)


def swap(x, axis, k):
    return lax.ppermute(x, axis, [(i, i ^ k) for i in range(lax.axis_size(axis))])


def exchange(x, axis):
    return [x] + [swap(x, axis, k) for k in range(1, lax.axis_size(axis))]


def exchange_chips(x):
    return [x] + [swap(x, "row", k) for k in range(2, lax.axis_size("row"), 2)]


def combine(kernel, parts):
    return call(kernel, [jax.ShapeDtypeStruct(parts[0].shape, parts[0].dtype)], parts)[0]


def per_device(source, target, target_potential, prev_moment):
    f32, bf16, shape = jnp.float32, jnp.bfloat16, jax.ShapeDtypeStruct
    ns, nt = lax.axis_size("col"), lax.axis_size("row")
    piece, width = source.shape[0], target.shape[0]
    depth = source.shape[1]
    rows, cols = piece * ns, width * nt
    rows_total, cols_total = rows * nt, cols * ns
    tile = shape((rows // LANES, LANES), f32)
    projected = shape((rows, depth), bf16)
    flops, exps = 2 * rows * cols * depth, rows * cols
    row_scores = pltpu.VMEM((LANES, cols), f32)
    small = pltpu.VMEM(tile.shape, f32)
    sums = pltpu.VMEM((rows, LANES), f32)

    groups = width // LANES
    tail = jnp.pad(target_potential.reshape(groups, LANES), ((0, SUB - groups), (0, 0)))
    block = jnp.concatenate([target, tail], axis=0)
    pieces = exchange(source, "col")
    far = exchange_chips(block)
    own = shape((piece, depth), bf16)
    s_own, a_own, moment_parts = call(
        own_kernel, [own, own, shape((3, depth, depth), bf16)], [source, prev_moment], flops=6 * piece * depth * depth
    )
    s, a = call(
        functools.partial(project_kernel, ns),
        [projected, projected],
        [s_own] + pieces[1:] + [a_own, moment_parts],
        flops=200 * rows * depth * depth,
    )
    far, a = lax.optimization_barrier((far, a))
    blocks = [x for pair in zip(far, [swap(x, "row", 1) for x in far]) for x in pair]
    augmented = shape((rows, 2 * depth), bf16)
    aug, top = call(
        functools.partial(shift_kernel, width), [augmented, tile], [a, far[0]], flops=2 * rows * width * depth
    )
    lse, carried, t, pot = call(
        functools.partial(couple_kernel, nt, width),
        [tile, shape((rows, depth), f32), shape((cols, 2 * depth), bf16), shape((nt, width), f32)],
        [a, aug, top] + blocks,
        [sums, pltpu.VMEM((rows, 2 * STAGE), bf16), row_scores],
        2 * flops,
        exps,
    )
    half = shape((depth // 2, depth), f32)
    keep, send = call(
        functools.partial(moment_kernel, ns, rows_total),
        [half, half],
        [s] + exchange(lse, "col") + [carried],
        [small, pltpu.VMEM((depth, depth), f32)],
        6 * rows * depth * depth,
    )
    part = combine(add_kernel, [keep, swap(send, "row", 1)])
    part = combine(add_kernel, exchange(part, "col"))
    part = combine(add_kernel, exchange_chips(part))
    moment, a, lse, top, e = call(
        first_rows_kernel,
        [shape((depth, depth), f32), projected, tile, tile, shape((rows, cols), bf16)],
        [s, t, pot, part, swap(part, "row", 1)],
        [sums, pltpu.VMEM(augmented.shape, bf16), row_scores],
        flops,
        exps,
    )
    for iteration in range(ITERS):
        last = iteration == ITERS - 1
        if iteration > 0:
            both = combine(log_sum_kernel, [column, swap(column, "row", 1)])
            lse, = call(
                functools.partial(rows_kernel, rows_total),
                [tile],
                [a, e, top, t, pot] + exchange_chips(both),
                [pltpu.VMEM((nt, width), f32), pltpu.VMEM((SUB, cols), bf16), row_scores],
                16 * rows * cols,
            )
        halves = shape((nt // 2, 1, width), f32)
        column, *sent, source_potential = call(
            functools.partial(columns_kernel, ns, cols_total, last),
            ([halves, halves] if last else [shape((nt, width), f32)]) + [tile],
            [a, e, top, t, pot] + exchange(lse, "col"),
            [
                small,
                pltpu.VMEM((SUB, rows), bf16),
                pltpu.VMEM((rows, LANES), f32),
                pltpu.VMEM((rows, width), f32),
            ],
            16 * rows * cols,
        )
    one = shape((1, width), f32)
    parts = call(split_kernel, [one] * (nt // 2), [column, swap(sent[0], "row", 1)])
    parts = [swap(x, "row", nt - 2 - 2 * k) for k, x in enumerate(parts[:-1])] + [parts[-1]]
    update, = call(functools.partial(update_kernel, rows_total), [one], parts)
    return moment, source_potential.reshape(rows), update.reshape(width)


def solution(mesh):
    placed = (P(("row", "col"), None), P(("col", "row"), None), P(("col", "row")), P())
    return jax.shard_map(
        per_device,
        mesh=mesh,
        in_specs=placed,
        out_specs=(P(), P("row"), P(("col", "row"))),
        check_vma=False,
    )
```

```python
import functools
import math

import jax
import jax.numpy as jnp
from jax import lax
from jax.experimental import pallas as pl
from jax.experimental.pallas import tpu as pltpu
from jax.sharding import PartitionSpec as P

ITERS = 2
LANES = 128
SUB = 16
STAGE = 256
SMALLEST = 1e-16
LARGEST = 1e12
NT_DIMS = (((1,), (1,)), ((), ()))
TN_DIMS = (((0,), (0,)), ((), ()))


def split3(x):
    high = x.astype(jnp.bfloat16)
    rest = x - high.astype(jnp.float32)
    mid = rest.astype(jnp.bfloat16)
    low = (rest - mid.astype(jnp.float32)).astype(jnp.bfloat16)
    return high, mid, low


def project4(rows, matrix_parts):
    total = None
    for part in reversed(matrix_parts):
        term = jnp.dot(rows, part, preferred_element_type=jnp.float32)
        total = term if total is None else total + term
    return (total.astype(jnp.bfloat16).astype(jnp.float32) * 4.0).astype(jnp.bfloat16)


def lane_fold(op, x):
    parts = [x[:, i : i + LANES] for i in range(0, x.shape[1], LANES)]
    return functools.reduce(op, parts)


def as_lanes(column):
    return jnp.broadcast_to(column, (LANES, LANES)).T[0:1, :]


def as_rows(lanes):
    return jnp.broadcast_to(lanes, (LANES, LANES)).T


def tree(op, parts):
    while len(parts) > 1:
        parts = [op(parts[i], parts[i + 1]) for i in range(0, len(parts), 2)]
    return parts[0]


def log_sum(parts):
    top = functools.reduce(jnp.maximum, parts)
    return top + jnp.log(tree(jnp.add, [jnp.exp(p - top) for p in parts]))


def within(masses):
    low = jnp.min(functools.reduce(jnp.minimum, masses))
    high = jnp.max(functools.reduce(jnp.maximum, masses))
    return jnp.logical_and(low > SMALLEST, high < LARGEST)


def block_of(t_ref, g, width):
    return t_ref[g * width : (g + 1) * width, :LANES]


def row_of(i, steps):
    per = steps // lax.axis_size("col")
    return pl.ds((lax.axis_index("col") ^ (i // per)) * per + i % per, 1)


def add_shifts(a_ref, t_ref, potential, aug_ref, top_ref):
    rows = a_ref.shape[0]
    steps = rows // LANES
    lane = lax.broadcasted_iota(jnp.int32, (LANES, LANES), 1)
    s = lax.dot_general(a_ref[...], t_ref[: potential.shape[1], :LANES], NT_DIMS, preferred_element_type=jnp.float32)
    aug_ref[:, :LANES] = a_ref[...]
    top = jnp.max(lane_fold(jnp.maximum, s + potential), axis=1, keepdims=True)
    for i in range(steps):
        at = slice(i * LANES, (i + 1) * LANES)
        shift = top[at, :].astype(jnp.bfloat16).astype(jnp.float32)
        aug_ref[at, LANES:] = jnp.where(lane == 0, 1.0, jnp.where(lane == 1, -shift, 0.0)).astype(jnp.bfloat16)
        top_ref[row_of(i, steps), :] = as_lanes(shift)


def shifted_rows(aug_ref, t_ref, width, lse_ref, top_ref, mass_ref, e_ref, carried_ref=None):
    rows = aug_ref.shape[0]
    steps = rows // LANES
    stages = t_ref.shape[0] // width
    keep = e_ref.shape[1] // width
    for g in range(stages + 1):
        if g > 0 and carried_ref is not None:
            e = e_ref[:, (g - 1) % keep * width : ((g - 1) % keep + 1) * width]
            d = jnp.dot(e, block_of(t_ref, g - 1, width), preferred_element_type=jnp.float32)
            carried_ref[...] = d if g == 1 else carried_ref[...] + d
        if g < stages:
            t = t_ref[g * width : (g + 1) * width, :]
            e = jnp.exp(lax.dot_general(aug_ref[...], t, NT_DIMS, preferred_element_type=jnp.float32))
            m = lane_fold(jnp.add, e)
            mass_ref[...] = m if g == 0 else mass_ref[...] + m
            e_ref[:, g % keep * width : (g % keep + 1) * width] = e.astype(jnp.bfloat16)
    masses = []
    for i in range(steps):
        at = slice(i * LANES, (i + 1) * LANES)
        mass = jnp.sum(mass_ref[at, :], axis=1, keepdims=True)
        masses.append(as_lanes(mass))
        row = row_of(i, steps)
        lse_ref[row, :] = top_ref[row, :] + jnp.log(masses[i])
        if carried_ref is not None:
            carried_ref[at, :] = carried_ref[at, :] / mass
    return within(masses)


def exact_rows(a_ref, t_ref, column, scores, lse_ref, top_ref=None, e_ref=None, carried_ref=None):
    steps = a_ref.shape[0] // LANES
    width = column[0].shape[1]

    @pl.loop(0, steps)
    def _(i):
        rows = pl.ds(pl.multiple_of(i * LANES, LANES), LANES)
        top = None
        for g in range(len(column)):
            t = block_of(t_ref, g, width)
            s = column[g] + lax.dot_general(a_ref[rows, :], t, NT_DIMS, preferred_element_type=jnp.float32)
            scores[:, g * width : (g + 1) * width] = s
            m = lane_fold(jnp.maximum, s)
            top = m if top is None else jnp.maximum(top, m)
        top = jnp.max(top, axis=1, keepdims=True)
        mass, carried = None, None
        for g in range(len(column)):
            cols = slice(g * width, (g + 1) * width)
            e = jnp.exp(scores[:, cols] - top)
            m = lane_fold(jnp.add, e)
            mass = m if mass is None else mass + m
            if e_ref is not None:
                e_ref[rows, cols] = e.astype(jnp.bfloat16)
            if carried_ref is not None:
                t = block_of(t_ref, g, width)
                d = jnp.dot(e.astype(jnp.bfloat16), t, preferred_element_type=jnp.float32)
                carried = d if carried is None else carried + d
        mass = jnp.sum(mass, axis=1, keepdims=True)
        row = row_of(i, steps)
        lse_ref[row, :] = as_lanes(top + jnp.log(mass))
        if top_ref is not None:
            top_ref[row, :] = as_lanes(top)
        if carried_ref is not None:
            carried_ref[rows, :] = carried / mass


def project_kernel(ns, *refs):
    s_refs, moment_ref, s_ref, a_ref = refs[:ns], *refs[ns:]
    piece = s_refs[0].shape[0]
    parts = split3(moment_ref[...])
    for k in range(ns):
        at = slice(k * piece, (k + 1) * piece)
        s_ref[at, :] = s_refs[k][...]
        a_ref[at, :] = project4(s_refs[k][...], parts)


def potential_of(block_ref, width):
    tail = block_ref[width:, :].astype(jnp.float32)
    return jnp.concatenate([tail[j : j + 1, :] for j in range(width // LANES)], axis=1)


def shift_kernel(width, a_ref, block_ref, aug_ref, top_ref):
    add_shifts(a_ref, block_ref, potential_of(block_ref, width), aug_ref, top_ref)


def couple_kernel(nt, width, *refs):
    a_ref, aug_ref, top_ref, t_refs = refs[0], refs[1], refs[2], refs[3 : 3 + nt]
    lse_ref, carried_ref, t_ref, pot_ref, mass_ref, e_ref, scores = refs[3 + nt :]
    lane = lax.broadcasted_iota(jnp.int32, (LANES, LANES), 1)
    for g in range(nt):
        t_ref[g * width : (g + 1) * width, :LANES] = t_refs[g][:width, :]
        pot_ref[g : g + 1, :] = potential_of(t_refs[g], width)
        for j in range(0, width, LANES):
            potential = as_rows(pot_ref[g : g + 1, j : j + LANES])
            added = jnp.where(lane == 0, potential, jnp.where(lane == 1, 1.0, 0.0))
            at = g * width + j
            t_ref[at : at + LANES, LANES:] = added.astype(jnp.bfloat16)
    fine = shifted_rows(aug_ref, t_ref, STAGE, lse_ref, top_ref, mass_ref, e_ref, carried_ref)

    @pl.when(jnp.logical_not(fine))
    def _():
        column = [pot_ref[g : g + 1, :] for g in range(nt)]
        exact_rows(a_ref, t_ref, column, scores, lse_ref, None, None, carried_ref)


def moment_kernel(ns, rows_total, *refs):
    s_ref, l_refs, carried_ref = refs[0], refs[1 : 1 + ns], refs[1 + ns]
    keep_ref, send_ref, weight_ref, total_ref = refs[2 + ns :]
    c, r = lax.axis_index("col"), lax.axis_index("row")
    per = s_ref.shape[0] // ns // LANES
    shift = log_sum([l[...] for l in l_refs])
    weight_ref[...] = jnp.exp(l_refs[0][...] - shift) * (1.0 / rows_total)
    total = None
    for k in range(ns):
        for j in range(per):
            w = as_rows(weight_ref[pl.ds((c ^ k) * per + j, 1), :])
            at = (k * per + j) * LANES
            x = carried_ref[at : at + LANES, :] * w
            s = s_ref[at : at + LANES, :]
            for part in reversed(split3(x)):
                term = lax.dot_general(s, part, TN_DIMS, preferred_element_type=jnp.float32)
                total = term if total is None else total + term
    total_ref[...] = total
    half = keep_ref.shape[0]
    keep_ref[...] = total_ref[pl.ds(pl.multiple_of((r % 2) * half, half), half), :]
    send_ref[...] = total_ref[pl.ds(pl.multiple_of((1 - r % 2) * half, half), half), :]


def add_kernel(*refs):
    refs[-1][...] = tree(jnp.add, [r[...] for r in refs[:-1]])


def log_sum_kernel(*refs):
    refs[-1][...] = log_sum([r[...] for r in refs[:-1]])


def first_rows_kernel(*refs):
    s_ref, t_ref, pot_ref, m_refs = refs[0], refs[1], refs[2], refs[3:5]
    moment_ref, a_ref, lse_ref, top_ref, e_ref, mass_ref, aug_ref, scores = refs[5:]
    r = lax.axis_index("row")
    half = m_refs[0].shape[0]
    for k in range(2):
        moment_ref[pl.ds(pl.multiple_of((k ^ (r % 2)) * half, half), half), :] = m_refs[k][...]
    a_ref[...] = project4(s_ref[...], split3(moment_ref[...]))
    add_shifts(a_ref, t_ref, pot_ref[0:1, :], aug_ref, top_ref)
    fine = shifted_rows(aug_ref, t_ref, STAGE, lse_ref, top_ref, mass_ref, e_ref)

    @pl.when(jnp.logical_not(fine))
    def _():
        column = [pot_ref[g : g + 1, :] for g in range(pot_ref.shape[0])]
        exact_rows(a_ref, t_ref, column, scores, lse_ref, top_ref, e_ref)


def high_low(x):
    high = x.astype(jnp.bfloat16).astype(jnp.float32)
    at = lax.broadcasted_iota(jnp.int32, (SUB, x.shape[1]), 0)
    return jnp.where(at == 0, high, jnp.where(at == 1, x - high, 0.0)).astype(jnp.bfloat16)


def on_vector_unit(part):
    return part % 8 in (2, 4, 6)


def rows_kernel(rows_total, *refs):
    a_ref, e_ref, top_ref, t_ref, pot_ref = refs[:5]
    l_refs, (lse_ref, column_ref, weights, scores) = refs[5:-4], refs[-4:]
    r = lax.axis_index("row")
    nt, width = pot_ref.shape
    column_ref[...] = math.log(rows_total) - log_sum([l[...] for l in l_refs])
    column = [column_ref[pl.ds(r ^ k, 1), :] for k in range(nt)]
    change = [column[k] - pot_ref[k : k + 1, :] for k in range(nt)]
    weight = [jnp.exp(x) for x in change]
    for k in range(nt):
        weights[:, k * width : (k + 1) * width] = high_low(weight[k])
    steps = a_ref.shape[0] // LANES
    masses = []
    for i in range(steps):
        at = slice(i * LANES, (i + 1) * LANES)
        if on_vector_unit(i):
            total = None
            for k in range(nt):
                e = e_ref[at, k * width : (k + 1) * width].astype(jnp.float32)
                m = lane_fold(jnp.add, e * weight[k])
                total = m if total is None else total + m
            masses.append(as_lanes(jnp.sum(total, axis=1, keepdims=True)))
        else:
            sums = lax.dot_general(weights[...], e_ref[at, :], NT_DIMS, preferred_element_type=jnp.float32)
            masses.append(sums[0:1, :] + sums[1:2, :])
        row = row_of(i, steps)
        lse_ref[row, :] = top_ref[row, :] + jnp.log(masses[i])

    @pl.when(jnp.logical_not(within(masses)))
    def _():
        exact_rows(a_ref, t_ref, column, scores, lse_ref)


def columns_kernel(ns, cols_total, last, *refs):
    a_ref, e_ref, top_ref, t_ref, pot_ref, l_refs = *refs[:5], refs[5 : 5 + ns]
    out_refs, (sp_ref, weight_rows, weights, spread_rows, scores) = refs[5 + ns : -5], refs[-5:]
    c, r = lax.axis_index("col"), lax.axis_index("row")
    nt, width = pot_ref.shape
    rows = a_ref.shape[0]
    per = rows // ns // LANES
    potential = math.log(cols_total) - log_sum([l[...] for l in l_refs])
    sp_ref[...] = potential
    weight_rows[...] = jnp.exp(potential + top_ref[...])
    for k in range(ns):
        for j in range(per):
            at = (k * per + j) * LANES
            weights[:, at : at + LANES] = high_low(weight_rows[pl.ds((c ^ k) * per + j, 1), :])

    def store(g, lse):
        if last:
            out_refs[g % 2][g // 2] = lse
        else:
            out_refs[0][pl.ds(r ^ g, 1), :] = lse

    sums = jnp.dot(weights[...], e_ref[...], preferred_element_type=jnp.float32)
    mass = sums[0:1, :] + sums[1:2, :]
    for g in range(nt):
        store(g, jnp.log(mass[:, g * width : (g + 1) * width]) - pot_ref[g : g + 1, :])

    @pl.when(jnp.logical_not(within([mass])))
    def _():
        exact_columns(ns, a_ref, t_ref, sp_ref, spread_rows, scores, store)


def exact_columns(ns, a_ref, t_ref, sp_ref, spread_rows, scores, store):
    c = lax.axis_index("col")
    rows, width = scores.shape
    per = rows // ns // LANES
    for k in range(ns):
        for j in range(per):
            at = (k * per + j) * LANES
            spread_rows[at : at + LANES, :] = as_rows(sp_ref[pl.ds((c ^ k) * per + j, 1), :])
    for g in range(t_ref.shape[0] // width):
        top = None
        for at in range(0, rows, LANES):
            a = a_ref[at : at + LANES, :]
            s = lax.dot_general(a, block_of(t_ref, g, width), NT_DIMS, preferred_element_type=jnp.float32)
            s = s + jnp.concatenate([spread_rows[at : at + LANES, :]] * (width // LANES), axis=1)
            scores[at : at + LANES, :] = s
            m = jnp.max(s.reshape(LANES // 8, 8, width), axis=0)
            top = m if top is None else jnp.maximum(top, m)
        top = jnp.max(top, axis=0, keepdims=True)
        mass = None
        for at in range(0, rows, LANES):
            e = jnp.exp(scores[at : at + LANES, :] - top)
            m = jnp.sum(e.reshape(LANES // 8, 8, width), axis=0)
            mass = m if mass is None else mass + m
        store(g, top + jnp.log(jnp.sum(mass, axis=0, keepdims=True)))


def split_kernel(x_ref, y_ref, *out_refs):
    for k, out_ref in enumerate(reversed(out_refs)):
        out_ref[...] = log_sum([x_ref[k], y_ref[k]])


def update_kernel(rows_total, *refs):
    refs[-1][...] = math.log(rows_total) - log_sum([l[...] for l in refs[:-1]])


def call(kernel, out, args, scratch=(), flops=0, exps=0):
    vmem = pl.BlockSpec(memory_space=pltpu.VMEM)
    bytes_accessed = sum(x.size * x.dtype.itemsize for x in list(args) + list(out))
    return pl.pallas_call(
        kernel,
        out_shape=list(out),
        in_specs=[vmem] * len(args),
        out_specs=[vmem] * len(out),
        scratch_shapes=list(scratch),
        compiler_params=pltpu.CompilerParams(vmem_limit_bytes=24 << 20),
        cost_estimate=pl.CostEstimate(flops=flops, bytes_accessed=bytes_accessed, transcendentals=exps),
    )(*args)


def swap(x, axis, k):
    return lax.ppermute(x, axis, [(i, i ^ k) for i in range(lax.axis_size(axis))])


def exchange(x, axis):
    return [x] + [swap(x, axis, k) for k in range(1, lax.axis_size(axis))]


def exchange_chips(x):
    return [x] + [swap(x, "row", k) for k in range(2, lax.axis_size("row"), 2)]


def combine(kernel, parts):
    return call(kernel, [jax.ShapeDtypeStruct(parts[0].shape, parts[0].dtype)], parts)[0]


def per_device(source, target, target_potential, prev_moment):
    f32, bf16, shape = jnp.float32, jnp.bfloat16, jax.ShapeDtypeStruct
    ns, nt = lax.axis_size("col"), lax.axis_size("row")
    piece, width = source.shape[0], target.shape[0]
    depth = source.shape[1]
    rows, cols = piece * ns, width * nt
    rows_total, cols_total = rows * nt, cols * ns
    tile = shape((rows // LANES, LANES), f32)
    projected = shape((rows, depth), bf16)
    flops, exps = 2 * rows * cols * depth, rows * cols
    row_scores = pltpu.VMEM((LANES, cols), f32)
    small = pltpu.VMEM(tile.shape, f32)
    sums = pltpu.VMEM((rows, LANES), f32)

    groups = width // LANES
    tail = jnp.pad(target_potential.reshape(groups, LANES), ((0, SUB - groups), (0, 0)))
    block = jnp.concatenate([target, tail], axis=0)
    pieces = exchange(source, "col")
    far = exchange_chips(block)
    s, a = call(
        functools.partial(project_kernel, ns),
        [projected, projected],
        pieces + [prev_moment],
        flops=200 * rows * depth * depth,
    )
    far = [lax.optimization_barrier((x, a))[0] for x in far]
    blocks = [x for pair in zip(far, [swap(x, "row", 1) for x in far]) for x in pair]
    augmented = shape((rows, 2 * depth), bf16)
    aug, top = call(
        functools.partial(shift_kernel, width), [augmented, tile], [a, far[0]], flops=2 * rows * width * depth
    )
    lse, carried, t, pot = call(
        functools.partial(couple_kernel, nt, width),
        [tile, shape((rows, depth), f32), shape((cols, 2 * depth), bf16), shape((nt, width), f32)],
        [a, aug, top] + blocks,
        [sums, pltpu.VMEM((rows, 2 * STAGE), bf16), row_scores],
        2 * flops,
        exps,
    )
    half = shape((depth // 2, depth), f32)
    keep, send = call(
        functools.partial(moment_kernel, ns, rows_total),
        [half, half],
        [s] + exchange(lse, "col") + [carried],
        [small, pltpu.VMEM((depth, depth), f32)],
        6 * rows * depth * depth,
    )
    part = combine(add_kernel, [keep, swap(send, "row", 1)])
    part = combine(add_kernel, exchange(part, "col"))
    part = combine(add_kernel, exchange_chips(part))
    moment, a, lse, top, e = call(
        first_rows_kernel,
        [shape((depth, depth), f32), projected, tile, tile, shape((rows, cols), bf16)],
        [s, t, pot, part, swap(part, "row", 1)],
        [sums, pltpu.VMEM(augmented.shape, bf16), row_scores],
        flops,
        exps,
    )
    for iteration in range(ITERS):
        last = iteration == ITERS - 1
        if iteration > 0:
            both = combine(log_sum_kernel, [column, swap(column, "row", 1)])
            lse, = call(
                functools.partial(rows_kernel, rows_total),
                [tile],
                [a, e, top, t, pot] + exchange_chips(both),
                [pltpu.VMEM((nt, width), f32), pltpu.VMEM((SUB, cols), bf16), row_scores],
                16 * rows * cols,
            )
        halves = shape((nt // 2, 1, width), f32)
        column, *sent, source_potential = call(
            functools.partial(columns_kernel, ns, cols_total, last),
            ([halves, halves] if last else [shape((nt, width), f32)]) + [tile],
            [a, e, top, t, pot] + exchange(lse, "col"),
            [
                small,
                pltpu.VMEM((SUB, rows), bf16),
                pltpu.VMEM((rows, LANES), f32),
                pltpu.VMEM((rows, width), f32),
            ],
            16 * rows * cols,
        )
    one = shape((1, width), f32)
    parts = call(split_kernel, [one] * (nt // 2), [column, swap(sent[0], "row", 1)])
    parts = [swap(x, "row", nt - 2 - 2 * k) for k, x in enumerate(parts[:-1])] + [parts[-1]]
    update, = call(functools.partial(update_kernel, rows_total), [one], parts)
    return moment, source_potential.reshape(rows), update.reshape(width)


def solution(mesh):
    placed = (P(("row", "col"), None), P(("col", "row"), None), P(("col", "row")), P())
    return jax.shard_map(
        per_device,
        mesh=mesh,
        in_specs=placed,
        out_specs=(P(), P("row"), P(("col", "row"))),
        check_vma=False,
    )
```

```python
import functools
import math

import jax
import jax.numpy as jnp
from jax import lax
from jax.experimental import pallas as pl
from jax.experimental.pallas import tpu as pltpu
from jax.sharding import PartitionSpec as P

ITERS = 2
LANES = 128
SUB = 16
STAGE = 256
SMALLEST = 1e-16
LARGEST = 1e12
NT_DIMS = (((1,), (1,)), ((), ()))
TN_DIMS = (((0,), (0,)), ((), ()))


def split3(x):
    high = x.astype(jnp.bfloat16)
    rest = x - high.astype(jnp.float32)
    mid = rest.astype(jnp.bfloat16)
    low = (rest - mid.astype(jnp.float32)).astype(jnp.bfloat16)
    return high, mid, low


def project4(rows, matrix_parts):
    total = None
    for part in reversed(matrix_parts):
        term = jnp.dot(rows, part, preferred_element_type=jnp.float32)
        total = term if total is None else total + term
    return (total.astype(jnp.bfloat16).astype(jnp.float32) * 4.0).astype(jnp.bfloat16)


def lane_fold(op, x):
    parts = [x[:, i : i + LANES] for i in range(0, x.shape[1], LANES)]
    return functools.reduce(op, parts)


def as_lanes(column):
    return jnp.broadcast_to(column, (LANES, LANES)).T[0:1, :]


def as_rows(lanes):
    return jnp.broadcast_to(lanes, (LANES, LANES)).T


def tree(op, parts):
    while len(parts) > 1:
        parts = [op(parts[i], parts[i + 1]) for i in range(0, len(parts), 2)]
    return parts[0]


def log_sum(parts):
    top = functools.reduce(jnp.maximum, parts)
    return top + jnp.log(tree(jnp.add, [jnp.exp(p - top) for p in parts]))


def within(masses):
    low = jnp.min(functools.reduce(jnp.minimum, masses))
    high = jnp.max(functools.reduce(jnp.maximum, masses))
    return jnp.logical_and(low > SMALLEST, high < LARGEST)


def block_of(t_ref, g, width):
    return t_ref[g * width : (g + 1) * width, :LANES]


def row_of(i, steps):
    per = steps // lax.axis_size("col")
    return pl.ds((lax.axis_index("col") ^ (i // per)) * per + i % per, 1)


def add_shifts(a_ref, t_ref, potential, aug_ref, top_ref):
    rows = a_ref.shape[0]
    steps = rows // LANES
    lane = lax.broadcasted_iota(jnp.int32, (LANES, LANES), 1)
    s = lax.dot_general(a_ref[...], t_ref[: potential.shape[1], :LANES], NT_DIMS, preferred_element_type=jnp.float32)
    aug_ref[:, :LANES] = a_ref[...]
    top = jnp.max(lane_fold(jnp.maximum, s + potential), axis=1, keepdims=True)
    for i in range(steps):
        at = slice(i * LANES, (i + 1) * LANES)
        shift = top[at, :].astype(jnp.bfloat16).astype(jnp.float32)
        aug_ref[at, LANES:] = jnp.where(lane == 0, 1.0, jnp.where(lane == 1, -shift, 0.0)).astype(jnp.bfloat16)
        top_ref[row_of(i, steps), :] = as_lanes(shift)


def shifted_rows(aug_ref, t_ref, width, lse_ref, top_ref, mass_ref, e_ref, carried_ref=None):
    rows = aug_ref.shape[0]
    steps = rows // LANES
    stages = t_ref.shape[0] // width
    keep = e_ref.shape[1] // width
    for g in range(stages + 1):
        if g > 0 and carried_ref is not None:
            e = e_ref[:, (g - 1) % keep * width : ((g - 1) % keep + 1) * width]
            d = jnp.dot(e, block_of(t_ref, g - 1, width), preferred_element_type=jnp.float32)
            carried_ref[...] = d if g == 1 else carried_ref[...] + d
        if g < stages:
            t = t_ref[g * width : (g + 1) * width, :]
            e = jnp.exp(lax.dot_general(aug_ref[...], t, NT_DIMS, preferred_element_type=jnp.float32))
            m = lane_fold(jnp.add, e)
            mass_ref[...] = m if g == 0 else mass_ref[...] + m
            e_ref[:, g % keep * width : (g % keep + 1) * width] = e.astype(jnp.bfloat16)
    masses = []
    for i in range(steps):
        at = slice(i * LANES, (i + 1) * LANES)
        mass = jnp.sum(mass_ref[at, :], axis=1, keepdims=True)
        masses.append(as_lanes(mass))
        row = row_of(i, steps)
        lse_ref[row, :] = top_ref[row, :] + jnp.log(masses[i])
        if carried_ref is not None:
            carried_ref[at, :] = carried_ref[at, :] / mass
    return within(masses)


def exact_rows(a_ref, t_ref, column, scores, lse_ref, top_ref=None, e_ref=None, carried_ref=None):
    steps = a_ref.shape[0] // LANES
    width = column[0].shape[1]

    @pl.loop(0, steps)
    def _(i):
        rows = pl.ds(pl.multiple_of(i * LANES, LANES), LANES)
        top = None
        for g in range(len(column)):
            t = block_of(t_ref, g, width)
            s = column[g] + lax.dot_general(a_ref[rows, :], t, NT_DIMS, preferred_element_type=jnp.float32)
            scores[:, g * width : (g + 1) * width] = s
            m = lane_fold(jnp.maximum, s)
            top = m if top is None else jnp.maximum(top, m)
        top = jnp.max(top, axis=1, keepdims=True)
        mass, carried = None, None
        for g in range(len(column)):
            cols = slice(g * width, (g + 1) * width)
            e = jnp.exp(scores[:, cols] - top)
            m = lane_fold(jnp.add, e)
            mass = m if mass is None else mass + m
            if e_ref is not None:
                e_ref[rows, cols] = e.astype(jnp.bfloat16)
            if carried_ref is not None:
                t = block_of(t_ref, g, width)
                d = jnp.dot(e.astype(jnp.bfloat16), t, preferred_element_type=jnp.float32)
                carried = d if carried is None else carried + d
        mass = jnp.sum(mass, axis=1, keepdims=True)
        row = row_of(i, steps)
        lse_ref[row, :] = as_lanes(top + jnp.log(mass))
        if top_ref is not None:
            top_ref[row, :] = as_lanes(top)
        if carried_ref is not None:
            carried_ref[rows, :] = carried / mass


def project_kernel(order, *refs):
    s_refs, moment_ref, s_ref, a_ref = refs[: len(order)], *refs[len(order) :]
    piece = s_refs[0].shape[0]
    parts = split3(moment_ref[...])
    for k, piece_ref in zip(order, s_refs):
        at = slice(k * piece, (k + 1) * piece)
        s_ref[at, :] = piece_ref[...]
        a_ref[at, :] = project4(piece_ref[...], parts)


def potential_of(block_ref, width):
    tail = block_ref[width:, :].astype(jnp.float32)
    return jnp.concatenate([tail[j : j + 1, :] for j in range(width // LANES)], axis=1)


def shift_kernel(width, a_ref, block_ref, aug_ref, top_ref):
    add_shifts(a_ref, block_ref, potential_of(block_ref, width), aug_ref, top_ref)


def couple_kernel(nt, width, *refs):
    a_ref, aug_ref, top_ref, t_refs = refs[0], refs[1], refs[2], refs[3 : 3 + nt]
    lse_ref, carried_ref, t_ref, pot_ref, mass_ref, e_ref, scores = refs[3 + nt :]
    lane = lax.broadcasted_iota(jnp.int32, (LANES, LANES), 1)
    for g in range(nt):
        t_ref[g * width : (g + 1) * width, :LANES] = t_refs[g][:width, :]
        pot_ref[g : g + 1, :] = potential_of(t_refs[g], width)
        for j in range(0, width, LANES):
            potential = as_rows(pot_ref[g : g + 1, j : j + LANES])
            added = jnp.where(lane == 0, potential, jnp.where(lane == 1, 1.0, 0.0))
            at = g * width + j
            t_ref[at : at + LANES, LANES:] = added.astype(jnp.bfloat16)
    fine = shifted_rows(aug_ref, t_ref, STAGE, lse_ref, top_ref, mass_ref, e_ref, carried_ref)

    @pl.when(jnp.logical_not(fine))
    def _():
        column = [pot_ref[g : g + 1, :] for g in range(nt)]
        exact_rows(a_ref, t_ref, column, scores, lse_ref, None, None, carried_ref)


def moment_kernel(ns, rows_total, *refs):
    s_ref, l_refs, carried_ref = refs[0], refs[1 : 1 + ns], refs[1 + ns]
    keep_ref, send_ref, weight_ref, total_ref = refs[2 + ns :]
    c, r = lax.axis_index("col"), lax.axis_index("row")
    per = s_ref.shape[0] // ns // LANES
    shift = log_sum([l[...] for l in l_refs])
    weight_ref[...] = jnp.exp(l_refs[0][...] - shift) * (1.0 / rows_total)
    total = None
    for k in range(ns):
        for j in range(per):
            w = as_rows(weight_ref[pl.ds((c ^ k) * per + j, 1), :])
            at = (k * per + j) * LANES
            x = carried_ref[at : at + LANES, :] * w
            s = s_ref[at : at + LANES, :]
            for part in reversed(split3(x)):
                term = lax.dot_general(s, part, TN_DIMS, preferred_element_type=jnp.float32)
                total = term if total is None else total + term
    total_ref[...] = total
    half = keep_ref.shape[0]
    keep_ref[...] = total_ref[pl.ds(pl.multiple_of((r % 2) * half, half), half), :]
    send_ref[...] = total_ref[pl.ds(pl.multiple_of((1 - r % 2) * half, half), half), :]


def add_kernel(*refs):
    refs[-1][...] = tree(jnp.add, [r[...] for r in refs[:-1]])


def log_sum_kernel(*refs):
    refs[-1][...] = log_sum([r[...] for r in refs[:-1]])


def first_rows_kernel(*refs):
    s_ref, t_ref, pot_ref, m_refs = refs[0], refs[1], refs[2], refs[3:5]
    moment_ref, a_ref, lse_ref, top_ref, e_ref, mass_ref, aug_ref, scores = refs[5:]
    r = lax.axis_index("row")
    half = m_refs[0].shape[0]
    for k in range(2):
        moment_ref[pl.ds(pl.multiple_of((k ^ (r % 2)) * half, half), half), :] = m_refs[k][...]
    a_ref[...] = project4(s_ref[...], split3(moment_ref[...]))
    add_shifts(a_ref, t_ref, pot_ref[0:1, :], aug_ref, top_ref)
    fine = shifted_rows(aug_ref, t_ref, STAGE, lse_ref, top_ref, mass_ref, e_ref)

    @pl.when(jnp.logical_not(fine))
    def _():
        column = [pot_ref[g : g + 1, :] for g in range(pot_ref.shape[0])]
        exact_rows(a_ref, t_ref, column, scores, lse_ref, top_ref, e_ref)


def high_low(x):
    high = x.astype(jnp.bfloat16).astype(jnp.float32)
    at = lax.broadcasted_iota(jnp.int32, (SUB, x.shape[1]), 0)
    return jnp.where(at == 0, high, jnp.where(at == 1, x - high, 0.0)).astype(jnp.bfloat16)


def on_vector_unit(part):
    return part % 8 in (2, 4, 6)


def rows_kernel(rows_total, *refs):
    a_ref, e_ref, top_ref, t_ref, pot_ref = refs[:5]
    l_refs, (lse_ref, column_ref, weights, scores) = refs[5:-4], refs[-4:]
    r = lax.axis_index("row")
    nt, width = pot_ref.shape
    column_ref[...] = math.log(rows_total) - log_sum([l[...] for l in l_refs])
    column = [column_ref[pl.ds(r ^ k, 1), :] for k in range(nt)]
    change = [column[k] - pot_ref[k : k + 1, :] for k in range(nt)]
    weight = [jnp.exp(x) for x in change]
    for k in range(nt):
        weights[:, k * width : (k + 1) * width] = high_low(weight[k])
    steps = a_ref.shape[0] // LANES
    masses = []
    for i in range(steps):
        at = slice(i * LANES, (i + 1) * LANES)
        if on_vector_unit(i):
            total = None
            for k in range(nt):
                e = e_ref[at, k * width : (k + 1) * width].astype(jnp.float32)
                m = lane_fold(jnp.add, e * weight[k])
                total = m if total is None else total + m
            masses.append(as_lanes(jnp.sum(total, axis=1, keepdims=True)))
        else:
            sums = lax.dot_general(weights[...], e_ref[at, :], NT_DIMS, preferred_element_type=jnp.float32)
            masses.append(sums[0:1, :] + sums[1:2, :])
        row = row_of(i, steps)
        lse_ref[row, :] = top_ref[row, :] + jnp.log(masses[i])

    @pl.when(jnp.logical_not(within(masses)))
    def _():
        exact_rows(a_ref, t_ref, column, scores, lse_ref)


def columns_kernel(ns, cols_total, last, *refs):
    a_ref, e_ref, top_ref, t_ref, pot_ref, l_refs = *refs[:5], refs[5 : 5 + ns]
    out_refs, (sp_ref, weight_rows, weights, spread_rows, scores) = refs[5 + ns : -5], refs[-5:]
    c, r = lax.axis_index("col"), lax.axis_index("row")
    nt, width = pot_ref.shape
    rows = a_ref.shape[0]
    per = rows // ns // LANES
    potential = math.log(cols_total) - log_sum([l[...] for l in l_refs])
    sp_ref[...] = potential
    weight_rows[...] = jnp.exp(potential + top_ref[...])
    for k in range(ns):
        for j in range(per):
            at = (k * per + j) * LANES
            weights[:, at : at + LANES] = high_low(weight_rows[pl.ds((c ^ k) * per + j, 1), :])

    def store(g, lse):
        if last:
            out_refs[g % 2][g // 2] = lse
        else:
            out_refs[0][pl.ds(r ^ g, 1), :] = lse

    sums = jnp.dot(weights[...], e_ref[...], preferred_element_type=jnp.float32)
    mass = sums[0:1, :] + sums[1:2, :]
    for g in range(nt):
        store(g, jnp.log(mass[:, g * width : (g + 1) * width]) - pot_ref[g : g + 1, :])

    @pl.when(jnp.logical_not(within([mass])))
    def _():
        exact_columns(ns, a_ref, t_ref, sp_ref, spread_rows, scores, store)


def exact_columns(ns, a_ref, t_ref, sp_ref, spread_rows, scores, store):
    c = lax.axis_index("col")
    rows, width = scores.shape
    per = rows // ns // LANES
    for k in range(ns):
        for j in range(per):
            at = (k * per + j) * LANES
            spread_rows[at : at + LANES, :] = as_rows(sp_ref[pl.ds((c ^ k) * per + j, 1), :])
    for g in range(t_ref.shape[0] // width):
        top = None
        for at in range(0, rows, LANES):
            a = a_ref[at : at + LANES, :]
            s = lax.dot_general(a, block_of(t_ref, g, width), NT_DIMS, preferred_element_type=jnp.float32)
            s = s + jnp.concatenate([spread_rows[at : at + LANES, :]] * (width // LANES), axis=1)
            scores[at : at + LANES, :] = s
            m = jnp.max(s.reshape(LANES // 8, 8, width), axis=0)
            top = m if top is None else jnp.maximum(top, m)
        top = jnp.max(top, axis=0, keepdims=True)
        mass = None
        for at in range(0, rows, LANES):
            e = jnp.exp(scores[at : at + LANES, :] - top)
            m = jnp.sum(e.reshape(LANES // 8, 8, width), axis=0)
            mass = m if mass is None else mass + m
        store(g, top + jnp.log(jnp.sum(mass, axis=0, keepdims=True)))


def split_kernel(x_ref, y_ref, *out_refs):
    for k, out_ref in enumerate(reversed(out_refs)):
        out_ref[...] = log_sum([x_ref[k], y_ref[k]])


def update_kernel(rows_total, *refs):
    refs[-1][...] = math.log(rows_total) - log_sum([l[...] for l in refs[:-1]])


def call(kernel, out, args, scratch=(), flops=0, exps=0):
    vmem = pl.BlockSpec(memory_space=pltpu.VMEM)
    bytes_accessed = sum(x.size * x.dtype.itemsize for x in list(args) + list(out))
    return pl.pallas_call(
        kernel,
        out_shape=list(out),
        in_specs=[vmem] * len(args),
        out_specs=[vmem] * len(out),
        scratch_shapes=list(scratch),
        compiler_params=pltpu.CompilerParams(vmem_limit_bytes=24 << 20),
        cost_estimate=pl.CostEstimate(flops=flops, bytes_accessed=bytes_accessed, transcendentals=exps),
    )(*args)


def swap(x, axis, k):
    return lax.ppermute(x, axis, [(i, i ^ k) for i in range(lax.axis_size(axis))])


def exchange(x, axis):
    return [x] + [swap(x, axis, k) for k in range(1, lax.axis_size(axis))]


def exchange_chips(x):
    return [x] + [swap(x, "row", k) for k in range(2, lax.axis_size("row"), 2)]


def combine(kernel, parts):
    return call(kernel, [jax.ShapeDtypeStruct(parts[0].shape, parts[0].dtype)], parts)[0]


def per_device(source, target, target_potential, prev_moment):
    f32, bf16, shape = jnp.float32, jnp.bfloat16, jax.ShapeDtypeStruct
    ns, nt = lax.axis_size("col"), lax.axis_size("row")
    piece, width = source.shape[0], target.shape[0]
    depth = source.shape[1]
    rows, cols = piece * ns, width * nt
    rows_total, cols_total = rows * nt, cols * ns
    tile = shape((rows // LANES, LANES), f32)
    projected = shape((rows, depth), bf16)
    flops, exps = 2 * rows * cols * depth, rows * cols
    row_scores = pltpu.VMEM((LANES, cols), f32)
    small = pltpu.VMEM(tile.shape, f32)
    sums = pltpu.VMEM((rows, LANES), f32)

    groups = width // LANES
    tail = jnp.pad(target_potential.reshape(groups, LANES), ((0, SUB - groups), (0, 0)))
    block = jnp.concatenate([target, tail], axis=0)
    pieces = exchange(source, "col")
    far = exchange_chips(block)
    order = [0, ns - 2, ns - 1] + list(range(ns - 3, 0, -1)) if ns > 2 else list(range(ns))
    s, a = call(
        functools.partial(project_kernel, order),
        [projected, projected],
        [pieces[k] for k in order] + [prev_moment],
        flops=200 * rows * depth * depth,
    )
    far = [lax.optimization_barrier((x, a))[0] for x in far]
    blocks = [x for pair in zip(far, [swap(x, "row", 1) for x in far]) for x in pair]
    augmented = shape((rows, 2 * depth), bf16)
    aug, top = call(
        functools.partial(shift_kernel, width), [augmented, tile], [a, far[0]], flops=2 * rows * width * depth
    )
    lse, carried, t, pot = call(
        functools.partial(couple_kernel, nt, width),
        [tile, shape((rows, depth), f32), shape((cols, 2 * depth), bf16), shape((nt, width), f32)],
        [a, aug, top] + blocks,
        [sums, pltpu.VMEM((rows, 2 * STAGE), bf16), row_scores],
        2 * flops,
        exps,
    )
    half = shape((depth // 2, depth), f32)
    keep, send = call(
        functools.partial(moment_kernel, ns, rows_total),
        [half, half],
        [s] + exchange(lse, "col") + [carried],
        [small, pltpu.VMEM((depth, depth), f32)],
        6 * rows * depth * depth,
    )
    part = combine(add_kernel, [keep, swap(send, "row", 1)])
    part = combine(add_kernel, exchange(part, "col"))
    part = combine(add_kernel, exchange_chips(part))
    moment, a, lse, top, e = call(
        first_rows_kernel,
        [shape((depth, depth), f32), projected, tile, tile, shape((rows, cols), bf16)],
        [s, t, pot, part, swap(part, "row", 1)],
        [sums, pltpu.VMEM(augmented.shape, bf16), row_scores],
        flops,
        exps,
    )
    for iteration in range(ITERS):
        last = iteration == ITERS - 1
        if iteration > 0:
            both = combine(log_sum_kernel, [column, swap(column, "row", 1)])
            lse, = call(
                functools.partial(rows_kernel, rows_total),
                [tile],
                [a, e, top, t, pot] + exchange_chips(both),
                [pltpu.VMEM((nt, width), f32), pltpu.VMEM((SUB, cols), bf16), row_scores],
                16 * rows * cols,
            )
        halves = shape((nt // 2, 1, width), f32)
        column, *sent, source_potential = call(
            functools.partial(columns_kernel, ns, cols_total, last),
            ([halves, halves] if last else [shape((nt, width), f32)]) + [tile],
            [a, e, top, t, pot] + exchange(lse, "col"),
            [
                small,
                pltpu.VMEM((SUB, rows), bf16),
                pltpu.VMEM((rows, LANES), f32),
                pltpu.VMEM((rows, width), f32),
            ],
            16 * rows * cols,
        )
    one = shape((1, width), f32)
    parts = call(split_kernel, [one] * (nt // 2), [column, swap(sent[0], "row", 1)])
    parts = [swap(x, "row", nt - 2 - 2 * k) for k, x in enumerate(parts[:-1])] + [parts[-1]]
    update, = call(functools.partial(update_kernel, rows_total), [one], parts)
    return moment, source_potential.reshape(rows), update.reshape(width)


def solution(mesh):
    placed = (P(("row", "col"), None), P(("col", "row"), None), P(("col", "row")), P())
    return jax.shard_map(
        per_device,
        mesh=mesh,
        in_specs=placed,
        out_specs=(P(), P("row"), P(("col", "row"))),
        check_vma=False,
    )
```

```python
import functools
import math

import jax
import jax.numpy as jnp
from jax import lax
from jax.experimental import pallas as pl
from jax.experimental.pallas import tpu as pltpu
from jax.sharding import PartitionSpec as P

ITERS = 2
LANES = 128
SUB = 16
STAGE = 256
SMALLEST = 1e-16
LARGEST = 1e12
NT_DIMS = (((1,), (1,)), ((), ()))
TN_DIMS = (((0,), (0,)), ((), ()))


def split3(x):
    high = x.astype(jnp.bfloat16)
    rest = x - high.astype(jnp.float32)
    mid = rest.astype(jnp.bfloat16)
    low = (rest - mid.astype(jnp.float32)).astype(jnp.bfloat16)
    return high, mid, low


def project4(rows, matrix_parts):
    total = None
    for part in reversed(matrix_parts):
        term = jnp.dot(rows, part, preferred_element_type=jnp.float32)
        total = term if total is None else total + term
    return (total.astype(jnp.bfloat16).astype(jnp.float32) * 4.0).astype(jnp.bfloat16)


def lane_fold(op, x):
    parts = [x[:, i : i + LANES] for i in range(0, x.shape[1], LANES)]
    return functools.reduce(op, parts)


def as_lanes(column):
    return jnp.broadcast_to(column, (LANES, LANES)).T[0:1, :]


def as_rows(lanes):
    return jnp.broadcast_to(lanes, (LANES, LANES)).T


def tree(op, parts):
    while len(parts) > 1:
        parts = [op(parts[i], parts[i + 1]) for i in range(0, len(parts), 2)]
    return parts[0]


def log_sum(parts):
    top = functools.reduce(jnp.maximum, parts)
    return top + jnp.log(tree(jnp.add, [jnp.exp(p - top) for p in parts]))


def within(masses):
    low = jnp.min(functools.reduce(jnp.minimum, masses))
    high = jnp.max(functools.reduce(jnp.maximum, masses))
    return jnp.logical_and(low > SMALLEST, high < LARGEST)


def block_of(t_ref, g, width):
    return t_ref[g * width : (g + 1) * width, :LANES]


def row_of(i, steps):
    per = steps // lax.axis_size("col")
    return pl.ds((lax.axis_index("col") ^ (i // per)) * per + i % per, 1)


def add_shifts(a_ref, t_ref, potential, aug_ref, top_ref):
    rows = a_ref.shape[0]
    steps = rows // LANES
    lane = lax.broadcasted_iota(jnp.int32, (LANES, LANES), 1)
    s = lax.dot_general(a_ref[...], t_ref[: potential.shape[1], :LANES], NT_DIMS, preferred_element_type=jnp.float32)
    aug_ref[:, :LANES] = a_ref[...]
    top = jnp.max(lane_fold(jnp.maximum, s + potential), axis=1, keepdims=True)
    for i in range(steps):
        at = slice(i * LANES, (i + 1) * LANES)
        shift = top[at, :].astype(jnp.bfloat16).astype(jnp.float32)
        aug_ref[at, LANES:] = jnp.where(lane == 0, 1.0, jnp.where(lane == 1, -shift, 0.0)).astype(jnp.bfloat16)
        top_ref[row_of(i, steps), :] = as_lanes(shift)


def shifted_rows(aug_ref, t_ref, width, lse_ref, top_ref, mass_ref, e_ref, carried_ref=None):
    rows = aug_ref.shape[0]
    steps = rows // LANES
    stages = t_ref.shape[0] // width
    keep = e_ref.shape[1] // width
    for g in range(stages + 1):
        if g > 0 and carried_ref is not None:
            e = e_ref[:, (g - 1) % keep * width : ((g - 1) % keep + 1) * width]
            d = jnp.dot(e, block_of(t_ref, g - 1, width), preferred_element_type=jnp.float32)
            carried_ref[...] = d if g == 1 else carried_ref[...] + d
        if g < stages:
            t = t_ref[g * width : (g + 1) * width, :]
            e = jnp.exp(lax.dot_general(aug_ref[...], t, NT_DIMS, preferred_element_type=jnp.float32))
            m = lane_fold(jnp.add, e)
            mass_ref[...] = m if g == 0 else mass_ref[...] + m
            e_ref[:, g % keep * width : (g % keep + 1) * width] = e.astype(jnp.bfloat16)
    masses = []
    for i in range(steps):
        at = slice(i * LANES, (i + 1) * LANES)
        mass = jnp.sum(mass_ref[at, :], axis=1, keepdims=True)
        masses.append(as_lanes(mass))
        row = row_of(i, steps)
        lse_ref[row, :] = top_ref[row, :] + jnp.log(masses[i])
        if carried_ref is not None:
            carried_ref[at, :] = carried_ref[at, :] / mass
    return within(masses)


def exact_rows(a_ref, t_ref, column, scores, lse_ref, top_ref=None, e_ref=None, carried_ref=None):
    steps = a_ref.shape[0] // LANES
    width = column[0].shape[1]

    @pl.loop(0, steps)
    def _(i):
        rows = pl.ds(pl.multiple_of(i * LANES, LANES), LANES)
        top = None
        for g in range(len(column)):
            t = block_of(t_ref, g, width)
            s = column[g] + lax.dot_general(a_ref[rows, :], t, NT_DIMS, preferred_element_type=jnp.float32)
            scores[:, g * width : (g + 1) * width] = s
            m = lane_fold(jnp.maximum, s)
            top = m if top is None else jnp.maximum(top, m)
        top = jnp.max(top, axis=1, keepdims=True)
        mass, carried = None, None
        for g in range(len(column)):
            cols = slice(g * width, (g + 1) * width)
            e = jnp.exp(scores[:, cols] - top)
            m = lane_fold(jnp.add, e)
            mass = m if mass is None else mass + m
            if e_ref is not None:
                e_ref[rows, cols] = e.astype(jnp.bfloat16)
            if carried_ref is not None:
                t = block_of(t_ref, g, width)
                d = jnp.dot(e.astype(jnp.bfloat16), t, preferred_element_type=jnp.float32)
                carried = d if carried is None else carried + d
        mass = jnp.sum(mass, axis=1, keepdims=True)
        row = row_of(i, steps)
        lse_ref[row, :] = as_lanes(top + jnp.log(mass))
        if top_ref is not None:
            top_ref[row, :] = as_lanes(top)
        if carried_ref is not None:
            carried_ref[rows, :] = carried / mass


def project_kernel(order, *refs):
    s_refs, moment_ref, s_ref, a_ref = refs[: len(order)], *refs[len(order) :]
    piece = s_refs[0].shape[0]
    parts = split3(moment_ref[...])
    for k, piece_ref in zip(order, s_refs):
        at = slice(k * piece, (k + 1) * piece)
        s_ref[at, :] = piece_ref[...]
        a_ref[at, :] = project4(piece_ref[...], parts)


def potential_of(block_ref, width):
    tail = block_ref[width:, :].astype(jnp.float32)
    return jnp.concatenate([tail[j : j + 1, :] for j in range(width // LANES)], axis=1)


def shift_kernel(width, a_ref, block_ref, aug_ref, top_ref):
    add_shifts(a_ref, block_ref, potential_of(block_ref, width), aug_ref, top_ref)


def block_at(slot):
    r = lax.axis_index("row")
    return (r - r % 2) ^ slot


def pair_kernel(own_ref, mate_ref, out_ref):
    core = lax.axis_index("row") % 2
    size = own_ref.shape[0]
    for at, ref in ((core, own_ref), (1 - core, mate_ref)):
        out_ref[pl.ds(pl.multiple_of(at * size, SUB), size), :] = ref[...]


def couple_kernel(chips, width, *refs):
    a_ref, aug_ref, top_ref, pair_ref = refs[:4]
    far_refs = refs[4 : 4 + chips]
    lse_ref, carried_ref, t_ref, pot_ref, mass_ref, e_ref, scores = refs[4 + chips :]
    core = lax.axis_index("row") % 2
    lane = lax.broadcasted_iota(jnp.int32, (LANES, LANES), 1)

    def place(ref, first, slot):
        at = pl.multiple_of(slot * width, LANES)
        t_ref[pl.ds(at, width), :LANES] = ref[first : first + width, :]
        tail = ref[first + width : first + width + SUB, :].astype(jnp.float32)
        for j in range(width // LANES):
            row = tail[j : j + 1, :]
            added = jnp.where(lane == 0, as_rows(row), jnp.where(lane == 1, 1.0, 0.0))
            t_ref[pl.ds(at + j * LANES, LANES), LANES:] = added.astype(jnp.bfloat16)
        rows = [tail[j : j + 1, :] for j in range(width // LANES)]
        pot_ref[pl.ds(slot, 1), :] = jnp.concatenate(rows, axis=1)

    for k in range(2):
        place(pair_ref, k * (width + SUB), k)
    for j in range(0, chips - 2, 2):
        for ref, chip in ((far_refs[j], j + 1 + core), (far_refs[j + 1], j + 2 - core)):
            for k in range(2):
                place(ref, k * (width + SUB), 2 * chip + k)
    place(far_refs[-2], 0, 2 * (chips - 1) + core)
    place(far_refs[-1], 0, 2 * (chips - 1) + 1 - core)
    fine = shifted_rows(aug_ref, t_ref, STAGE, lse_ref, top_ref, mass_ref, e_ref, carried_ref)

    @pl.when(jnp.logical_not(fine))
    def _():
        column = [pot_ref[g : g + 1, :] for g in range(2 * chips)]
        exact_rows(a_ref, t_ref, column, scores, lse_ref, None, None, carried_ref)


def moment_kernel(ns, rows_total, *refs):
    s_ref, l_refs, carried_ref = refs[0], refs[1 : 1 + ns], refs[1 + ns]
    keep_ref, send_ref, weight_ref, total_ref = refs[2 + ns :]
    c, r = lax.axis_index("col"), lax.axis_index("row")
    per = s_ref.shape[0] // ns // LANES
    shift = log_sum([l[...] for l in l_refs])
    weight_ref[...] = jnp.exp(l_refs[0][...] - shift) * (1.0 / rows_total)
    total = None
    for k in range(ns):
        for j in range(per):
            w = as_rows(weight_ref[pl.ds((c ^ k) * per + j, 1), :])
            at = (k * per + j) * LANES
            x = carried_ref[at : at + LANES, :] * w
            s = s_ref[at : at + LANES, :]
            for part in reversed(split3(x)):
                term = lax.dot_general(s, part, TN_DIMS, preferred_element_type=jnp.float32)
                total = term if total is None else total + term
    total_ref[...] = total
    half = keep_ref.shape[0]
    keep_ref[...] = total_ref[pl.ds(pl.multiple_of((r % 2) * half, half), half), :]
    send_ref[...] = total_ref[pl.ds(pl.multiple_of((1 - r % 2) * half, half), half), :]


def add_kernel(*refs):
    refs[-1][...] = tree(jnp.add, [r[...] for r in refs[:-1]])


def log_sum_kernel(*refs):
    refs[-1][...] = log_sum([r[...] for r in refs[:-1]])


def first_rows_kernel(*refs):
    s_ref, t_ref, pot_ref, m_refs = refs[0], refs[1], refs[2], refs[3:5]
    moment_ref, a_ref, lse_ref, top_ref, e_ref, mass_ref, aug_ref, scores = refs[5:]
    r = lax.axis_index("row")
    half = m_refs[0].shape[0]
    for k in range(2):
        moment_ref[pl.ds(pl.multiple_of((k ^ (r % 2)) * half, half), half), :] = m_refs[k][...]
    a_ref[...] = project4(s_ref[...], split3(moment_ref[...]))
    add_shifts(a_ref, t_ref, pot_ref[0:1, :], aug_ref, top_ref)
    fine = shifted_rows(aug_ref, t_ref, STAGE, lse_ref, top_ref, mass_ref, e_ref)

    @pl.when(jnp.logical_not(fine))
    def _():
        column = [pot_ref[g : g + 1, :] for g in range(pot_ref.shape[0])]
        exact_rows(a_ref, t_ref, column, scores, lse_ref, top_ref, e_ref)


def high_low(x):
    high = x.astype(jnp.bfloat16).astype(jnp.float32)
    at = lax.broadcasted_iota(jnp.int32, (SUB, x.shape[1]), 0)
    return jnp.where(at == 0, high, jnp.where(at == 1, x - high, 0.0)).astype(jnp.bfloat16)


def on_vector_unit(part):
    return part % 8 in (2, 4, 6)


def rows_kernel(rows_total, *refs):
    a_ref, e_ref, top_ref, t_ref, pot_ref = refs[:5]
    l_refs, (lse_ref, column_ref, weights, scores) = refs[5:-4], refs[-4:]
    nt, width = pot_ref.shape
    column_ref[...] = math.log(rows_total) - log_sum([l[...] for l in l_refs])
    column = [column_ref[pl.ds(block_at(k), 1), :] for k in range(nt)]
    change = [column[k] - pot_ref[k : k + 1, :] for k in range(nt)]
    weight = [jnp.exp(x) for x in change]
    for k in range(nt):
        weights[:, k * width : (k + 1) * width] = high_low(weight[k])
    steps = a_ref.shape[0] // LANES
    masses = []
    for i in range(steps):
        at = slice(i * LANES, (i + 1) * LANES)
        if on_vector_unit(i):
            total = None
            for k in range(nt):
                e = e_ref[at, k * width : (k + 1) * width].astype(jnp.float32)
                m = lane_fold(jnp.add, e * weight[k])
                total = m if total is None else total + m
            masses.append(as_lanes(jnp.sum(total, axis=1, keepdims=True)))
        else:
            sums = lax.dot_general(weights[...], e_ref[at, :], NT_DIMS, preferred_element_type=jnp.float32)
            masses.append(sums[0:1, :] + sums[1:2, :])
        row = row_of(i, steps)
        lse_ref[row, :] = top_ref[row, :] + jnp.log(masses[i])

    @pl.when(jnp.logical_not(within(masses)))
    def _():
        exact_rows(a_ref, t_ref, column, scores, lse_ref)


def columns_kernel(ns, cols_total, last, *refs):
    a_ref, e_ref, top_ref, t_ref, pot_ref, l_refs = *refs[:5], refs[5 : 5 + ns]
    out_refs, (sp_ref, weight_rows, weights, spread_rows, scores, both) = refs[5 + ns : -6], refs[-6:]
    c = lax.axis_index("col")
    nt, width = pot_ref.shape
    rows = a_ref.shape[0]
    per = rows // ns // LANES
    potential = math.log(cols_total) - log_sum([l[...] for l in l_refs])
    sp_ref[...] = potential
    weight_rows[...] = jnp.exp(potential + top_ref[...])
    for k in range(ns):
        for j in range(per):
            at = (k * per + j) * LANES
            weights[:, at : at + LANES] = high_low(weight_rows[pl.ds((c ^ k) * per + j, 1), :])

    def store(g, lse):
        if last:
            both[(g + lax.axis_index("row")) % 2, g // 2] = lse
        else:
            out_refs[0][pl.ds(block_at(g), 1), :] = lse

    sums = jnp.dot(weights[...], e_ref[...], preferred_element_type=jnp.float32)
    mass = sums[0:1, :] + sums[1:2, :]
    for g in range(nt):
        store(g, jnp.log(mass[:, g * width : (g + 1) * width]) - pot_ref[g : g + 1, :])

    @pl.when(jnp.logical_not(within([mass])))
    def _():
        exact_columns(ns, a_ref, t_ref, sp_ref, spread_rows, scores, store)

    if last:
        for k in range(2):
            out_refs[k][...] = both[k]


def exact_columns(ns, a_ref, t_ref, sp_ref, spread_rows, scores, store):
    c = lax.axis_index("col")
    rows, width = scores.shape
    per = rows // ns // LANES
    for k in range(ns):
        for j in range(per):
            at = (k * per + j) * LANES
            spread_rows[at : at + LANES, :] = as_rows(sp_ref[pl.ds((c ^ k) * per + j, 1), :])
    for g in range(t_ref.shape[0] // width):
        top = None
        for at in range(0, rows, LANES):
            a = a_ref[at : at + LANES, :]
            s = lax.dot_general(a, block_of(t_ref, g, width), NT_DIMS, preferred_element_type=jnp.float32)
            s = s + jnp.concatenate([spread_rows[at : at + LANES, :]] * (width // LANES), axis=1)
            scores[at : at + LANES, :] = s
            m = jnp.max(s.reshape(LANES // 8, 8, width), axis=0)
            top = m if top is None else jnp.maximum(top, m)
        top = jnp.max(top, axis=0, keepdims=True)
        mass = None
        for at in range(0, rows, LANES):
            e = jnp.exp(scores[at : at + LANES, :] - top)
            m = jnp.sum(e.reshape(LANES // 8, 8, width), axis=0)
            mass = m if mass is None else mass + m
        store(g, top + jnp.log(jnp.sum(mass, axis=0, keepdims=True)))


def split_kernel(x_ref, y_ref, *out_refs):
    for k, out_ref in enumerate(reversed(out_refs)):
        out_ref[...] = log_sum([x_ref[k], y_ref[k]])


def update_kernel(rows_total, *refs):
    refs[-1][...] = math.log(rows_total) - log_sum([l[...] for l in refs[:-1]])


def call(kernel, out, args, scratch=(), flops=0, exps=0):
    vmem = pl.BlockSpec(memory_space=pltpu.VMEM)
    bytes_accessed = sum(x.size * x.dtype.itemsize for x in list(args) + list(out))
    return pl.pallas_call(
        kernel,
        out_shape=list(out),
        in_specs=[vmem] * len(args),
        out_specs=[vmem] * len(out),
        scratch_shapes=list(scratch),
        compiler_params=pltpu.CompilerParams(vmem_limit_bytes=24 << 20),
        cost_estimate=pl.CostEstimate(flops=flops, bytes_accessed=bytes_accessed, transcendentals=exps),
    )(*args)


def swap(x, axis, k):
    return lax.ppermute(x, axis, [(i, i ^ k) for i in range(lax.axis_size(axis))])


def swap_by_core(x, even, odd):
    return lax.ppermute(x, "row", [(i, i ^ (odd if i % 2 else even)) for i in range(lax.axis_size("row"))])


def exchange(x, axis):
    return [x] + [swap(x, axis, k) for k in range(1, lax.axis_size(axis))]


def exchange_chips(x):
    return [x] + [swap(x, "row", k) for k in range(2, lax.axis_size("row"), 2)]


def combine(kernel, parts):
    return call(kernel, [jax.ShapeDtypeStruct(parts[0].shape, parts[0].dtype)], parts)[0]


def per_device(source, target, target_potential, prev_moment):
    f32, bf16, shape = jnp.float32, jnp.bfloat16, jax.ShapeDtypeStruct
    ns, nt = lax.axis_size("col"), lax.axis_size("row")
    piece, width = source.shape[0], target.shape[0]
    depth = source.shape[1]
    rows, cols = piece * ns, width * nt
    rows_total, cols_total = rows * nt, cols * ns
    tile = shape((rows // LANES, LANES), f32)
    projected = shape((rows, depth), bf16)
    flops, exps = 2 * rows * cols * depth, rows * cols
    row_scores = pltpu.VMEM((LANES, cols), f32)
    small = pltpu.VMEM(tile.shape, f32)
    sums = pltpu.VMEM((rows, LANES), f32)

    groups = width // LANES
    tail = jnp.pad(target_potential.reshape(groups, LANES), ((0, SUB - groups), (0, 0)))
    block = jnp.concatenate([target, tail], axis=0)
    chips = nt // 2
    mate = swap(block, "row", 1)
    pieces = exchange(source, "col")
    pair, = call(pair_kernel, [shape((2 * block.shape[0], LANES), bf16)], [block, mate])
    far = [swap_by_core(pair, 2 * j, 2 * j + 2) for j in range(1, chips - 1, 2)] + [swap(block, "row", nt - 2)]
    order = [0, ns - 2, ns - 1] + list(range(ns - 3, 0, -1)) if ns > 2 else list(range(ns))
    s, a = call(
        functools.partial(project_kernel, order),
        [projected, projected],
        [pieces[k] for k in order] + [prev_moment],
        flops=200 * rows * depth * depth,
    )
    far = [lax.optimization_barrier((x, a))[0] for x in far]
    far = [x for got in far for x in (got, swap(got, "row", 1))]
    augmented = shape((rows, 2 * depth), bf16)
    aug, top = call(
        functools.partial(shift_kernel, width), [augmented, tile], [a, block], flops=2 * rows * width * depth
    )
    lse, carried, t, pot = call(
        functools.partial(couple_kernel, chips, width),
        [tile, shape((rows, depth), f32), shape((cols, 2 * depth), bf16), shape((nt, width), f32)],
        [a, aug, top, pair] + far,
        [sums, pltpu.VMEM((rows, 2 * STAGE), bf16), row_scores],
        2 * flops,
        exps,
    )
    half = shape((depth // 2, depth), f32)
    keep, send = call(
        functools.partial(moment_kernel, ns, rows_total),
        [half, half],
        [s] + exchange(lse, "col") + [carried],
        [small, pltpu.VMEM((depth, depth), f32)],
        6 * rows * depth * depth,
    )
    part = combine(add_kernel, [keep, swap(send, "row", 1)])
    part = combine(add_kernel, exchange(part, "col"))
    part = combine(add_kernel, exchange_chips(part))
    moment, a, lse, top, e = call(
        first_rows_kernel,
        [shape((depth, depth), f32), projected, tile, tile, shape((rows, cols), bf16)],
        [s, t, pot, part, swap(part, "row", 1)],
        [sums, pltpu.VMEM(augmented.shape, bf16), row_scores],
        flops,
        exps,
    )
    for iteration in range(ITERS):
        last = iteration == ITERS - 1
        if iteration > 0:
            both = combine(log_sum_kernel, [column, swap(column, "row", 1)])
            lse, = call(
                functools.partial(rows_kernel, rows_total),
                [tile],
                [a, e, top, t, pot] + exchange_chips(both),
                [pltpu.VMEM((nt, width), f32), pltpu.VMEM((SUB, cols), bf16), row_scores],
                16 * rows * cols,
            )
        halves = shape((nt // 2, 1, width), f32)
        column, *sent, source_potential = call(
            functools.partial(columns_kernel, ns, cols_total, last),
            ([halves, halves] if last else [shape((nt, width), f32)]) + [tile],
            [a, e, top, t, pot] + exchange(lse, "col"),
            [
                small,
                pltpu.VMEM((SUB, rows), bf16),
                pltpu.VMEM((rows, LANES), f32),
                pltpu.VMEM((rows, width), f32),
                pltpu.VMEM((2, nt // 2, 1, width), f32),
            ],
            16 * rows * cols,
        )
    one = shape((1, width), f32)
    parts = call(split_kernel, [one] * (nt // 2), [column, swap(sent[0], "row", 1)])
    parts = [swap(x, "row", nt - 2 - 2 * k) for k, x in enumerate(parts[:-1])] + [parts[-1]]
    update, = call(functools.partial(update_kernel, rows_total), [one], parts)
    return moment, source_potential.reshape(rows), update.reshape(width)


def solution(mesh):
    placed = (P(("row", "col"), None), P(("col", "row"), None), P(("col", "row")), P())
    return jax.shard_map(
        per_device,
        mesh=mesh,
        in_specs=placed,
        out_specs=(P(), P("row"), P(("col", "row"))),
        check_vma=False,
    )
```

```python
import functools
import math

import jax
import jax.numpy as jnp
from jax import lax
from jax.experimental import pallas as pl
from jax.experimental.pallas import tpu as pltpu
from jax.sharding import PartitionSpec as P

ITERS = 2
LANES = 128
SUB = 16
STAGE = 512
SMALLEST = 1e-16
LARGEST = 1e12
NT_DIMS = (((1,), (1,)), ((), ()))
TN_DIMS = (((0,), (0,)), ((), ()))


def split3(x):
    high = x.astype(jnp.bfloat16)
    rest = x - high.astype(jnp.float32)
    mid = rest.astype(jnp.bfloat16)
    low = (rest - mid.astype(jnp.float32)).astype(jnp.bfloat16)
    return high, mid, low


def project4(rows, matrix_parts):
    total = None
    for part in reversed(matrix_parts):
        term = jnp.dot(rows, part, preferred_element_type=jnp.float32)
        total = term if total is None else total + term
    return (total.astype(jnp.bfloat16).astype(jnp.float32) * 4.0).astype(jnp.bfloat16)


def lane_fold(op, x):
    parts = [x[:, i : i + LANES] for i in range(0, x.shape[1], LANES)]
    return functools.reduce(op, parts)


def as_lanes(column):
    return jnp.broadcast_to(column, (LANES, LANES)).T[0:1, :]


def as_rows(lanes):
    return jnp.broadcast_to(lanes, (LANES, LANES)).T


def tree(op, parts):
    while len(parts) > 1:
        parts = [op(parts[i], parts[i + 1]) for i in range(0, len(parts), 2)]
    return parts[0]


def log_sum(parts):
    top = functools.reduce(jnp.maximum, parts)
    return top + jnp.log(tree(jnp.add, [jnp.exp(p - top) for p in parts]))


def within(masses):
    low = jnp.min(functools.reduce(jnp.minimum, masses))
    high = jnp.max(functools.reduce(jnp.maximum, masses))
    return jnp.logical_and(low > SMALLEST, high < LARGEST)


def block_of(t_ref, g, width):
    return t_ref[g * width : (g + 1) * width, :LANES]


def row_of(i, steps):
    per = steps // lax.axis_size("col")
    return pl.ds((lax.axis_index("col") ^ (i // per)) * per + i % per, 1)


def add_shifts(a_ref, t_ref, potential, aug_ref, top_ref):
    rows = a_ref.shape[0]
    steps = rows // LANES
    lane = lax.broadcasted_iota(jnp.int32, (LANES, LANES), 1)
    s = lax.dot_general(a_ref[...], t_ref[: potential.shape[1], :LANES], NT_DIMS, preferred_element_type=jnp.float32)
    aug_ref[:, :LANES] = a_ref[...]
    top = jnp.max(lane_fold(jnp.maximum, s + potential), axis=1, keepdims=True)
    for i in range(steps):
        at = slice(i * LANES, (i + 1) * LANES)
        shift = top[at, :].astype(jnp.bfloat16).astype(jnp.float32)
        aug_ref[at, LANES:] = jnp.where(lane == 0, 1.0, jnp.where(lane == 1, -shift, 0.0)).astype(jnp.bfloat16)
        top_ref[row_of(i, steps), :] = as_lanes(shift)


def exponentials(aug_ref, t_ref, e_ref, width, mass_ref=None):
    for at in range(0, t_ref.shape[0], width):
        t = t_ref[at : at + width, :]
        e = jnp.exp(lax.dot_general(aug_ref[...], t, NT_DIMS, preferred_element_type=jnp.float32))
        if mass_ref is not None:
            m = lane_fold(jnp.add, e)
            mass_ref[...] = m if at == 0 else mass_ref[...] + m
        e_ref[:, at : at + width] = e.astype(jnp.bfloat16)


def shifted_rows(aug_ref, t_ref, lse_ref, top_ref, mass_ref, e_ref):
    exponentials(aug_ref, t_ref, e_ref, STAGE, mass_ref)
    steps = aug_ref.shape[0] // LANES
    masses = []
    for i in range(steps):
        at = slice(i * LANES, (i + 1) * LANES)
        masses.append(as_lanes(jnp.sum(mass_ref[at, :], axis=1, keepdims=True)))
        row = row_of(i, steps)
        lse_ref[row, :] = top_ref[row, :] + jnp.log(masses[i])
    return within(masses)


def shifted_couple(aug_ref, t_ref, lse_ref, top_ref, e_ref, carried_ref):
    exponentials(aug_ref, t_ref, e_ref, STAGE)
    rows = aug_ref.shape[0]
    steps = rows // LANES
    masses = []
    for h in range(0, rows, 4 * LANES):
        d = jnp.dot(e_ref[h : h + 4 * LANES, :], t_ref[...], preferred_element_type=jnp.float32)
        for i in range(h // LANES, h // LANES + 4):
            at = slice(i * LANES - h, (i + 1) * LANES - h)
            mass = d[at, LANES + 1 : LANES + 2]
            carried_ref[i * LANES : (i + 1) * LANES, :] = d[at, :LANES] / mass
            masses.append(as_lanes(mass))
            row = row_of(i, steps)
            lse_ref[row, :] = top_ref[row, :] + jnp.log(masses[i])
    return within(masses)


def exact_rows(a_ref, t_ref, column, scores, lse_ref, top_ref=None, e_ref=None, carried_ref=None):
    steps = a_ref.shape[0] // LANES
    width = column[0].shape[1]

    @pl.loop(0, steps)
    def _(i):
        rows = pl.ds(pl.multiple_of(i * LANES, LANES), LANES)
        top = None
        for g in range(len(column)):
            t = block_of(t_ref, g, width)
            s = column[g] + lax.dot_general(a_ref[rows, :], t, NT_DIMS, preferred_element_type=jnp.float32)
            scores[:, g * width : (g + 1) * width] = s
            m = lane_fold(jnp.maximum, s)
            top = m if top is None else jnp.maximum(top, m)
        top = jnp.max(top, axis=1, keepdims=True)
        mass, carried = None, None
        for g in range(len(column)):
            cols = slice(g * width, (g + 1) * width)
            e = jnp.exp(scores[:, cols] - top)
            m = lane_fold(jnp.add, e)
            mass = m if mass is None else mass + m
            if e_ref is not None:
                e_ref[rows, cols] = e.astype(jnp.bfloat16)
            if carried_ref is not None:
                t = block_of(t_ref, g, width)
                d = jnp.dot(e.astype(jnp.bfloat16), t, preferred_element_type=jnp.float32)
                carried = d if carried is None else carried + d
        mass = jnp.sum(mass, axis=1, keepdims=True)
        row = row_of(i, steps)
        lse_ref[row, :] = as_lanes(top + jnp.log(mass))
        if top_ref is not None:
            top_ref[row, :] = as_lanes(top)
        if carried_ref is not None:
            carried_ref[rows, :] = carried / mass


def project_kernel(order, *refs):
    s_refs, moment_ref, s_ref, a_ref = refs[: len(order)], *refs[len(order) :]
    piece = s_refs[0].shape[0]
    parts = split3(moment_ref[...])
    for k, piece_ref in zip(order, s_refs):
        at = slice(k * piece, (k + 1) * piece)
        s_ref[at, :] = piece_ref[...]
        a_ref[at, :] = project4(piece_ref[...], parts)


def potential_of(block_ref, width):
    tail = block_ref[width:, :].astype(jnp.float32)
    return jnp.concatenate([tail[j : j + 1, :] for j in range(width // LANES)], axis=1)


def shift_kernel(width, a_ref, block_ref, aug_ref, top_ref):
    add_shifts(a_ref, block_ref, potential_of(block_ref, width), aug_ref, top_ref)


def couple_kernel(nt, width, *refs):
    a_ref, aug_ref, top_ref, t_refs = refs[0], refs[1], refs[2], refs[3 : 3 + nt]
    lse_ref, carried_ref, t_ref, pot_ref, e_ref, scores = refs[3 + nt :]
    lane = lax.broadcasted_iota(jnp.int32, (LANES, LANES), 1)
    for g in range(nt):
        t_ref[g * width : (g + 1) * width, :LANES] = t_refs[g][:width, :]
        pot_ref[g : g + 1, :] = potential_of(t_refs[g], width)
        for j in range(0, width, LANES):
            potential = as_rows(pot_ref[g : g + 1, j : j + LANES])
            added = jnp.where(lane == 0, potential, jnp.where(lane == 1, 1.0, 0.0))
            at = g * width + j
            t_ref[at : at + LANES, LANES:] = added.astype(jnp.bfloat16)
    fine = shifted_couple(aug_ref, t_ref, lse_ref, top_ref, e_ref, carried_ref)

    @pl.when(jnp.logical_not(fine))
    def _():
        column = [pot_ref[g : g + 1, :] for g in range(nt)]
        exact_rows(a_ref, t_ref, column, scores, lse_ref, None, None, carried_ref)


def moment_kernel(ns, rows_total, *refs):
    s_ref, l_refs, carried_ref = refs[0], refs[1 : 1 + ns], refs[1 + ns]
    keep_ref, send_ref, weight_ref, total_ref = refs[2 + ns :]
    c, r = lax.axis_index("col"), lax.axis_index("row")
    per = s_ref.shape[0] // ns // LANES
    shift = log_sum([l[...] for l in l_refs])
    weight_ref[...] = jnp.exp(l_refs[0][...] - shift) * (1.0 / rows_total)
    total = None
    for k in range(ns):
        for j in range(per):
            w = as_rows(weight_ref[pl.ds((c ^ k) * per + j, 1), :])
            at = (k * per + j) * LANES
            x = carried_ref[at : at + LANES, :] * w
            s = s_ref[at : at + LANES, :]
            for part in reversed(split3(x)):
                term = lax.dot_general(s, part, TN_DIMS, preferred_element_type=jnp.float32)
                total = term if total is None else total + term
    total_ref[...] = total
    half = keep_ref.shape[0]
    keep_ref[...] = total_ref[pl.ds(pl.multiple_of((r % 2) * half, half), half), :]
    send_ref[...] = total_ref[pl.ds(pl.multiple_of((1 - r % 2) * half, half), half), :]


def add_kernel(*refs):
    refs[-1][...] = tree(jnp.add, [r[...] for r in refs[:-1]])


def log_sum_kernel(*refs):
    refs[-1][...] = log_sum([r[...] for r in refs[:-1]])


def first_rows_kernel(*refs):
    s_ref, t_ref, pot_ref, m_refs = refs[0], refs[1], refs[2], refs[3:5]
    moment_ref, a_ref, lse_ref, top_ref, e_ref, mass_ref, aug_ref, scores = refs[5:]
    r = lax.axis_index("row")
    half = m_refs[0].shape[0]
    for k in range(2):
        moment_ref[pl.ds(pl.multiple_of((k ^ (r % 2)) * half, half), half), :] = m_refs[k][...]
    a_ref[...] = project4(s_ref[...], split3(moment_ref[...]))
    add_shifts(a_ref, t_ref, pot_ref[0:1, :], aug_ref, top_ref)
    fine = shifted_rows(aug_ref, t_ref, lse_ref, top_ref, mass_ref, e_ref)

    @pl.when(jnp.logical_not(fine))
    def _():
        column = [pot_ref[g : g + 1, :] for g in range(pot_ref.shape[0])]
        exact_rows(a_ref, t_ref, column, scores, lse_ref, top_ref, e_ref)


def high_low(x):
    high = x.astype(jnp.bfloat16).astype(jnp.float32)
    at = lax.broadcasted_iota(jnp.int32, (SUB, x.shape[1]), 0)
    return jnp.where(at == 0, high, jnp.where(at == 1, x - high, 0.0)).astype(jnp.bfloat16)


def on_vector_unit(part):
    return part % 8 in (2, 4, 6)


def rows_kernel(rows_total, *refs):
    a_ref, e_ref, top_ref, t_ref, pot_ref = refs[:5]
    l_refs, (lse_ref, column_ref, weights, scores) = refs[5:-4], refs[-4:]
    r = lax.axis_index("row")
    nt, width = pot_ref.shape
    column_ref[...] = math.log(rows_total) - log_sum([l[...] for l in l_refs])
    column = [column_ref[pl.ds(r ^ k, 1), :] for k in range(nt)]
    change = [column[k] - pot_ref[k : k + 1, :] for k in range(nt)]
    weight = [jnp.exp(x) for x in change]
    for k in range(nt):
        weights[:, k * width : (k + 1) * width] = high_low(weight[k])
    steps = a_ref.shape[0] // LANES
    masses = []
    for i in range(steps):
        at = slice(i * LANES, (i + 1) * LANES)
        if on_vector_unit(i):
            total = None
            for k in range(nt):
                e = e_ref[at, k * width : (k + 1) * width].astype(jnp.float32)
                m = lane_fold(jnp.add, e * weight[k])
                total = m if total is None else total + m
            masses.append(as_lanes(jnp.sum(total, axis=1, keepdims=True)))
        else:
            sums = lax.dot_general(weights[...], e_ref[at, :], NT_DIMS, preferred_element_type=jnp.float32)
            masses.append(sums[0:1, :] + sums[1:2, :])
        row = row_of(i, steps)
        lse_ref[row, :] = top_ref[row, :] + jnp.log(masses[i])

    @pl.when(jnp.logical_not(within(masses)))
    def _():
        exact_rows(a_ref, t_ref, column, scores, lse_ref)


def columns_kernel(ns, cols_total, last, *refs):
    a_ref, e_ref, top_ref, t_ref, pot_ref, l_refs = *refs[:5], refs[5 : 5 + ns]
    out_refs, (sp_ref, weight_rows, weights, spread_rows, scores) = refs[5 + ns : -5], refs[-5:]
    c, r = lax.axis_index("col"), lax.axis_index("row")
    nt, width = pot_ref.shape
    rows = a_ref.shape[0]
    per = rows // ns // LANES
    potential = math.log(cols_total) - log_sum([l[...] for l in l_refs])
    sp_ref[...] = potential
    weight_rows[...] = jnp.exp(potential + top_ref[...])
    for k in range(ns):
        for j in range(per):
            at = (k * per + j) * LANES
            weights[:, at : at + LANES] = high_low(weight_rows[pl.ds((c ^ k) * per + j, 1), :])

    def store(g, lse):
        if last:
            out_refs[g % 2][g // 2] = lse
        else:
            out_refs[0][pl.ds(r ^ g, 1), :] = lse

    sums = jnp.dot(weights[...], e_ref[...], preferred_element_type=jnp.float32)
    mass = sums[0:1, :] + sums[1:2, :]
    for g in range(nt):
        store(g, jnp.log(mass[:, g * width : (g + 1) * width]) - pot_ref[g : g + 1, :])

    @pl.when(jnp.logical_not(within([mass])))
    def _():
        exact_columns(ns, a_ref, t_ref, sp_ref, spread_rows, scores, store)


def exact_columns(ns, a_ref, t_ref, sp_ref, spread_rows, scores, store):
    c = lax.axis_index("col")
    rows, width = scores.shape
    per = rows // ns // LANES
    for k in range(ns):
        for j in range(per):
            at = (k * per + j) * LANES
            spread_rows[at : at + LANES, :] = as_rows(sp_ref[pl.ds((c ^ k) * per + j, 1), :])
    for g in range(t_ref.shape[0] // width):
        top = None
        for at in range(0, rows, LANES):
            a = a_ref[at : at + LANES, :]
            s = lax.dot_general(a, block_of(t_ref, g, width), NT_DIMS, preferred_element_type=jnp.float32)
            s = s + jnp.concatenate([spread_rows[at : at + LANES, :]] * (width // LANES), axis=1)
            scores[at : at + LANES, :] = s
            m = jnp.max(s.reshape(LANES // 8, 8, width), axis=0)
            top = m if top is None else jnp.maximum(top, m)
        top = jnp.max(top, axis=0, keepdims=True)
        mass = None
        for at in range(0, rows, LANES):
            e = jnp.exp(scores[at : at + LANES, :] - top)
            m = jnp.sum(e.reshape(LANES // 8, 8, width), axis=0)
            mass = m if mass is None else mass + m
        store(g, top + jnp.log(jnp.sum(mass, axis=0, keepdims=True)))


def split_kernel(x_ref, y_ref, *out_refs):
    for k, out_ref in enumerate(reversed(out_refs)):
        out_ref[...] = log_sum([x_ref[k], y_ref[k]])


def update_kernel(rows_total, *refs):
    refs[-1][...] = math.log(rows_total) - log_sum([l[...] for l in refs[:-1]])


def call(kernel, out, args, scratch=(), flops=0, exps=0):
    vmem = pl.BlockSpec(memory_space=pltpu.VMEM)
    bytes_accessed = sum(x.size * x.dtype.itemsize for x in list(args) + list(out))
    return pl.pallas_call(
        kernel,
        out_shape=list(out),
        in_specs=[vmem] * len(args),
        out_specs=[vmem] * len(out),
        scratch_shapes=list(scratch),
        compiler_params=pltpu.CompilerParams(vmem_limit_bytes=24 << 20),
        cost_estimate=pl.CostEstimate(flops=flops, bytes_accessed=bytes_accessed, transcendentals=exps),
    )(*args)


def swap(x, axis, k):
    return lax.ppermute(x, axis, [(i, i ^ k) for i in range(lax.axis_size(axis))])


def exchange(x, axis):
    return [x] + [swap(x, axis, k) for k in range(1, lax.axis_size(axis))]


def exchange_chips(x):
    return [x] + [swap(x, "row", k) for k in range(2, lax.axis_size("row"), 2)]


def combine(kernel, parts):
    return call(kernel, [jax.ShapeDtypeStruct(parts[0].shape, parts[0].dtype)], parts)[0]


def per_device(source, target, target_potential, prev_moment):
    f32, bf16, shape = jnp.float32, jnp.bfloat16, jax.ShapeDtypeStruct
    ns, nt = lax.axis_size("col"), lax.axis_size("row")
    piece, width = source.shape[0], target.shape[0]
    depth = source.shape[1]
    rows, cols = piece * ns, width * nt
    rows_total, cols_total = rows * nt, cols * ns
    tile = shape((rows // LANES, LANES), f32)
    projected = shape((rows, depth), bf16)
    flops, exps = 2 * rows * cols * depth, rows * cols
    row_scores = pltpu.VMEM((LANES, cols), f32)
    small = pltpu.VMEM(tile.shape, f32)
    sums = pltpu.VMEM((rows, LANES), f32)

    groups = width // LANES
    tail = jnp.pad(target_potential.reshape(groups, LANES), ((0, SUB - groups), (0, 0)))
    block = jnp.concatenate([target, tail], axis=0)
    pieces = exchange(source, "col")
    far = exchange_chips(block)
    order = [0, ns - 2, ns - 1] + list(range(ns - 3, 0, -1)) if ns > 2 else list(range(ns))
    s, a = call(
        functools.partial(project_kernel, order),
        [projected, projected],
        [pieces[k] for k in order] + [prev_moment],
        flops=200 * rows * depth * depth,
    )
    far = [lax.optimization_barrier((x, a))[0] for x in far]
    blocks = [x for pair in zip(far, [swap(x, "row", 1) for x in far]) for x in pair]
    augmented = shape((rows, 2 * depth), bf16)
    aug, top = call(
        functools.partial(shift_kernel, width), [augmented, tile], [a, far[0]], flops=2 * rows * width * depth
    )
    lse, carried, t, pot = call(
        functools.partial(couple_kernel, nt, width),
        [tile, shape((rows, depth), f32), shape((cols, 2 * depth), bf16), shape((nt, width), f32)],
        [a, aug, top] + blocks,
        [pltpu.VMEM((rows, cols), bf16), row_scores],
        2 * flops,
        exps,
    )
    half = shape((depth // 2, depth), f32)
    keep, send = call(
        functools.partial(moment_kernel, ns, rows_total),
        [half, half],
        [s] + exchange(lse, "col") + [carried],
        [small, pltpu.VMEM((depth, depth), f32)],
        6 * rows * depth * depth,
    )
    part = combine(add_kernel, [keep, swap(send, "row", 1)])
    part = combine(add_kernel, exchange(part, "col"))
    part = combine(add_kernel, exchange_chips(part))
    moment, a, lse, top, e = call(
        first_rows_kernel,
        [shape((depth, depth), f32), projected, tile, tile, shape((rows, cols), bf16)],
        [s, t, pot, part, swap(part, "row", 1)],
        [sums, pltpu.VMEM(augmented.shape, bf16), row_scores],
        flops,
        exps,
    )
    for iteration in range(ITERS):
        last = iteration == ITERS - 1
        if iteration > 0:
            both = combine(log_sum_kernel, [column, swap(column, "row", 1)])
            lse, = call(
                functools.partial(rows_kernel, rows_total),
                [tile],
                [a, e, top, t, pot] + exchange_chips(both),
                [pltpu.VMEM((nt, width), f32), pltpu.VMEM((SUB, cols), bf16), row_scores],
                16 * rows * cols,
            )
        halves = shape((nt // 2, 1, width), f32)
        column, *sent, source_potential = call(
            functools.partial(columns_kernel, ns, cols_total, last),
            ([halves, halves] if last else [shape((nt, width), f32)]) + [tile],
            [a, e, top, t, pot] + exchange(lse, "col"),
            [
                small,
                pltpu.VMEM((SUB, rows), bf16),
                pltpu.VMEM((rows, LANES), f32),
                pltpu.VMEM((rows, width), f32),
            ],
            16 * rows * cols,
        )
    one = shape((1, width), f32)
    parts = call(split_kernel, [one] * (nt // 2), [column, swap(sent[0], "row", 1)])
    parts = [swap(x, "row", nt - 2 - 2 * k) for k, x in enumerate(parts[:-1])] + [parts[-1]]
    update, = call(functools.partial(update_kernel, rows_total), [one], parts)
    return moment, source_potential.reshape(rows), update.reshape(width)


def solution(mesh):
    placed = (P(("row", "col"), None), P(("col", "row"), None), P(("col", "row")), P())
    return jax.shard_map(
        per_device,
        mesh=mesh,
        in_specs=placed,
        out_specs=(P(), P("row"), P(("col", "row"))),
        check_vma=False,
    )
```

```python
import functools
import math

import jax
import jax.numpy as jnp
from jax import lax
from jax.experimental import pallas as pl
from jax.experimental.pallas import tpu as pltpu
from jax.sharding import PartitionSpec as P

ITERS = 2
LANES = 128
SUB = 16
SMALLEST = 1e-16
LARGEST = 1e12
NT_DIMS = (((1,), (1,)), ((), ()))
TN_DIMS = (((0,), (0,)), ((), ()))


def split3(x):
    high = x.astype(jnp.bfloat16)
    rest = x - high.astype(jnp.float32)
    mid = rest.astype(jnp.bfloat16)
    low = (rest - mid.astype(jnp.float32)).astype(jnp.bfloat16)
    return high, mid, low


def project4(rows, matrix_parts):
    total = None
    for part in reversed(matrix_parts):
        term = jnp.dot(rows, part, preferred_element_type=jnp.float32)
        total = term if total is None else total + term
    return (total.astype(jnp.bfloat16).astype(jnp.float32) * 4.0).astype(jnp.bfloat16)


def lane_fold(op, x):
    parts = [x[:, i : i + LANES] for i in range(0, x.shape[1], LANES)]
    return functools.reduce(op, parts)


def as_lanes(column):
    return jnp.broadcast_to(column, (LANES, LANES)).T[0:1, :]


def as_rows(lanes):
    return jnp.broadcast_to(lanes, (LANES, LANES)).T


def tree(op, parts):
    while len(parts) > 1:
        parts = [op(parts[i], parts[i + 1]) for i in range(0, len(parts), 2)]
    return parts[0]


def log_sum(parts):
    top = functools.reduce(jnp.maximum, parts)
    return top + jnp.log(tree(jnp.add, [jnp.exp(p - top) for p in parts]))


def within(masses):
    low = jnp.min(functools.reduce(jnp.minimum, masses))
    high = jnp.max(functools.reduce(jnp.maximum, masses))
    return jnp.logical_and(low > SMALLEST, high < LARGEST)


def block_of(t_ref, g, width):
    return t_ref[g * width : (g + 1) * width, :LANES]


def row_of(i, steps):
    per = steps // lax.axis_size("col")
    return pl.ds((lax.axis_index("col") ^ (i // per)) * per + i % per, 1)


def add_shifts(a_ref, t_ref, potential, shift_ref, top_ref):
    steps = a_ref.shape[0] // LANES
    t = t_ref[: potential.shape[1], :LANES]
    s = lax.dot_general(a_ref[...], t, NT_DIMS, preferred_element_type=jnp.float32)
    top = jnp.max(lane_fold(jnp.maximum, s + potential), axis=1, keepdims=True)
    for i in range(steps):
        at = slice(i * LANES, (i + 1) * LANES)
        shift_ref[at, :] = jnp.broadcast_to(top[at, :], (LANES, LANES))
        top_ref[row_of(i, steps), :] = as_lanes(top[at, :])


def exponentials(a_ref, t_ref, pot_ref, shift_ref, e_ref, mass_ref=None):
    width = pot_ref.shape[1]
    for g in range(pot_ref.shape[0]):
        cols = slice(g * width, (g + 1) * width)
        for h in range(0, a_ref.shape[0], 2 * LANES):
            at = slice(h, h + 2 * LANES)
            s = lax.dot_general(a_ref[at, :], t_ref[cols, :LANES], NT_DIMS, preferred_element_type=jnp.float32)
            shift = jnp.concatenate([shift_ref[at, :]] * (width // LANES), axis=1)
            e = jnp.exp(s + pot_ref[g : g + 1, :] - shift)
            if mass_ref is not None:
                m = lane_fold(jnp.add, e)
                mass_ref[at, :] = m if g == 0 else mass_ref[at, :] + m
            e_ref[at, cols] = e.astype(jnp.bfloat16)


def shifted_rows(a_ref, t_ref, pot_ref, shift_ref, lse_ref, top_ref, mass_ref, e_ref):
    exponentials(a_ref, t_ref, pot_ref, shift_ref, e_ref, mass_ref)
    steps = a_ref.shape[0] // LANES
    masses = []
    for i in range(steps):
        at = slice(i * LANES, (i + 1) * LANES)
        masses.append(as_lanes(jnp.sum(mass_ref[at, :], axis=1, keepdims=True)))
        row = row_of(i, steps)
        lse_ref[row, :] = top_ref[row, :] + jnp.log(masses[i])
    return within(masses)


def shifted_couple(a_ref, t_ref, pot_ref, shift_ref, lse_ref, top_ref, e_ref, carried_ref):
    exponentials(a_ref, t_ref, pot_ref, shift_ref, e_ref)
    rows = a_ref.shape[0]
    steps = rows // LANES
    masses = []
    for h in range(0, rows, 4 * LANES):
        d = jnp.dot(e_ref[h : h + 4 * LANES, :], t_ref[...], preferred_element_type=jnp.float32)
        for i in range(h // LANES, h // LANES + 4):
            at = slice(i * LANES - h, (i + 1) * LANES - h)
            mass = d[at, LANES : LANES + 1]
            carried_ref[i * LANES : (i + 1) * LANES, :] = d[at, :LANES] / mass
            masses.append(as_lanes(mass))
            row = row_of(i, steps)
            lse_ref[row, :] = top_ref[row, :] + jnp.log(masses[i])
    return within(masses)


def exact_rows(a_ref, t_ref, column, scores, lse_ref, top_ref=None, e_ref=None, carried_ref=None):
    steps = a_ref.shape[0] // LANES
    width = column[0].shape[1]

    @pl.loop(0, steps)
    def _(i):
        rows = pl.ds(pl.multiple_of(i * LANES, LANES), LANES)
        top = None
        for g in range(len(column)):
            t = block_of(t_ref, g, width)
            s = column[g] + lax.dot_general(a_ref[rows, :], t, NT_DIMS, preferred_element_type=jnp.float32)
            scores[:, g * width : (g + 1) * width] = s
            m = lane_fold(jnp.maximum, s)
            top = m if top is None else jnp.maximum(top, m)
        top = jnp.max(top, axis=1, keepdims=True)
        mass, carried = None, None
        for g in range(len(column)):
            cols = slice(g * width, (g + 1) * width)
            e = jnp.exp(scores[:, cols] - top)
            m = lane_fold(jnp.add, e)
            mass = m if mass is None else mass + m
            if e_ref is not None:
                e_ref[rows, cols] = e.astype(jnp.bfloat16)
            if carried_ref is not None:
                t = block_of(t_ref, g, width)
                d = jnp.dot(e.astype(jnp.bfloat16), t, preferred_element_type=jnp.float32)
                carried = d if carried is None else carried + d
        mass = jnp.sum(mass, axis=1, keepdims=True)
        row = row_of(i, steps)
        lse_ref[row, :] = as_lanes(top + jnp.log(mass))
        if top_ref is not None:
            top_ref[row, :] = as_lanes(top)
        if carried_ref is not None:
            carried_ref[rows, :] = carried / mass


def project_kernel(order, *refs):
    s_refs, moment_ref, s_ref, a_ref = refs[: len(order)], *refs[len(order) :]
    piece = s_refs[0].shape[0]
    parts = split3(moment_ref[...])
    for k, piece_ref in zip(order, s_refs):
        at = slice(k * piece, (k + 1) * piece)
        s_ref[at, :] = piece_ref[...]
        a_ref[at, :] = project4(piece_ref[...], parts)


def potential_of(block_ref, width):
    tail = block_ref[width:, :].astype(jnp.float32)
    return jnp.concatenate([tail[j : j + 1, :] for j in range(width // LANES)], axis=1)


def shift_kernel(width, a_ref, block_ref, shift_ref, top_ref):
    add_shifts(a_ref, block_ref, potential_of(block_ref, width), shift_ref, top_ref)


def couple_kernel(nt, width, *refs):
    a_ref, shift_ref, top_ref, t_refs = refs[0], refs[1], refs[2], refs[3 : 3 + nt]
    lse_ref, carried_ref, t_ref, pot_ref, e_ref, scores = refs[3 + nt :]
    lane = lax.broadcasted_iota(jnp.int32, (width, LANES), 1)
    one = jnp.where(lane == 0, 1.0, 0.0).astype(jnp.bfloat16)
    for g in range(nt):
        at = slice(g * width, (g + 1) * width)
        t_ref[at, :LANES] = t_refs[g][:width, :]
        t_ref[at, LANES:] = one
        pot_ref[g : g + 1, :] = potential_of(t_refs[g], width)
    fine = shifted_couple(a_ref, t_ref, pot_ref, shift_ref, lse_ref, top_ref, e_ref, carried_ref)

    @pl.when(jnp.logical_not(fine))
    def _():
        column = [pot_ref[g : g + 1, :] for g in range(nt)]
        exact_rows(a_ref, t_ref, column, scores, lse_ref, None, None, carried_ref)


def moment_kernel(ns, rows_total, *refs):
    s_ref, l_refs, carried_ref = refs[0], refs[1 : 1 + ns], refs[1 + ns]
    keep_ref, send_ref, weight_ref, total_ref = refs[2 + ns :]
    c, r = lax.axis_index("col"), lax.axis_index("row")
    per = s_ref.shape[0] // ns // LANES
    shift = log_sum([l[...] for l in l_refs])
    weight_ref[...] = jnp.exp(l_refs[0][...] - shift) * (1.0 / rows_total)
    total = None
    for k in range(ns):
        for j in range(per):
            w = as_rows(weight_ref[pl.ds((c ^ k) * per + j, 1), :])
            at = (k * per + j) * LANES
            x = carried_ref[at : at + LANES, :] * w
            s = s_ref[at : at + LANES, :]
            for part in reversed(split3(x)):
                term = lax.dot_general(s, part, TN_DIMS, preferred_element_type=jnp.float32)
                total = term if total is None else total + term
    total_ref[...] = total
    half = keep_ref.shape[0]
    keep_ref[...] = total_ref[pl.ds(pl.multiple_of((r % 2) * half, half), half), :]
    send_ref[...] = total_ref[pl.ds(pl.multiple_of((1 - r % 2) * half, half), half), :]


def add_kernel(*refs):
    refs[-1][...] = tree(jnp.add, [r[...] for r in refs[:-1]])


def log_sum_kernel(*refs):
    refs[-1][...] = log_sum([r[...] for r in refs[:-1]])


def first_rows_kernel(*refs):
    s_ref, t_ref, pot_ref, m_refs = refs[0], refs[1], refs[2], refs[3:5]
    moment_ref, a_ref, lse_ref, top_ref, e_ref, mass_ref, shift_ref, scores = refs[5:]
    r = lax.axis_index("row")
    half = m_refs[0].shape[0]
    for k in range(2):
        moment_ref[pl.ds(pl.multiple_of((k ^ (r % 2)) * half, half), half), :] = m_refs[k][...]
    a_ref[...] = project4(s_ref[...], split3(moment_ref[...]))
    add_shifts(a_ref, t_ref, pot_ref[0:1, :], shift_ref, top_ref)
    fine = shifted_rows(a_ref, t_ref, pot_ref, shift_ref, lse_ref, top_ref, mass_ref, e_ref)

    @pl.when(jnp.logical_not(fine))
    def _():
        column = [pot_ref[g : g + 1, :] for g in range(pot_ref.shape[0])]
        exact_rows(a_ref, t_ref, column, scores, lse_ref, top_ref, e_ref)


def high_low(x):
    high = x.astype(jnp.bfloat16).astype(jnp.float32)
    at = lax.broadcasted_iota(jnp.int32, (SUB, x.shape[1]), 0)
    return jnp.where(at == 0, high, jnp.where(at == 1, x - high, 0.0)).astype(jnp.bfloat16)


def on_vector_unit(part):
    return part % 8 in (2, 4, 6)


def rows_kernel(rows_total, *refs):
    a_ref, e_ref, top_ref, t_ref, pot_ref = refs[:5]
    l_refs, (lse_ref, column_ref, weights, scores) = refs[5:-4], refs[-4:]
    r = lax.axis_index("row")
    nt, width = pot_ref.shape
    column_ref[...] = math.log(rows_total) - log_sum([l[...] for l in l_refs])
    column = [column_ref[pl.ds(r ^ k, 1), :] for k in range(nt)]
    change = [column[k] - pot_ref[k : k + 1, :] for k in range(nt)]
    weight = [jnp.exp(x) for x in change]
    for k in range(nt):
        weights[:, k * width : (k + 1) * width] = high_low(weight[k])
    steps = a_ref.shape[0] // LANES
    masses = []
    for i in range(steps):
        at = slice(i * LANES, (i + 1) * LANES)
        if on_vector_unit(i):
            total = None
            for k in range(nt):
                e = e_ref[at, k * width : (k + 1) * width].astype(jnp.float32)
                m = lane_fold(jnp.add, e * weight[k])
                total = m if total is None else total + m
            masses.append(as_lanes(jnp.sum(total, axis=1, keepdims=True)))
        else:
            sums = lax.dot_general(weights[...], e_ref[at, :], NT_DIMS, preferred_element_type=jnp.float32)
            masses.append(sums[0:1, :] + sums[1:2, :])
        row = row_of(i, steps)
        lse_ref[row, :] = top_ref[row, :] + jnp.log(masses[i])

    @pl.when(jnp.logical_not(within(masses)))
    def _():
        exact_rows(a_ref, t_ref, column, scores, lse_ref)


def columns_kernel(ns, cols_total, last, *refs):
    a_ref, e_ref, top_ref, t_ref, pot_ref, l_refs = *refs[:5], refs[5 : 5 + ns]
    out_refs, (sp_ref, weight_rows, weights, spread_rows, scores) = refs[5 + ns : -5], refs[-5:]
    c, r = lax.axis_index("col"), lax.axis_index("row")
    nt, width = pot_ref.shape
    rows = a_ref.shape[0]
    per = rows // ns // LANES
    potential = math.log(cols_total) - log_sum([l[...] for l in l_refs])
    sp_ref[...] = potential
    weight_rows[...] = jnp.exp(potential + top_ref[...])
    for k in range(ns):
        for j in range(per):
            at = (k * per + j) * LANES
            weights[:, at : at + LANES] = high_low(weight_rows[pl.ds((c ^ k) * per + j, 1), :])

    def store(g, lse):
        if last:
            out_refs[g % 2][g // 2] = lse
        else:
            out_refs[0][pl.ds(r ^ g, 1), :] = lse

    sums = jnp.dot(weights[...], e_ref[...], preferred_element_type=jnp.float32)
    mass = sums[0:1, :] + sums[1:2, :]
    for g in range(nt):
        store(g, jnp.log(mass[:, g * width : (g + 1) * width]) - pot_ref[g : g + 1, :])

    @pl.when(jnp.logical_not(within([mass])))
    def _():
        exact_columns(ns, a_ref, t_ref, sp_ref, spread_rows, scores, store)


def exact_columns(ns, a_ref, t_ref, sp_ref, spread_rows, scores, store):
    c = lax.axis_index("col")
    rows, width = scores.shape
    per = rows // ns // LANES
    for k in range(ns):
        for j in range(per):
            at = (k * per + j) * LANES
            spread_rows[at : at + LANES, :] = as_rows(sp_ref[pl.ds((c ^ k) * per + j, 1), :])
    for g in range(t_ref.shape[0] // width):
        top = None
        for at in range(0, rows, LANES):
            a = a_ref[at : at + LANES, :]
            s = lax.dot_general(a, block_of(t_ref, g, width), NT_DIMS, preferred_element_type=jnp.float32)
            s = s + jnp.concatenate([spread_rows[at : at + LANES, :]] * (width // LANES), axis=1)
            scores[at : at + LANES, :] = s
            m = jnp.max(s.reshape(LANES // 8, 8, width), axis=0)
            top = m if top is None else jnp.maximum(top, m)
        top = jnp.max(top, axis=0, keepdims=True)
        mass = None
        for at in range(0, rows, LANES):
            e = jnp.exp(scores[at : at + LANES, :] - top)
            m = jnp.sum(e.reshape(LANES // 8, 8, width), axis=0)
            mass = m if mass is None else mass + m
        store(g, top + jnp.log(jnp.sum(mass, axis=0, keepdims=True)))


def split_kernel(x_ref, y_ref, *out_refs):
    for k, out_ref in enumerate(reversed(out_refs)):
        out_ref[...] = log_sum([x_ref[k], y_ref[k]])


def update_kernel(rows_total, *refs):
    refs[-1][...] = math.log(rows_total) - log_sum([l[...] for l in refs[:-1]])


def call(kernel, out, args, scratch=(), flops=0, exps=0):
    vmem = pl.BlockSpec(memory_space=pltpu.VMEM)
    bytes_accessed = sum(x.size * x.dtype.itemsize for x in list(args) + list(out))
    return pl.pallas_call(
        kernel,
        out_shape=list(out),
        in_specs=[vmem] * len(args),
        out_specs=[vmem] * len(out),
        scratch_shapes=list(scratch),
        compiler_params=pltpu.CompilerParams(vmem_limit_bytes=24 << 20),
        cost_estimate=pl.CostEstimate(flops=flops, bytes_accessed=bytes_accessed, transcendentals=exps),
    )(*args)


def swap(x, axis, k):
    return lax.ppermute(x, axis, [(i, i ^ k) for i in range(lax.axis_size(axis))])


def exchange(x, axis):
    return [x] + [swap(x, axis, k) for k in range(1, lax.axis_size(axis))]


def exchange_chips(x):
    return [x] + [swap(x, "row", k) for k in range(2, lax.axis_size("row"), 2)]


def combine(kernel, parts):
    return call(kernel, [jax.ShapeDtypeStruct(parts[0].shape, parts[0].dtype)], parts)[0]


def per_device(source, target, target_potential, prev_moment):
    f32, bf16, shape = jnp.float32, jnp.bfloat16, jax.ShapeDtypeStruct
    ns, nt = lax.axis_size("col"), lax.axis_size("row")
    piece, width = source.shape[0], target.shape[0]
    depth = source.shape[1]
    rows, cols = piece * ns, width * nt
    rows_total, cols_total = rows * nt, cols * ns
    tile = shape((rows // LANES, LANES), f32)
    projected = shape((rows, depth), bf16)
    flops, exps = 2 * rows * cols * depth, rows * cols
    row_scores = pltpu.VMEM((LANES, cols), f32)
    small = pltpu.VMEM(tile.shape, f32)
    sums = pltpu.VMEM((rows, LANES), f32)

    groups = width // LANES
    tail = jnp.pad(target_potential.reshape(groups, LANES), ((0, SUB - groups), (0, 0)))
    block = jnp.concatenate([target, tail], axis=0)
    pieces = exchange(source, "col")
    far = exchange_chips(block)
    order = [0, ns - 2, ns - 1] + list(range(ns - 3, 0, -1)) if ns > 2 else list(range(ns))
    s, a = call(
        functools.partial(project_kernel, order),
        [projected, projected],
        [pieces[k] for k in order] + [prev_moment],
        flops=200 * rows * depth * depth,
    )
    far = [lax.optimization_barrier((x, a))[0] for x in far]
    blocks = [x for pair in zip(far, [swap(x, "row", 1) for x in far]) for x in pair]
    shift, top = call(
        functools.partial(shift_kernel, width), [shape((rows, LANES), f32), tile], [a, far[0]], flops=2 * rows * width * depth
    )
    lse, carried, t, pot = call(
        functools.partial(couple_kernel, nt, width),
        [tile, shape((rows, depth), f32), shape((cols, 2 * depth), bf16), shape((nt, width), f32)],
        [a, shift, top] + blocks,
        [pltpu.VMEM((rows, cols), bf16), row_scores],
        2 * flops,
        exps,
    )
    half = shape((depth // 2, depth), f32)
    keep, send = call(
        functools.partial(moment_kernel, ns, rows_total),
        [half, half],
        [s] + exchange(lse, "col") + [carried],
        [small, pltpu.VMEM((depth, depth), f32)],
        6 * rows * depth * depth,
    )
    part = combine(add_kernel, [keep, swap(send, "row", 1)])
    part = combine(add_kernel, exchange(part, "col"))
    part = combine(add_kernel, exchange_chips(part))
    moment, a, lse, top, e = call(
        first_rows_kernel,
        [shape((depth, depth), f32), projected, tile, tile, shape((rows, cols), bf16)],
        [s, t, pot, part, swap(part, "row", 1)],
        [sums, sums, row_scores],
        flops,
        exps,
    )
    for iteration in range(ITERS):
        last = iteration == ITERS - 1
        if iteration > 0:
            both = combine(log_sum_kernel, [column, swap(column, "row", 1)])
            lse, = call(
                functools.partial(rows_kernel, rows_total),
                [tile],
                [a, e, top, t, pot] + exchange_chips(both),
                [pltpu.VMEM((nt, width), f32), pltpu.VMEM((SUB, cols), bf16), row_scores],
                16 * rows * cols,
            )
        halves = shape((nt // 2, 1, width), f32)
        column, *sent, source_potential = call(
            functools.partial(columns_kernel, ns, cols_total, last),
            ([halves, halves] if last else [shape((nt, width), f32)]) + [tile],
            [a, e, top, t, pot] + exchange(lse, "col"),
            [
                small,
                pltpu.VMEM((SUB, rows), bf16),
                pltpu.VMEM((rows, LANES), f32),
                pltpu.VMEM((rows, width), f32),
            ],
            16 * rows * cols,
        )
    one = shape((1, width), f32)
    parts = call(split_kernel, [one] * (nt // 2), [column, swap(sent[0], "row", 1)])
    parts = [swap(x, "row", nt - 2 - 2 * k) for k, x in enumerate(parts[:-1])] + [parts[-1]]
    update, = call(functools.partial(update_kernel, rows_total), [one], parts)
    return moment, source_potential.reshape(rows), update.reshape(width)


def solution(mesh):
    placed = (P(("row", "col"), None), P(("col", "row"), None), P(("col", "row")), P())
    return jax.shard_map(
        per_device,
        mesh=mesh,
        in_specs=placed,
        out_specs=(P(), P("row"), P(("col", "row"))),
        check_vma=False,
    )
```
